32 devices in a mesh: head: 4 (over x, core), tok: 8 (over z, y).
Axes of the slice: x: 2, y: 2, z: 4, core: 2. Of those that a mesh axis runs over, the one named last changes fastest.
Arguments:
- residual_in: bfloat16 [4096, 768], P('tok', 'head')
- cotangent: bfloat16 [4096, 768], P('tok', 'head'), may hold values from -6 to 6
- w_qkv: bfloat16 [2, 768, 3, 768], P(None, None, None, 'head'), may hold values from -0.21875 to 0.21875
- b_qv: bfloat16 [2, 2, 768], P(None, None, 'head'), may hold values from -2 to 2
- w_out: bfloat16 [2, 768, 768], P(None, 'head'), may hold values from -0.875 to 0.875
- b_out: bfloat16 [2, 768], P(None, 'head'), may hold values from -2 to 2
- w_up: bfloat16 [2, 768, 3072], P(None, None, 'head')
- b_up: bfloat16 [2, 3072], P(None, 'head'), may hold values from -2 to 2
- w_down: bfloat16 [2, 3072, 768], P(None, 'head'), may hold values from -0.109375 to 0.109375
- b_down: bfloat16 [2, 768], P(None, 'head'), may hold values from -2 to 2
- ln_gain: bfloat16 [2, 2, 768], P(None, None, 'head'), may hold values from 0.5 to 1.5
- ln_bias: bfloat16 [2, 2, 768], P(None, None, 'head'), may hold values from -1.1953125 to 1.1953125
- selection: int32 [12, 64, 4], P('head'), may hold values from 0 to 255, as said below
- lengths: int32 [2], replicated, may hold values from 128 to 3968, as said below
- valid: int32 [4096], replicated, may hold values 0 or 1
Outputs:
- residual_out: bfloat16 [4096, 768], P('tok', 'head')
- grad_residual: bfloat16 [4096, 768], P('tok', 'head')
- grad_w_qkv: float32 [2, 768, 3, 768], P(None, None, None, 'head')
- grad_b_qv: float32 [2, 2, 768], P(None, None, 'head')
- grad_w_out: float32 [2, 768, 768], P(None, 'head')
- grad_b_out: float32 [2, 768], P(None, 'head')
- grad_w_up: float32 [2, 768, 3072], P(None, None, 'head')
- grad_b_up: float32 [2, 3072], P(None, 'head')
- grad_w_down: float32 [2, 3072, 768], P(None, 'head')
- grad_b_down: float32 [2, 768], P(None, 'head')
- grad_ln_gain: float32 [2, 2, 768], P(None, None, 'head')
- grad_ln_bias: float32 [2, 2, 768], P(None, None, 'head')
- statistics: float32 [2, 3], replicated
The draws below stay inside these ranges and needn't reach their ends.
Inputs may be any that keep to these rules, and one draw needn't show every extreme that they name: `lengths`: two sequences laid end to end that fill all 4096 tokens, in either order; the shorter has 128 tokens. `selection`: where a query block has usable blocks in its sequence ending 64 or more tokens before it, each slot names one of them, and slot 0 names one of the 8 latest of them; otherwise the slot holds 255.
All inputs are finite; a program needn't handle non-finite values.
Results may differ from the reference program's by a relative error of at most 0.03.
Values may be sent and summed in bfloat16 or wider, within the bound.
No kernel may reach another device: no remote copies, remote signals or barrier semaphores. Data moves between devices by JAX's collectives and lax.ppermute only.
A program may use at most 256 MiB of HBM per device.

```python
import jax
import jax.numpy as jnp
from jax import lax

D = 768
NH = 12
HD = 64
FF = 3072
LAYERS = 2
WINDOW = 64
KB = 16
SEL = 4
QB = 64
TOK_DEV = 512
TOKENS = 4096


def sequence_boundary(key):
    order_key = jax.random.fold_in(key, 0)
    flipped = jax.random.randint(order_key, (), 0, 2)
    shorter = TOK_DEV // 4
    return jnp.where(flipped == 0, shorter, TOKENS - shorter).astype(jnp.int32)


def draw_residual_in(key, part):
    key = jax.random.fold_in(key, 11)
    ramp = 1.0 + 2.0 * jnp.arange(TOKENS, dtype=jnp.float32) / TOKENS
    noise = jax.random.normal(key, (TOKENS, D), jnp.float32)
    return (noise * ramp[:, None]).astype(jnp.bfloat16)


def draw_w_up(key, part):
    key = jax.random.fold_in(key, 17)
    noise_key, common_key = jax.random.split(key)
    noise = jax.random.normal(noise_key, (LAYERS, D, FF), jnp.float32)
    common = jax.random.normal(common_key, (LAYERS, 1, FF), jnp.float32)
    return ((noise + 0.6 * common) * D ** (-0.5)).astype(jnp.bfloat16)


def draw_lengths(key, part):
    boundary = sequence_boundary(key)
    return jnp.stack([boundary, TOKENS - boundary]).astype(jnp.int32)


def draw_selection(key, part):
    boundary = sequence_boundary(key)
    key = jax.random.fold_in(key, 13)
    starts = QB * jnp.arange(TOKENS // QB, dtype=jnp.int32)
    anchor = jnp.where(starts >= boundary, (boundary + KB - 1) // KB * KB, 0)
    lowest = anchor // KB
    limit = (starts - WINDOW) // KB
    usable = limit - lowest
    random_bits = jax.random.randint(key, (NH, TOKENS // QB, SEL), 0, 1 << 30)
    spread_pick = lowest[None, :, None] + random_bits % jnp.maximum(usable, 1)[None, :, None]
    recent_span = jnp.minimum(jnp.maximum(usable, 1), 2 * QB // KB)[None, :, None]
    recent_pick = limit[None, :, None] - 1 - random_bits % recent_span
    slot_index = jnp.arange(SEL, dtype=jnp.int32)[None, None, :]
    picked = jnp.where(slot_index == 0, recent_pick, spread_pick)
    return jnp.where(usable[None, :, None] > 0, picked, TOKENS // KB - 1).astype(jnp.int32)


def plant(values, key, smallest, top_value):
    dims = values.shape
    index_at = [jax.random.randint(jax.random.fold_in(key, axis), (), 0, dims[axis]) for axis in range(len(dims))]
    values = values.at[tuple(index_at)].set(smallest)
    longest = dims.index(max(dims))
    index_at[longest] = (index_at[longest] + 1) % dims[longest]
    return values.at[tuple(index_at)].set(top_value)


def steps_of(rng, dims, pieces, low, largest):
    def one(axis_at, parts):
        steps = jax.random.uniform(jax.random.fold_in(jax.random.fold_in(rng, 6), axis_at), (parts,), jnp.float32, low / len(pieces), largest / len(pieces))
        return jnp.repeat(jnp.exp(steps), dims[axis_at] // parts).reshape((-1,) + (1,) * (len(dims) - axis_at - 1))

    factor_of = one(*pieces[0])
    for cut in pieces[1:]:
        factor_of = factor_of * one(*cut)
    return factor_of


def gaussian(stream_key, dims, deviation, most, shards=(), kind=jnp.bfloat16):
    values = deviation * jax.random.normal(stream_key, dims, jnp.float32)
    if shards:
        values = values * steps_of(stream_key, dims, shards, -0.22, 0.18)
    return jnp.clip(values, -most, most).astype(kind)


def setup_inputs(seed: int = 0) -> dict:
    splits = jax.random.split(jax.random.key(seed), 16)
    residual_in = draw_residual_in(jax.random.fold_in(splits[15], 71), 0)
    cotangent = gaussian(splits[1], (TOKENS, D), 1.0, 6.0, ((0, 8), (1, 4)))
    w_qkv = gaussian(splits[2], (LAYERS, D, 3, D), D ** -0.5, 0.21875, ((3, 4),))
    b_qv = gaussian(splits[3], (LAYERS, 2, D), 0.3, 2.0, ((2, 4),))
    w_out = gaussian(splits[4], (LAYERS, D, D), (D // 16) ** -0.5, 0.875, ((1, 4),))
    b_out = gaussian(splits[5], (LAYERS, D), 0.3, 2.0, ((1, 4),))
    w_up = draw_w_up(jax.random.fold_in(splits[15], 71), 0)
    b_up = gaussian(splits[7], (LAYERS, FF), 0.3, 2.0, ((1, 4),))
    w_down = gaussian(splits[8], (LAYERS, FF, D), FF ** -0.5, 0.109375, ((1, 4),))
    b_down = gaussian(splits[9], (LAYERS, D), 0.3, 2.0, ((1, 4),))
    ln_gain = jnp.clip(1.0 + 0.1 * jax.random.normal(splits[10], (LAYERS, 2, D), jnp.float32), 0.5, 1.5).astype(jnp.bfloat16)
    ln_bias = gaussian(splits[11], (LAYERS, 2, D), 0.2, 1.1953125, ((2, 4),))
    selection = draw_selection(jax.random.fold_in(splits[15], 71), 0)
    lengths = draw_lengths(jax.random.fold_in(splits[15], 71), 0)
    valid = plant((jax.random.randint(splits[14], (TOKENS,), 0, 8) < 7).astype(jnp.int32), jax.random.fold_in(splits[14], 1), 0, 1)
    return {"residual_in": residual_in, "cotangent": cotangent, "w_qkv": w_qkv, "b_qv": b_qv, "w_out": w_out, "b_out": b_out, "w_up": w_up, "b_up": b_up, "w_down": w_down, "b_down": b_down, "ln_gain": ln_gain, "ln_bias": ln_bias, "selection": selection, "lengths": lengths, "valid": valid}


@jax.custom_vjp
def low(v):
    return lax.optimization_barrier(v.astype(jnp.bfloat16)).astype(jnp.float32)

@jax.custom_vjp
def low_back(v):
    return v

def low_keep(v):
    return (low(v), None)

def low_pass(kept, grad):
    return (grad,)

def back_keep(v):
    return (v, None)

def back_low(kept, grad):
    return (low(grad),)
low.defvjp(low_keep, low_pass)
low_back.defvjp(back_keep, back_low)
epsilon = 1e-05
negative = -1e+30
highest = lax.Precision.HIGHEST
block_rows = 512

def layer_norm(rounded, gain, shift):
    average = lax.optimization_barrier(jnp.mean(rounded, axis=-1, keepdims=True))
    centred = rounded - average
    spread = lax.optimization_barrier(jnp.mean(centred * centred, axis=-1, keepdims=True))
    return centred * lax.rsqrt(spread + epsilon) * gain + shift

def matmul(left, right):
    return jnp.dot(left, right, precision=highest, preferred_element_type=jnp.float32)

def attention_masks(chosen, valid, boundary, first_row, row_count):
    head_count, block_count, pick_count = chosen.shape
    query_pos = first_row + jnp.arange(row_count, dtype=jnp.int32)
    key_pos = first_row - WINDOW + jnp.arange(row_count + WINDOW, dtype=jnp.int32)
    padded_valid = jnp.concatenate([jnp.zeros((WINDOW,), jnp.int32), valid])
    key_valid = lax.dynamic_slice_in_dim(padded_valid, first_row, row_count + WINDOW) > 0
    query_seq = query_pos >= boundary
    key_seq = key_pos >= boundary
    query_col = query_pos[:, None]
    key_line = key_pos[None, :]
    window_ok = (key_line <= query_col) & (key_line > query_col - WINDOW) & (key_line >= 0)
    window_ok = window_ok & (key_seq[None, :] == query_seq[:, None]) & (key_valid[None, :] | (key_line == query_col))
    token_index = (chosen[..., None] * KB + jnp.arange(KB, dtype=jnp.int32)).reshape(head_count, block_count, pick_count * KB)
    block_first = first_row + QB * jnp.arange(block_count, dtype=jnp.int32)
    early = chosen[..., None] * KB + KB <= block_first[None, :, None, None] - WINDOW
    early = jnp.broadcast_to(early, (head_count, block_count, pick_count, KB)).reshape(head_count, block_count, pick_count * KB)
    picked_valid = jnp.take(valid, token_index) > 0
    picked_seq = token_index >= boundary
    query_blocks = query_seq.reshape(block_count, QB)
    picked_ok = early[:, :, None, :] & picked_valid[:, :, None, :] & (picked_seq[:, :, None, :] == query_blocks[None, :, :, None])
    return (window_ok, picked_ok.reshape(head_count, row_count, pick_count * KB), token_index)

def pick_rows(source, indices):
    return source[indices]

def attend(queries, pairs, selection, valid, boundary):
    padded = jnp.concatenate([jnp.zeros((WINDOW, NH, 2 * HD), jnp.float32), pairs], 0)
    by_head = jnp.transpose(pairs, (1, 0, 2))
    block_count = block_rows // QB
    width = block_rows + WINDOW

    def one_block(block_index):
        first_row = block_index * block_rows
        query_part = lax.dynamic_slice_in_dim(queries, first_row, block_rows, 0)
        window_kv = lax.dynamic_slice_in_dim(padded, first_row, width, 0)
        chosen = lax.dynamic_slice_in_dim(selection, block_index * block_count, block_count, 1)
        window_ok, picked_ok, token_index = attention_masks(chosen, valid, boundary, first_row, block_rows)
        picked_kv = jax.vmap(pick_rows)(by_head, token_index)
        near = jnp.einsum('qhd,khd->hqk', query_part, window_kv[..., :HD], precision=highest, preferred_element_type=jnp.float32)
        grouped = query_part.reshape(block_count, QB, NH, HD)
        far = jnp.einsum('bqhd,hbjd->hbqj', grouped, picked_kv[..., :HD], precision=highest, preferred_element_type=jnp.float32)
        scores = low_back(jnp.concatenate([near, far.reshape(NH, block_rows, SEL * KB)], axis=-1))
        allowed = jnp.concatenate([jnp.broadcast_to(window_ok, (NH,) + window_ok.shape), picked_ok], axis=-1)
        masked = jnp.where(allowed, scores, negative)
        maximum = lax.optimization_barrier(jnp.max(masked, axis=-1, keepdims=True))
        exponent = jnp.exp(masked - maximum)
        weights = low(exponent / lax.optimization_barrier(jnp.sum(exponent, axis=-1, keepdims=True)))
        near_out = jnp.einsum('hqk,khd->qhd', weights[..., :width], window_kv[..., HD:], precision=highest, preferred_element_type=jnp.float32)
        far_weights = weights[..., width:].reshape(NH, block_count, QB, SEL * KB)
        far_out = jnp.einsum('hbqj,hbjd->bqhd', far_weights, picked_kv[..., HD:], precision=highest, preferred_element_type=jnp.float32)
        return near_out + far_out.reshape(block_rows, NH, HD)
    outputs = lax.map(jax.checkpoint(one_block), jnp.arange(TOKENS // block_rows, dtype=jnp.int32))
    return outputs.reshape(TOKENS, NH, HD)

def forward(residual_in, w_qkv, b_qv, w_out, b_out, w_up, b_up, w_down, b_down, ln_gain, ln_bias, selection, valid, boundary):
    residual = residual_in
    scale = HD ** (-0.5)
    weight_valid = valid.astype(jnp.float32)[:, None]
    valid_count = jnp.maximum(jnp.sum(valid.astype(jnp.float32)), 1.0)
    squares = []
    for layer_index in range(LAYERS):
        normed = low(layer_norm(low(residual), ln_gain[layer_index, 0], ln_bias[layer_index, 0]))
        projected = matmul(normed, w_qkv[layer_index].reshape(D, 3 * D)).reshape(TOKENS, 3, D)
        queries = low_back(low((projected[:, 0] + b_qv[layer_index, 0]) * scale)).reshape(TOKENS, NH, HD)
        key_rows = low_back(low(projected[:, 1])).reshape(TOKENS, NH, HD)
        value_rows = low_back(low(projected[:, 2] + b_qv[layer_index, 1])).reshape(TOKENS, NH, HD)
        pairs = jnp.concatenate([key_rows, value_rows], axis=-1)
        mixed_heads = low_back(low(attend(queries, pairs, selection, valid, boundary).reshape(TOKENS, D)))
        branch = low_back(matmul(mixed_heads, w_out[layer_index]) + b_out[layer_index])
        residual = residual + branch
        normed_second = low(layer_norm(low(residual), ln_gain[layer_index, 1], ln_bias[layer_index, 1]))
        inner_act = low_back(matmul(normed_second, w_up[layer_index]) + b_up[layer_index])
        hidden = low(jax.nn.gelu(inner_act, approximate=True))
        second = low_back(matmul(hidden, w_down[layer_index]) + b_down[layer_index])
        residual = residual + second
        for member in (residual, branch, second):
            squares.append(jnp.sqrt(jnp.sum(weight_valid * member * member) / (valid_count * D)))
    return (residual, jnp.stack(squares).reshape(LAYERS, 3))

def reference(residual_in, cotangent, w_qkv, b_qv, w_out, b_out, w_up, b_up, w_down, b_down, ln_gain, ln_bias, selection, lengths, valid):
    boundary = lengths[0]
    floats = [array.astype(jnp.float32) for array in (residual_in, w_qkv, b_qv, w_out, b_out, w_up, b_up, w_down, b_down, ln_gain, ln_bias)]

    def wrapped(*arrays):
        return forward(*arrays, selection, valid, boundary)
    residual_out, pullback, statistics = jax.vjp(wrapped, *floats, has_aux=True)
    grads = pullback(cotangent.astype(jnp.float32))
    return (residual_out.astype(jnp.bfloat16), grads[0].astype(jnp.bfloat16), grads[1], grads[2], grads[3], grads[4], grads[5], grads[6], grads[7], grads[8], grads[9], grads[10], statistics)
```

```python
import functools

import jax
import jax.numpy as jnp
from jax import lax
from jax.experimental import pallas as pl
from jax.experimental.pallas import tpu as pltpu
from jax.sharding import PartitionSpec as P

D = 768
HD = 64
LAYERS = 2
WINDOW = 64
KB = 16
SEL = 4
QB = 64
WIDE = 2 * HD

epsilon = 1e-05
negative = -1e30
scale = HD ** (-0.5)
bf16 = jnp.bfloat16
f32 = jnp.float32

STEPS = (0, 2, 1, 3)
GAIN, SHIFT, B_OUT, B_DOWN, PARAM_ROWS = 0, 4, 8, 10, 16


def params(megabytes):
    return pltpu.CompilerParams(vmem_limit_bytes=megabytes * 2**20)


def cost(flops, moved, special=0):
    return pl.CostEstimate(flops=int(flops), bytes_accessed=int(moved), transcendentals=int(special))


def swap(value, axis, step):
    return lax.ppermute(value, axis, [(i, i ^ step) for i in range(lax.axis_size(axis))])


def shift_by(value, axis, step):
    count = lax.axis_size(axis)
    return lax.ppermute(
        value, axis, [(i, i + step) for i in range(count) if 0 <= i + step < count]
    )


def share_quarters(own):
    across = swap(own, "head", 2)
    beside = swap(own, "head", 1)
    both = swap(across, "head", 1)
    return own, across, beside, both


def sum_quarters(pieces):
    own, across, beside, both = pieces
    first = swap(both, "head", 1)
    onward = (across.astype(f32) + first.astype(f32)).astype(bf16)
    second = swap(beside, "head", 1)
    third = swap(onward, "head", 2)
    return own, second, third


def small_sum(value, axes):
    for axis in axes:
        step = 1
        while step < lax.axis_size(axis):
            value = value + swap(value, axis, step)
            step *= 2
    return value


def block_sum(value):
    count = lax.axis_size("tok")
    position = lax.axis_index("tok")
    columns = value.shape[1]
    steps = []
    step = 1
    while step < count:
        steps.append(step)
        step *= 2
    for step in steps:
        bit = (position // step) % 2
        half = value.shape[0] // 2
        pair = value.reshape(2, half, columns)
        give = lax.dynamic_index_in_dim(pair, 1 - bit, 0, keepdims=False)
        keep = lax.dynamic_index_in_dim(pair, bit, 0, keepdims=False)
        value = (keep.astype(f32) + swap(give, "tok", step).astype(f32)).astype(bf16)
    for step in reversed(steps):
        bit = (position // step) % 2
        other = swap(value, "tok", step)
        value = jnp.concatenate(
            [jnp.where(bit == 0, value, other), jnp.where(bit == 0, other, value)], axis=0
        )
    return value.astype(f32)


def ring_form(count):
    return count == 8


def gather_blocks(own):
    count = lax.axis_size("tok")
    if not ring_form(count):
        return [lax.all_gather(own, "tok")]
    current = own
    parts = []
    for hop in range(count // 2):
        other = swap(current, "tok", 1)
        if hop < count // 2 - 1:
            after = shift_by(current, "tok", 2)
            current, other, after = lax.optimization_barrier((current, other, after))
        parts += [current, other]
        current = after
    return parts


def return_blocks(parts):
    count = lax.axis_size("tok")
    if not ring_form(count):
        return [lax.psum_scatter(parts[0], "tok", scatter_dimension=0, tiled=False)]
    running = None
    for d in range(count // 2 - 1, 0, -1):
        got = swap(parts[2 * d + 1], "tok", 1)
        total = parts[2 * d].astype(f32) + got.astype(f32)
        if running is not None:
            total = total + running.astype(f32)
        running = shift_by(total.astype(bf16), "tok", -2)
    return [parts[0], swap(parts[1], "tok", 1), running]


def slot_of(block, tok, count):
    if not ring_form(count):
        return block
    away = (tok >> 1) - (block >> 1)
    return 2 * jnp.maximum(away, 0) + ((tok ^ block) & 1)


def normalise(rows):
    average = jnp.mean(rows, axis=-1, keepdims=True)
    centred = rows - average
    spread = jnp.mean(centred * centred, axis=-1, keepdims=True)
    inverse = lax.rsqrt(spread + epsilon)
    return centred * inverse, inverse


def row(ref, index):
    return ref[index : index + 1, :].astype(f32)


def piece_rows(place, step, size):
    return pl.ds(pl.multiple_of((place[0] ^ step) * size, size), size)


def project_kernel(place, *refs, heads, first):
    if first:
        rows_ref, param_ref, w_ref, bias_ref, normed_ref, q_ref, kv_ref = refs
    else:
        own, across, beside, both, w_ref, bias_ref, normed_ref, q_ref, kv_ref = refs
    size = normed_ref.shape[0] // 4
    for k in range(4):
        if first:
            rows = pl.ds(k * size, size)
            unit, _ = normalise(rows_ref[rows, :].astype(f32))
            normed = (unit * row(param_ref, GAIN) + row(param_ref, SHIFT)).astype(bf16)
        else:
            rows = piece_rows(place, STEPS[k], size)
            normed = (own, across, beside, both)[k][...]
        normed_ref[rows, :] = normed
        projected = jnp.dot(normed, w_ref[...], preferred_element_type=f32) + bias_ref[...]
        for h in range(heads):
            q_ref[h, rows, :] = (projected[:, h * WIDE : (h + 1) * WIDE] * scale).astype(bf16)
            at = (heads + h) * WIDE
            kv_ref[h, rows, :] = projected[:, at : at + WIDE].astype(bf16)


def whole(shape):
    return pl.BlockSpec(shape, lambda *_: (0,) * len(shape))


def param_spec(rows):
    return pl.BlockSpec((PARAM_ROWS, D), lambda *_: (rows // PARAM_ROWS, 0))


def project(place, source, gathered, w_all, bias_all, rows, heads):
    first = source is None
    quarter = rows // 4
    columns = w_all.shape[1]
    if first:
        arrays = (gathered, gathered)
        specs = [whole((rows, D)), param_spec(rows)]
    else:
        arrays = tuple(source)
        specs = [whole((quarter, D))] * 4
    return pl.pallas_call(
        functools.partial(project_kernel, heads=heads, first=first),
        grid_spec=pltpu.PrefetchScalarGridSpec(
            num_scalar_prefetch=1,
            grid=(1,),
            in_specs=specs + [whole(w_all.shape), whole(bias_all.shape)],
            out_specs=[whole((rows, D)), whole((heads, rows, WIDE)), whole((heads, rows, WIDE))],
        ),
        out_shape=[
            jax.ShapeDtypeStruct((rows, D), bf16),
            jax.ShapeDtypeStruct((heads, rows, WIDE), bf16),
            jax.ShapeDtypeStruct((heads, rows, WIDE), bf16),
        ],
        compiler_params=params(32),
        cost_estimate=cost(2 * rows * D * columns, 2 * D * columns + 8 * rows * D),
        name="project",
    )(place, *arrays, w_all, bias_all)


def copies(parts, scratch, sems, head, buffer, rows):
    if len(parts) == 1:
        count = parts[0].shape[0]
        return [
            pltpu.make_async_copy(
                parts[0].at[slot, head],
                scratch.at[buffer, pl.ds(slot * rows, rows), :],
                sems.at[buffer, slot],
            )
            for slot in range(count)
        ]
    return [
        pltpu.make_async_copy(
            part.at[head], scratch.at[buffer, pl.ds(slot * rows, rows), :], sems.at[buffer, slot]
        )
        for slot, part in enumerate(parts)
    ]


def bring_blocks(parts, scratch, sems, heads, rows):
    head = pl.program_id(0)
    buffer = lax.rem(head, 2)

    @pl.when(head == 0)
    def _():
        for copy in copies(parts, scratch, sems, 0, 0, rows):
            copy.start()

    @pl.when(head + 1 < heads)
    def _():
        for copy in copies(parts, scratch, sems, head + 1, 1 - buffer, rows):
            copy.start()

    for copy in copies(parts, scratch, sems, head, buffer, rows):
        copy.wait()
    return head, buffer


class Listed:
    def __init__(self, place, chosen, keys, near_valid, far_valid, rows, count):
        self.place, self.chosen, self.keys = place, chosen, keys
        self.near_valid, self.far_valid = near_valid, far_valid
        self.rows, self.count = rows, count
        self.tok = place[1]
        self.boundary = place[2]
        self.own = slot_of(self.tok, self.tok, count) * rows
        self.before = slot_of(jnp.maximum(self.tok - 1, 0), self.tok, count) * rows
        line = lax.broadcasted_iota(jnp.int32, (QB, 2 * WINDOW), 1)
        column = lax.broadcasted_iota(jnp.int32, (QB, 2 * WINDOW), 0)
        self.band = (line > column) & (line <= column + WINDOW)
        self.diagonal = line == column + WINDOW

    def near_starts(self, b):
        if b == 0:
            return [
                (pl.multiple_of(self.before + self.rows - WINDOW, WINDOW), WINDOW),
                (pl.multiple_of(self.own, WINDOW), WINDOW),
            ]
        return [(pl.multiple_of(self.own + (b - 1) * QB, WINDOW), 2 * WINDOW)]

    def far_start(self, head, b, s):
        block = self.chosen[head, b * SEL + s]
        per_device = self.rows // KB
        device = lax.div(block, per_device)
        at = slot_of(device, self.tok, self.count) * self.rows + lax.rem(block, per_device) * KB
        return pl.multiple_of(at, KB)

    def load(self, buffer, starts):
        loaded = [self.keys[buffer, pl.ds(start, size), :] for start, size in starts]
        return loaded[0] if len(loaded) == 1 else jnp.concatenate(loaded, axis=0)

    def masks(self, head, b):
        first = self.tok * self.rows + b * QB
        in_second = lambda position: jnp.where(position >= self.boundary, 1, 0)
        query = first + lax.broadcasted_iota(jnp.int32, (QB, 1), 0)
        query_seq = in_second(query)
        key = first - WINDOW + lax.broadcasted_iota(jnp.int32, (1, 2 * WINDOW), 1)
        valid = self.near_valid[b : b + 1, :] > 0.0
        near = self.band & (self.diagonal | valid) & (in_second(key) == query_seq)
        lane = lax.broadcasted_iota(jnp.int32, (1, SEL * KB), 1)
        usable = jnp.zeros((1, SEL * KB), f32)
        token = lane & (KB - 1)
        for s in range(SEL):
            block = self.chosen[head, b * SEL + s]
            here = (lane >= s * KB) & (lane < (s + 1) * KB)
            early = block * KB + KB <= first - WINDOW
            here_usable = here & early
            usable = jnp.where(here_usable, self.far_valid[pl.ds(block, 1), :], usable)
            token = token + jnp.where(here, block * KB, 0)
        far = (usable > 0.0) & (in_second(token) == query_seq)
        return near, far


def softmax(queries, near_kv, far_kv, near_ok, far_ok):
    transposed = (((1,), (1,)), ((), ()))
    near = lax.dot_general(queries, near_kv, transposed, preferred_element_type=f32)
    far = lax.dot_general(queries, far_kv, transposed, preferred_element_type=f32)
    near = jnp.where(near_ok, near, negative)
    far = jnp.where(far_ok, far, negative)
    top = jnp.maximum(
        jnp.max(near, axis=-1, keepdims=True), jnp.max(far, axis=-1, keepdims=True)
    )
    near = jnp.exp(near - top)
    far = jnp.exp(far - top)
    total = jnp.sum(near, axis=-1, keepdims=True) + jnp.sum(far, axis=-1, keepdims=True)
    part = 1.0 / total
    return near * part, far * part


def attend_kernel(place, chosen, *refs, heads, count, blocks, parts):
    q_ref, w_ref, near_valid, far_valid = refs[:4]
    kv_parts = refs[4 : 4 + parts]
    mixed_ref = refs[4 + parts]
    outs = refs[5 + parts : 9 + parts]
    keys, gathered, sems = refs[9 + parts :]
    rows = blocks * QB
    head, buffer = bring_blocks(kv_parts, keys, sems, heads, rows)
    listed = Listed(place, chosen, keys, near_valid, far_valid, rows, count)
    for b in range(blocks):
        at = pl.ds(b * QB, QB)
        near_kv = listed.load(buffer, listed.near_starts(b))
        far_kv = listed.load(buffer, [(listed.far_start(head, b, s), KB) for s in range(SEL)])
        near_ok, far_ok = listed.masks(head, b)
        near, far = softmax(q_ref[0, at, :], near_kv, far_kv, near_ok, far_ok)
        out = jnp.dot(near.astype(bf16), near_kv, preferred_element_type=f32)
        out = out + jnp.dot(far.astype(bf16), far_kv, preferred_element_type=f32)
        out = out.astype(bf16)
        mixed_ref[0, at, :] = out
        gathered[head, at, :] = out

    @pl.when(head == heads - 1)
    def _():
        size = rows // 4
        for k in range(4):
            at = piece_rows(place, STEPS[k], size)
            mixed = jnp.concatenate([gathered[h, at, :] for h in range(heads)], axis=1)
            outs[k][...] = jnp.dot(mixed, w_ref[...], preferred_element_type=f32).astype(bf16)


def attend(place, chosen, queries, w_out, near_valid, far_valid, parts, count):
    heads, rows, _ = queries.shape
    blocks = rows // QB
    quarter = rows // 4
    per_head = pl.BlockSpec((1, rows, WIDE), lambda h, *_: (h, 0, 0))
    slots = count if len(parts) == 1 else len(parts)
    return pl.pallas_call(
        functools.partial(
            attend_kernel, heads=heads, count=count, blocks=blocks, parts=len(parts)
        ),
        grid_spec=pltpu.PrefetchScalarGridSpec(
            num_scalar_prefetch=2,
            grid=(heads,),
            in_specs=[
                per_head,
                whole(w_out.shape),
                whole(near_valid.shape),
                whole(far_valid.shape),
            ]
            + [pl.BlockSpec(memory_space=pl.ANY)] * len(parts),
            out_specs=[per_head] + [whole((quarter, D))] * 4,
            scratch_shapes=[
                pltpu.VMEM((2, slots * rows, WIDE), bf16),
                pltpu.VMEM((heads, rows, WIDE), bf16),
                pltpu.SemaphoreType.DMA((2, slots)),
            ],
        ),
        out_shape=[jax.ShapeDtypeStruct((heads, rows, WIDE), bf16)]
        + [jax.ShapeDtypeStruct((quarter, D), bf16)] * 4,
        compiler_params=params(44),
        cost_estimate=cost(
            2 * rows * heads * WIDE * (D + 512), 2 * heads * WIDE * rows * (slots + 4)
        ),
        name="attend",
    )(place, chosen, queries, w_out, near_valid, far_valid, *parts)


def attend_back_kernel(place, chosen, *refs, heads, count, blocks, parts):
    q_ref, w_ref, near_valid, far_valid = refs[:4]
    pieces = refs[4:8]
    kv_parts = refs[8 : 8 + parts]
    dq_ref, grad_ref = refs[8 + parts : 10 + parts]
    outs = refs[10 + parts : 10 + 2 * parts]
    keys, sums, sems = refs[10 + 2 * parts :]
    rows = blocks * QB
    size = rows // 4
    head, buffer = bring_blocks(kv_parts, keys, sems, heads, rows)
    listed = Listed(place, chosen, keys, near_valid, far_valid, rows, count)

    @pl.when(head == 0)
    def _():
        for k in range(4):
            grad_ref[piece_rows(place, STEPS[k], size), :] = pieces[k][...]

    sums[...] = jnp.zeros_like(sums)
    transposed = (((1,), (1,)), ((), ()))
    over_queries = (((0,), (0,)), ((), ()))
    for b in range(blocks):
        at = pl.ds(b * QB, QB)
        near_at = listed.near_starts(b)
        far_at = [(listed.far_start(head, b, s), KB) for s in range(SEL)]
        near_kv = listed.load(buffer, near_at)
        far_kv = listed.load(buffer, far_at)
        near_ok, far_ok = listed.masks(head, b)
        queries = q_ref[0, at, :]
        near, far = softmax(queries, near_kv, far_kv, near_ok, far_ok)
        mixed = lax.dot_general(
            grad_ref[at, :], w_ref[...], transposed, preferred_element_type=f32
        ).astype(bf16)
        near_grad = lax.dot_general(mixed, near_kv, transposed, preferred_element_type=f32)
        far_grad = lax.dot_general(mixed, far_kv, transposed, preferred_element_type=f32)
        inner = jnp.sum(near * near_grad, axis=-1, keepdims=True)
        inner = inner + jnp.sum(far * far_grad, axis=-1, keepdims=True)
        near_scores = (near * (near_grad - inner)).astype(bf16)
        far_scores = (far * (far_grad - inner)).astype(bf16)
        grad_q = jnp.dot(near_scores, near_kv, preferred_element_type=f32)
        grad_q = grad_q + jnp.dot(far_scores, far_kv, preferred_element_type=f32)
        dq_ref[0, at, :] = (grad_q.astype(bf16).astype(f32) * scale).astype(bf16)
        near_sum = lax.dot_general(
            near_scores, queries, over_queries, preferred_element_type=f32
        ) + lax.dot_general(near.astype(bf16), mixed, over_queries, preferred_element_type=f32)
        far_sum = lax.dot_general(
            far_scores, queries, over_queries, preferred_element_type=f32
        ) + lax.dot_general(far.astype(bf16), mixed, over_queries, preferred_element_type=f32)
        done = 0
        for start, length in near_at:
            sums[pl.ds(start, length), :] += near_sum[done : done + length]
            done += length
        for s, (start, length) in enumerate(far_at):
            sums[pl.ds(start, length), :] += far_sum[s * KB : (s + 1) * KB]
    if parts == 1:
        for slot in range(count):
            outs[0][slot, 0] = sums[pl.ds(slot * rows, rows), :].astype(bf16)
    else:
        for slot in range(parts):
            outs[slot][0] = sums[pl.ds(slot * rows, rows), :].astype(bf16)


def attend_back(place, chosen, queries, w_out, near_valid, far_valid, pieces, parts, count):
    heads, rows, _ = queries.shape
    blocks = rows // QB
    quarter = rows // 4
    per_head = pl.BlockSpec((1, rows, WIDE), lambda h, *_: (h, 0, 0))
    slots = count if len(parts) == 1 else len(parts)
    if len(parts) == 1:
        out_specs = [pl.BlockSpec((count, 1, rows, WIDE), lambda h, *_: (0, h, 0, 0))]
    else:
        out_specs = [per_head] * len(parts)
    return pl.pallas_call(
        functools.partial(
            attend_back_kernel, heads=heads, count=count, blocks=blocks, parts=len(parts)
        ),
        grid_spec=pltpu.PrefetchScalarGridSpec(
            num_scalar_prefetch=2,
            grid=(heads,),
            in_specs=[
                per_head,
                pl.BlockSpec((WIDE, D), lambda h, *_: (h, 0)),
                whole(near_valid.shape),
                whole(far_valid.shape),
            ]
            + [whole((quarter, D))] * 4
            + [pl.BlockSpec(memory_space=pl.ANY)] * len(parts),
            out_specs=[per_head, whole((rows, D))] + out_specs,
            scratch_shapes=[
                pltpu.VMEM((2, slots * rows, WIDE), bf16),
                pltpu.VMEM((slots * rows, WIDE), f32),
                pltpu.SemaphoreType.DMA((2, slots)),
            ],
        ),
        out_shape=[
            jax.ShapeDtypeStruct((heads, rows, WIDE), bf16),
            jax.ShapeDtypeStruct((rows, D), bf16),
        ]
        + [jax.ShapeDtypeStruct(part.shape, bf16) for part in parts],
        compiler_params=params(62 if len(parts) == 1 else 44),
        cost_estimate=cost(
            2 * rows * heads * WIDE * (D + 1536), 4 * heads * WIDE * rows * (slots + 4)
        ),
        name="attend_back",
    )(place, chosen, queries, w_out, near_valid, far_valid, *pieces, *parts)


def project_back_kernel(place, *refs, heads, terms):
    dq_ref, w_ref = refs[:2]
    kv_refs = refs[2 : 2 + terms]
    dkv_ref, bias_ref = refs[2 + terms : 4 + terms]
    outs = refs[4 + terms :]
    rows = dq_ref.shape[1]
    size = rows // 4
    for h in range(heads):
        total = kv_refs[0][h].astype(f32)
        for term in kv_refs[1:]:
            total = total + term[h].astype(f32)
        low = total.astype(bf16)
        dkv_ref[h] = low
        bias_ref[h : h + 1, :] = jnp.sum(dq_ref[h].astype(f32), axis=0, keepdims=True)
        bias_ref[heads + h : heads + h + 1, :] = jnp.sum(low.astype(f32), axis=0, keepdims=True)
    for k in range(4):
        at = piece_rows(place, STEPS[k], size)
        grads = jnp.concatenate(
            [dq_ref[h, at, :] for h in range(heads)] + [dkv_ref[h, at, :] for h in range(heads)],
            axis=1,
        )
        outs[k][...] = lax.dot_general(
            grads, w_ref[...], (((1,), (1,)), ((), ())), preferred_element_type=f32
        ).astype(bf16)


def project_back(place, dq, w_all, kv_terms):
    heads, rows, _ = dq.shape
    quarter = rows // 4
    return pl.pallas_call(
        functools.partial(project_back_kernel, heads=heads, terms=len(kv_terms)),
        grid_spec=pltpu.PrefetchScalarGridSpec(
            num_scalar_prefetch=1,
            grid=(1,),
            in_specs=[whole(dq.shape), whole(w_all.shape)] + [whole(dq.shape)] * len(kv_terms),
            out_specs=[whole(dq.shape), whole((2 * heads, WIDE))] + [whole((quarter, D))] * 4,
        ),
        out_shape=[
            jax.ShapeDtypeStruct(dq.shape, bf16),
            jax.ShapeDtypeStruct((2 * heads, WIDE), f32),
        ]
        + [jax.ShapeDtypeStruct((quarter, D), bf16)] * 4,
        compiler_params=params(32),
        cost_estimate=cost(4 * rows * D * heads * WIDE, 4 * D * heads * WIDE + 12 * rows * D),
        name="project_back",
    )(place, dq, w_all, *kv_terms)


def feed_kernel(place, *refs):
    pieces = refs[:4]
    up_ref, bias_ref, down_ref, normed_ref, hidden_ref, slope_ref = refs[4:10]
    outs = refs[10:]
    size = pieces[0].shape[0]
    root = 0.7978845608028654
    cubic = 0.044715
    for k in range(4):
        at = pl.ds(k * size, size)
        normed = pieces[k][...]
        normed_ref[at, :] = normed
        inner = jnp.dot(normed, up_ref[...], preferred_element_type=f32) + bias_ref[...]
        square = inner * inner
        bend = jnp.tanh(root * inner * (1.0 + cubic * square))
        half = 0.5 * (1.0 + bend)
        hidden = (inner * half).astype(bf16)
        hidden_ref[at, :] = hidden
        slope = half + 0.5 * inner * (1.0 - bend * bend) * (root * (1.0 + 3.0 * cubic * square))
        slope_ref[at, :] = slope.astype(bf16)
        outs[k][...] = jnp.dot(hidden, down_ref[...], preferred_element_type=f32).astype(bf16)


def feed(place, pieces, w_up, b_up, w_down):
    quarter = pieces[0].shape[0]
    rows = 4 * quarter
    units = w_up.shape[1]
    return pl.pallas_call(
        feed_kernel,
        grid_spec=pltpu.PrefetchScalarGridSpec(
            num_scalar_prefetch=1,
            grid=(1,),
            in_specs=[whole((quarter, D))] * 4
            + [whole(w_up.shape), whole(b_up.shape), whole(w_down.shape)],
            out_specs=[whole((rows, D)), whole((rows, units)), whole((rows, units))]
            + [whole((quarter, D))] * 4,
        ),
        out_shape=[
            jax.ShapeDtypeStruct((rows, D), bf16),
            jax.ShapeDtypeStruct((rows, units), bf16),
            jax.ShapeDtypeStruct((rows, units), bf16),
        ]
        + [jax.ShapeDtypeStruct((quarter, D), bf16)] * 4,
        compiler_params=params(32),
        cost_estimate=cost(4 * rows * D * units, 4 * D * units + 10 * rows * D, rows * units),
        name="feed",
    )(place, *pieces, w_up, b_up, w_down)


def feed_back_kernel(place, *refs):
    pieces = refs[:4]
    down_ref, up_ref, slope_ref, grad_ref, inner_ref, bias_ref = refs[4:10]
    outs = refs[10:]
    size = pieces[0].shape[0]
    transposed = (((1,), (1,)), ((), ()))
    total = None
    for k in range(4):
        at = pl.ds(k * size, size)
        grad = pieces[k][...]
        grad_ref[at, :] = grad
        hidden = lax.dot_general(grad, down_ref[...], transposed, preferred_element_type=f32)
        inner = (hidden * slope_ref[at, :].astype(f32)).astype(bf16)
        inner_ref[at, :] = inner
        part = jnp.sum(inner.astype(f32), axis=0, keepdims=True)
        total = part if total is None else total + part
        outs[k][...] = lax.dot_general(
            inner, up_ref[...], transposed, preferred_element_type=f32
        ).astype(bf16)
    bias_ref[...] = total


def feed_back(place, pieces, w_up, w_down, slope):
    rows, units = slope.shape
    quarter = rows // 4
    if len(pieces) == 1:
        arrays = tuple(pieces) * 4
        specs = [
            pl.BlockSpec((quarter, D), lambda i, place, step=step: (place[0] ^ step, 0))
            for step in STEPS
        ]
    else:
        arrays = tuple(pieces)
        specs = [whole((quarter, D))] * 4
    return pl.pallas_call(
        feed_back_kernel,
        grid_spec=pltpu.PrefetchScalarGridSpec(
            num_scalar_prefetch=1,
            grid=(1,),
            in_specs=specs + [whole(w_down.shape), whole(w_up.shape), whole(slope.shape)],
            out_specs=[whole((rows, D)), whole((rows, units)), whole((1, units))]
            + [whole((quarter, D))] * 4,
        ),
        out_shape=[
            jax.ShapeDtypeStruct((rows, D), bf16),
            jax.ShapeDtypeStruct((rows, units), bf16),
            jax.ShapeDtypeStruct((1, units), f32),
        ]
        + [jax.ShapeDtypeStruct((quarter, D), bf16)] * 4,
        compiler_params=params(32),
        cost_estimate=cost(4 * rows * D * units, 4 * D * units + 10 * rows * D),
        name="feed_back",
    )(place, *arrays, w_down, w_up, slope)


def add_norm_kernel(place, *refs, bias_row, norm_row):
    a, b, c, residual, param, valid = refs[:6]
    out_ref, low_ref, normed_ref, squares_ref = refs[6:]
    branch = a[...].astype(f32) + b[...].astype(f32) + c[...].astype(f32) + row(param, bias_row)
    total = residual[...].astype(f32) + branch
    out_ref[...] = total
    low = total.astype(bf16)
    low_ref[...] = low
    if norm_row is not None:
        unit, _ = normalise(low.astype(f32))
        gain, shift = row(param, GAIN + norm_row), row(param, SHIFT + norm_row)
        normed_ref[...] = (unit * gain + shift).astype(bf16)
    else:
        normed_ref[...] = low
    weight = valid[...]
    squares_ref[0:1, :] = jnp.sum(weight * branch * branch, axis=0, keepdims=True)
    squares_ref[1:2, :] = jnp.sum(weight * total * total, axis=0, keepdims=True)


def own_quarter(quarter):
    return pl.BlockSpec((quarter, D), lambda i, place: (place[0], 0))


def add_norm(place, terms, residual, gathered, valid, rows, bias_row, norm_row):
    quarter = rows // 4
    spec = whole((quarter, D))
    return pl.pallas_call(
        functools.partial(add_norm_kernel, bias_row=bias_row, norm_row=norm_row),
        grid_spec=pltpu.PrefetchScalarGridSpec(
            num_scalar_prefetch=1,
            grid=(1,),
            in_specs=[spec] * 3
            + [
                own_quarter(quarter) if residual is gathered else spec,
                param_spec(rows),
                whole(valid.shape),
            ],
            out_specs=[spec, spec, spec, whole((2, D))],
        ),
        out_shape=[
            jax.ShapeDtypeStruct((quarter, D), f32),
            jax.ShapeDtypeStruct((quarter, D), bf16),
            jax.ShapeDtypeStruct((quarter, D), bf16),
            jax.ShapeDtypeStruct((2, D), f32),
        ],
        compiler_params=params(16),
        cost_estimate=cost(20 * quarter * D, 18 * quarter * D),
        name="add_norm",
    )(place, *terms, residual, gathered, valid)


def norm_back_kernel(place, *refs, norm_row):
    a, b, c, source, gradient, param = refs[:6]
    out_ref, low_ref, sums_ref = refs[6:]
    grad_normed = a[...].astype(f32) + b[...].astype(f32) + c[...].astype(f32)
    unit, inverse = normalise(source[...].astype(f32))
    grad_unit = grad_normed * row(param, GAIN + norm_row)
    first = jnp.mean(grad_unit, axis=-1, keepdims=True)
    second = jnp.mean(grad_unit * unit, axis=-1, keepdims=True)
    total = gradient[...].astype(f32) + inverse * (grad_unit - first - unit * second)
    out_ref[...] = total
    low = total.astype(bf16)
    low_ref[...] = low
    sums_ref[0:1, :] = jnp.sum(grad_normed * unit, axis=0, keepdims=True)
    sums_ref[1:2, :] = jnp.sum(grad_normed, axis=0, keepdims=True)
    sums_ref[2:3, :] = jnp.sum(low.astype(f32), axis=0, keepdims=True)


def norm_back(place, terms, source, gradient, gathered, rows, norm_row):
    quarter = rows // 4
    spec = whole((quarter, D))
    pick = lambda array: spec if array.shape[0] == quarter else own_quarter(quarter)
    return pl.pallas_call(
        functools.partial(norm_back_kernel, norm_row=norm_row),
        grid_spec=pltpu.PrefetchScalarGridSpec(
            num_scalar_prefetch=1,
            grid=(1,),
            in_specs=[spec] * 3 + [pick(source), pick(gradient), param_spec(rows)],
            out_specs=[spec, spec, whole((3, D))],
        ),
        out_shape=[
            jax.ShapeDtypeStruct((quarter, D), f32),
            jax.ShapeDtypeStruct((quarter, D), bf16),
            jax.ShapeDtypeStruct((3, D), f32),
        ],
        compiler_params=params(16),
        cost_estimate=cost(20 * quarter * D, 18 * quarter * D),
        name="norm_back",
    )(place, *terms, source, gradient, gathered)


def columns_kernel(place, *refs):
    pieces, out = refs[:4], refs[4]
    size = pieces[0].shape[0]
    width = out.shape[1]
    for p in range(4):

        @pl.when(place[0] == p)
        def _():
            for k in range(4):
                at = piece_rows(place, STEPS[k], size)
                out[at, :] = pieces[k][:, p * width : (p + 1) * width]


def columns(place, pieces):
    quarter = pieces[0].shape[0]
    return pl.pallas_call(
        columns_kernel,
        grid_spec=pltpu.PrefetchScalarGridSpec(
            num_scalar_prefetch=1,
            grid=(1,),
            in_specs=[whole((quarter, D))] * 4,
            out_specs=whole((4 * quarter, D // 4)),
        ),
        out_shape=jax.ShapeDtypeStruct((4 * quarter, D // 4), bf16),
        compiler_params=params(16),
        cost_estimate=cost(quarter * D, 16 * quarter * D),
        name="columns",
    )(place, *pieces)


def on_device(
    residual_in,
    cotangent,
    w_qkv,
    b_qv,
    w_out,
    b_out,
    w_up,
    b_up,
    w_down,
    b_down,
    ln_gain,
    ln_bias,
    selection,
    lengths,
    valid,
):
    rows = residual_in.shape[0]
    heads = selection.shape[0]
    blocks = rows // QB
    quarter = rows // 4
    count = lax.axis_size("tok")
    position = lax.axis_index("tok")
    member = lax.axis_index("head")
    width = D // 4
    place = jnp.stack(
        [member.astype(jnp.int32), position.astype(jnp.int32), lengths[0], jnp.int32(0)]
    )
    first_row = position * rows

    small = jnp.concatenate(
        [ln_gain.reshape(-1, width), ln_bias.reshape(-1, width), b_out, b_down], axis=0
    )
    small = jnp.pad(small, ((0, PARAM_ROWS - small.shape[0]), (0, 0)))
    gathered = lax.all_gather(
        jnp.concatenate([residual_in, small], axis=0), "head", axis=1, tiled=True
    )
    cotangent_full = lax.all_gather(cotangent, "head", axis=1, tiled=True)

    split = w_qkv.reshape(LAYERS, D, 3, heads, HD)
    w_all = jnp.concatenate(
        [
            jnp.pad(split[:, :, 0], ((0, 0), (0, 0), (0, 0), (0, WIDE - HD))),
            jnp.concatenate([split[:, :, 1], split[:, :, 2]], axis=-1),
        ],
        axis=2,
    ).reshape(LAYERS, D, 2 * heads * WIDE)
    b_split = b_qv.reshape(LAYERS, 2, heads, HD)
    b_all = (
        jnp.concatenate(
            [
                jnp.pad(b_split[:, 0], ((0, 0), (0, 0), (0, HD))),
                jnp.pad(b_split[:, 1], ((0, 0), (0, 0), (HD, 0))),
            ],
            axis=1,
        )
        .reshape(LAYERS, 1, 2 * heads * WIDE)
        .astype(f32)
    )
    w_mix = jnp.pad(
        w_out.reshape(LAYERS, heads, HD, D), ((0, 0), (0, 0), (HD, 0), (0, 0))
    ).reshape(LAYERS, heads * WIDE, D)
    b_inner = b_up.astype(f32)

    chosen = lax.dynamic_slice_in_dim(selection, position * blocks, blocks, 1).reshape(heads, -1)
    far_valid = jnp.tile(valid.reshape(-1, KB), (1, SEL)).astype(f32)
    padded = jnp.concatenate([jnp.zeros((WINDOW,), jnp.int32), valid])
    near = lax.dynamic_slice_in_dim(padded, first_row, rows + WINDOW).reshape(-1, WINDOW)
    near_valid = jnp.concatenate([near[:-1], near[1:]], axis=1).astype(f32)
    own_valid = lax.dynamic_slice_in_dim(valid, first_row + member * quarter, quarter)
    own_valid = own_valid.astype(f32)[:, None]

    residual = gathered
    normed_pieces = None
    lows = []
    kept = []
    squares = []
    for l in range(LAYERS):
        normed, queries, own_kv = project(
            place, normed_pieces, gathered, w_all[l], b_all[l], rows, heads
        )
        parts = gather_blocks(own_kv)
        mixed, *pieces = attend(
            place, chosen, queries, w_mix[l], near_valid, far_valid, parts, count
        )
        residual, low_second, normed_own, branch_squares = add_norm(
            place, sum_quarters(pieces), residual, gathered, own_valid, rows, B_OUT + l, 2 * l + 1
        )
        normed_second, hidden, slope, *pieces = feed(
            place, share_quarters(normed_own), w_up[l], b_inner[l : l + 1], w_down[l]
        )
        residual, low_next, normed_own, second_squares = add_norm(
            place,
            sum_quarters(pieces),
            residual,
            gathered,
            own_valid,
            rows,
            B_DOWN + l,
            2 * l + 2 if l + 1 < LAYERS else None,
        )
        squares.append((second_squares[1], branch_squares[0], second_squares[0]))
        kept.append((normed, queries, parts, mixed, low_second, normed_second, hidden, slope))
        lows.append(low_next)
        if l + 1 < LAYERS:
            normed_pieces = share_quarters(normed_own)
    residual_out = columns(place, share_quarters(lows[-1]))

    gradient = cotangent_full
    own_low = lax.dynamic_slice_in_dim(cotangent_full, member * quarter, quarter, 0)
    grad_pieces = (cotangent_full,)
    grads = [None] * LAYERS
    sums_down = jnp.sum(own_low.astype(f32), axis=0)
    for l in reversed(range(LAYERS)):
        normed, queries, parts, mixed, low_second, normed_second, hidden, slope = kept[l]
        second_full, grad_inner, grad_b_up, *pieces = feed_back(
            place, grad_pieces, w_up[l], w_down[l], slope
        )
        grad_w_down = jnp.einsum(
            "tf,td->fd", hidden, second_full, preferred_element_type=f32
        ).astype(bf16)
        grad_w_up = jnp.einsum(
            "td,tf->df", normed_second, grad_inner, preferred_element_type=f32
        ).astype(bf16)
        gradient, low, second_sums = norm_back(
            place, sum_quarters(pieces), low_second, gradient, gathered, rows, 2 * l + 1
        )
        dq, branch_full, *kv_grads = attend_back(
            place,
            chosen,
            queries,
            w_mix[l],
            near_valid,
            far_valid,
            share_quarters(low),
            parts,
            count,
        )
        grad_w_out = jnp.einsum(
            "htc,td->hcd", mixed, branch_full, preferred_element_type=f32
        ).astype(bf16)[:, HD:].reshape(heads * HD, D)
        dkv, bias_sums, *pieces = project_back(place, dq, w_all[l], return_blocks(kv_grads))
        grad_q = jnp.einsum("td,htc->dhc", normed, dq, preferred_element_type=f32).astype(bf16)
        grad_kv = jnp.einsum("td,htc->dhc", normed, dkv, preferred_element_type=f32).astype(bf16)
        grad_w_qkv = jnp.stack(
            [
                grad_q[..., :HD].reshape(D, -1),
                grad_kv[..., :HD].reshape(D, -1),
                grad_kv[..., HD:].reshape(D, -1),
            ],
            axis=1,
        )
        gradient, low, first_sums = norm_back(
            place,
            sum_quarters(pieces),
            lows[l - 1] if l else gathered,
            gradient,
            gathered,
            rows,
            2 * l,
        )
        fed = block_sum(jnp.concatenate([grad_w_up, grad_w_down], axis=0))
        attended = block_sum(
            jnp.concatenate([grad_w_out, grad_w_qkv.reshape(-1, D)], axis=0)
        )
        out_rows = heads * HD
        weights = (
            attended[out_rows:].reshape(D, 3, out_rows),
            attended[:out_rows],
            fed[:D],
            fed[D:],
        )
        grads[l] = (
            weights,
            grad_b_up[0],
            jnp.concatenate(
                [
                    bias_sums[:heads, :HD].reshape(-1),
                    bias_sums[heads:, HD:].reshape(-1),
                    jnp.zeros((D - 2 * heads * HD,), f32),
                ]
            ),
            jnp.stack([first_sums[0], second_sums[0]]),
            jnp.stack([first_sums[1], second_sums[1]]),
            second_sums[2],
            sums_down,
        )
        sums_down = first_sums[2]
        if l:
            grad_pieces = share_quarters(low)
    grad_residual = columns(place, share_quarters(low))

    over_all = jnp.concatenate(
        [grads[l][3] for l in range(LAYERS)]
        + [grads[l][4] for l in range(LAYERS)]
        + [jnp.stack([grads[l][5] for l in range(LAYERS)])]
        + [jnp.stack([grads[l][6] for l in range(LAYERS)])]
        + [jnp.stack([vector for layer in squares for vector in layer])],
        axis=0,
    )
    over_tok = jnp.stack(
        [grads[l][1] for l in range(LAYERS)] + [grads[l][2] for l in range(LAYERS)]
    )
    packed = small_sum(
        jnp.concatenate([small_sum(over_all, ("head",)), over_tok], axis=0), ("tok",)
    )
    stat_row = 4 * LAYERS + 2 * LAYERS
    tok_row = stat_row + 3 * LAYERS
    mine = lax.dynamic_slice_in_dim(packed[:stat_row], member * width, width, 1)
    grad_ln_gain = mine[: 2 * LAYERS].reshape(LAYERS, 2, width)
    grad_ln_bias = mine[2 * LAYERS : 4 * LAYERS].reshape(LAYERS, 2, width)
    grad_b_out = mine[4 * LAYERS : 5 * LAYERS]
    grad_b_down = mine[5 * LAYERS : 6 * LAYERS]
    square_sums = jnp.sum(packed[stat_row:tok_row], axis=-1).reshape(LAYERS, 3)
    valid_count = jnp.maximum(jnp.sum(valid.astype(f32)), 1.0)
    statistics = jnp.sqrt(square_sums / (valid_count * D))
    grad_b_up = packed[tok_row : tok_row + LAYERS]
    grad_b_qv = packed[tok_row + LAYERS :, : 2 * heads * HD].reshape(LAYERS, 2, heads * HD)
    stacked = [
        jnp.stack([grads[l][0][m] for l in range(LAYERS)]) for m in range(4)
    ]
    return (
        residual_out,
        grad_residual,
        stacked[0],
        grad_b_qv,
        stacked[1],
        grad_b_out,
        stacked[2],
        grad_b_up,
        stacked[3],
        grad_b_down,
        grad_ln_gain,
        grad_ln_bias,
        statistics,
    )


def solution(mesh):
    in_specs = (
        P("tok", "head"),
        P("tok", "head"),
        P(None, None, None, "head"),
        P(None, None, "head"),
        P(None, "head", None),
        P(None, "head"),
        P(None, None, "head"),
        P(None, "head"),
        P(None, "head", None),
        P(None, "head"),
        P(None, None, "head"),
        P(None, None, "head"),
        P("head", None, None),
        P(),
        P(),
    )
    out_specs = (
        P("tok", "head"),
        P("tok", "head"),
        P(None, None, None, "head"),
        P(None, None, "head"),
        P(None, "head", None),
        P(None, "head"),
        P(None, None, "head"),
        P(None, "head"),
        P(None, "head", None),
        P(None, "head"),
        P(None, None, "head"),
        P(None, None, "head"),
        P(),
    )
    return jax.shard_map(
        on_device, mesh=mesh, in_specs=in_specs, out_specs=out_specs, check_vma=False
    )
```

```python
import functools

import jax
import jax.numpy as jnp
from jax import lax
from jax.experimental import pallas as pl
from jax.experimental.pallas import tpu as pltpu
from jax.sharding import PartitionSpec as P

D = 768
HD = 64
LAYERS = 2
WINDOW = 64
KB = 16
SEL = 4
QB = 64
WIDE = 2 * HD

epsilon = 1e-05
negative = -1e30
scale = HD ** (-0.5)
bf16 = jnp.bfloat16
f32 = jnp.float32

STEPS = (0, 2, 1, 3)
GAIN, SHIFT, B_OUT, B_DOWN, PARAM_ROWS = 0, 4, 8, 10, 16


def params(megabytes):
    return pltpu.CompilerParams(vmem_limit_bytes=megabytes * 2**20)


def cost(flops, moved, special=0):
    return pl.CostEstimate(flops=int(flops), bytes_accessed=int(moved), transcendentals=int(special))


def swap(value, axis, step):
    return lax.ppermute(value, axis, [(i, i ^ step) for i in range(lax.axis_size(axis))])


def rotate(value, axis, step):
    count = lax.axis_size(axis)
    return lax.ppermute(value, axis, [(i, (i + step) % count) for i in range(count)])


def share_quarters(own):
    across = swap(own, "head", 2)
    beside = swap(own, "head", 1)
    both = swap(across, "head", 1)
    return own, across, beside, both


def sum_quarters(pieces):
    own, across, beside, both = pieces
    first = swap(both, "head", 1)
    onward = (across.astype(f32) + first.astype(f32)).astype(bf16)
    second = swap(beside, "head", 1)
    third = swap(onward, "head", 2)
    return own, second, third


def small_sum(value, axes):
    for axis in axes:
        step = 1
        while step < lax.axis_size(axis):
            value = value + swap(value, axis, step)
            step *= 2
    return value


def ring_form(count):
    return count == 8


ORDERS = ((0, 1, 2), (1, 2, 0))


class Bundle:
    def __init__(self, halves):
        self.ring = ring_form(lax.axis_size("tok"))
        self.step = 0
        if not self.ring:
            self.result = lax.psum(halves, "tok")
            return
        self.kept = [keep for keep, give in halves]
        self.start([give for keep, give in halves], 0)

    def start(self, values, stage):
        self.coming = [
            swap(value, "tok", 1 << order[stage]) for value, order in zip(values, ORDERS)
        ]

    def advance(self, other):
        if not self.ring or self.step == 6:
            return other
        coming, other = lax.optimization_barrier((self.coming, other))
        self.step += 1
        if self.step < 3:
            self.kept, gives = fold(self.kept, coming)
            self.start(gives, self.step)
        elif self.step == 3:
            self.kept, _ = fold(self.kept, coming)
            self.start(self.kept, 2)
        elif self.step < 6:
            self.kept = join(self.kept, coming)
            self.start(self.kept, 5 - self.step)
        else:
            self.result = list(zip(self.kept, coming))
        return other


def gather_blocks(own):
    count = lax.axis_size("tok")
    if not ring_form(count):
        return [lax.all_gather(own, "tok")]
    current = own
    parts = []
    for hop in range(count // 2):
        other = swap(current, "tok", 1)
        after = None
        if hop < count // 2 - 1:
            after = rotate(current, "tok", 2)
            current, other, after = lax.optimization_barrier((current, other, after))
        parts += [current, other]
        current = after
    return parts


def return_blocks(parts, between):
    count = lax.axis_size("tok")
    if not ring_form(count):
        return [lax.psum_scatter(parts[0], "tok", scatter_dimension=0, tiled=False)]
    running = None
    for d in range(count // 2 - 1, 0, -1):
        got = swap(parts[2 * d + 1], "tok", 1)
        total = parts[2 * d].astype(f32) + got.astype(f32)
        if running is not None:
            total = total + running.astype(f32)
        running = rotate(total.astype(bf16), "tok", -2)
        if d == 2:
            running = between(running)
    return [parts[0], swap(parts[1], "tok", 1), running]


def slot_of(block, tok, count):
    if not ring_form(count):
        return block
    away = (tok >> 1) - (block >> 1)
    return 2 * jnp.maximum(away, 0) + ((tok ^ block) & 1)


ON_LANES = (((1,), (1,)), ((), ()))
ON_ROWS = (((0,), (0,)), ((), ()))


def normalise(rows):
    average = jnp.mean(rows, axis=-1, keepdims=True)
    centred = rows - average
    spread = jnp.mean(centred * centred, axis=-1, keepdims=True)
    inverse = lax.rsqrt(spread + epsilon)
    return centred * inverse, inverse


def row(ref, index):
    return ref[index : index + 1, :].astype(f32)


def piece_rows(place, step, size):
    return pl.ds(pl.multiple_of((place[0] ^ step) * size, size), size)


def project_kernel(place, *refs, heads, first):
    pieces = refs[:4]
    if first:
        param_pieces = refs[4:8]
        w_ref, bias_ref, normed_ref, q_ref, kv_ref, low_ref, param_ref, staged, turned = refs[8:]
        width = staged.shape[0] // 4
        for k in range(4):
            staged[piece_rows(place, STEPS[k], width), :] = pieces[k][...]
            turned[piece_rows(place, STEPS[k], width), :] = param_pieces[k][...].astype(f32)
        param_ref[...] = jnp.transpose(turned[...])[:PARAM_ROWS]
    else:
        w_ref, bias_ref, normed_ref, q_ref, kv_ref = refs[4:]
    size = normed_ref.shape[0] // 4
    for k in range(4):
        if first:
            rows = pl.ds(k * size, size)
            part = jnp.transpose(staged[:, k * size : (k + 1) * size].astype(f32))

            @pl.when(place[0] == k)
            def _():
                low_ref[...] = part.astype(bf16)

            unit, _ = normalise(part)
            normed = (unit * row(param_ref, GAIN) + row(param_ref, SHIFT)).astype(bf16)
        else:
            rows = piece_rows(place, STEPS[k], size)
            normed = pieces[k][...]
        normed_ref[rows, :] = normed
        projected = lax.dot_general(normed, w_ref[...], ON_LANES, preferred_element_type=f32)
        projected = projected + bias_ref[...]
        for h in range(heads):
            q_ref[h, rows, :] = (projected[:, h * WIDE : (h + 1) * WIDE] * scale).astype(bf16)
            at = (heads + h) * WIDE
            kv_ref[h, rows, :] = projected[:, at : at + WIDE].astype(bf16)


def whole(shape):
    return pl.BlockSpec(shape, lambda *_: (0,) * len(shape))


def project(place, pieces, param_pieces, w_all, bias_all, rows, heads):
    first = param_pieces is not None
    arrays = tuple(pieces) + (tuple(param_pieces) if first else ())
    columns = w_all.shape[0]
    out_shapes = [
        jax.ShapeDtypeStruct((rows, D), bf16),
        jax.ShapeDtypeStruct((heads, rows, WIDE), bf16),
        jax.ShapeDtypeStruct((heads, rows, WIDE), bf16),
    ]
    scratch = []
    if first:
        out_shapes += [
            jax.ShapeDtypeStruct((rows // 4, D), bf16),
            jax.ShapeDtypeStruct((PARAM_ROWS, D), f32),
        ]
        scratch = [pltpu.VMEM((D, rows), bf16), pltpu.VMEM((D, 128), f32)]
    return pl.pallas_call(
        functools.partial(project_kernel, heads=heads, first=first),
        grid_spec=pltpu.PrefetchScalarGridSpec(
            num_scalar_prefetch=1,
            grid=(1,),
            in_specs=[whole(array.shape) for array in arrays + (w_all, bias_all)],
            out_specs=[whole(shape.shape) for shape in out_shapes],
            scratch_shapes=scratch,
        ),
        out_shape=out_shapes,
        compiler_params=params(12),
        cost_estimate=cost(2 * rows * D * columns, 2 * D * columns + 8 * rows * D),
        name="project",
    )(place, *arrays, w_all, bias_all)


def turn_kernel(place, *refs):
    pieces = refs[:4]
    out_ref, sums_ref, staged = refs[4:]
    width = staged.shape[0] // 4
    size = out_ref.shape[0] // 4
    for k in range(4):
        staged[piece_rows(place, STEPS[k], width), :] = pieces[k][...]
    for k in range(4):
        part = jnp.transpose(staged[:, k * size : (k + 1) * size].astype(f32))
        out_ref[k * size : (k + 1) * size, :] = part.astype(bf16)

        @pl.when(place[0] == k)
        def _():
            sums_ref[...] = jnp.sum(part, axis=0, keepdims=True)


def turn(place, pieces):
    width, rows = pieces[0].shape
    return pl.pallas_call(
        turn_kernel,
        grid_spec=pltpu.PrefetchScalarGridSpec(
            num_scalar_prefetch=1,
            grid=(1,),
            in_specs=[whole((width, rows))] * 4,
            out_specs=[whole((rows, D)), whole((1, D))],
            scratch_shapes=[pltpu.VMEM((D, rows), bf16)],
        ),
        out_shape=[jax.ShapeDtypeStruct((rows, D), bf16), jax.ShapeDtypeStruct((1, D), f32)],
        compiler_params=params(6),
        cost_estimate=cost(rows * D, 4 * rows * D),
        name="turn",
    )(place, *pieces)


def fold_kernel(*refs, count):
    for half in range(2):
        kept, came = refs[2 * half : 2 * half + 2]
        keep_ref = refs[4 + half]
        total = lambda at: (kept[at].astype(f32) + came[at].astype(f32)).astype(bf16)
        if count == 1:
            keep_ref[...] = total(slice(0, 1))
        else:
            keep_ref[...] = total(slice(0, count // 2))
            refs[6 + half][...] = total(slice(count // 2, count))


def fold(kept, came):
    count = kept[0].shape[0]
    after = max(count // 2, 1)
    outs = 2 if count == 1 else 4
    shapes = [(after,) + kept[i % 2].shape[1:] for i in range(outs)]
    results = pl.pallas_call(
        functools.partial(fold_kernel, count=count),
        grid=(1,),
        in_specs=[whole(kept[i // 2].shape) for i in range(4)],
        out_specs=[whole(shape) for shape in shapes],
        out_shape=[jax.ShapeDtypeStruct(shape, bf16) for shape in shapes],
        compiler_params=params(8),
        cost_estimate=cost(2 * kept[0].size, 12 * kept[0].size),
        name="fold",
    )(kept[0], came[0], kept[1], came[1])
    return list(results[:2]), list(results[2:])


def join_kernel(*refs):
    for half in range(2):
        count = refs[half].shape[0]
        refs[4 + half][:count] = refs[half][...]
        refs[4 + half][count:] = refs[2 + half][...]


def join(kept, came):
    shapes = [(2 * array.shape[0],) + array.shape[1:] for array in kept]
    return pl.pallas_call(
        join_kernel,
        grid=(1,),
        in_specs=[whole(array.shape) for array in (*kept, *came)],
        out_specs=[whole(shape) for shape in shapes],
        out_shape=[jax.ShapeDtypeStruct(shape, bf16) for shape in shapes],
        compiler_params=params(6),
        cost_estimate=cost(kept[0].size, 16 * kept[0].size),
        name="join",
    )(*kept, *came)


def copies(parts, scratch, sems, head, buffer, rows):
    if len(parts) == 1:
        count = parts[0].shape[0]
        return [
            pltpu.make_async_copy(
                parts[0].at[slot, head],
                scratch.at[buffer, pl.ds(slot * rows, rows), :],
                sems.at[buffer, slot],
            )
            for slot in range(count)
        ]
    return [
        pltpu.make_async_copy(
            part.at[head], scratch.at[buffer, pl.ds(slot * rows, rows), :], sems.at[buffer, slot]
        )
        for slot, part in enumerate(parts)
    ]


def bring_blocks(parts, scratch, sems, heads, rows):
    head = pl.program_id(0)
    buffer = lax.rem(head, 2)

    @pl.when(head == 0)
    def _():
        for copy in copies(parts, scratch, sems, 0, 0, rows):
            copy.start()

    @pl.when(head + 1 < heads)
    def _():
        for copy in copies(parts, scratch, sems, head + 1, 1 - buffer, rows):
            copy.start()

    for copy in copies(parts, scratch, sems, head, buffer, rows):
        copy.wait()
    return head, buffer


def listed_rows(place, starts, head, b, rows):
    own, before = place[3], place[4]
    if b == 0:
        near = [
            (pl.multiple_of(before + rows - WINDOW, WINDOW), WINDOW),
            (pl.multiple_of(own, WINDOW), WINDOW),
        ]
    else:
        near = [(pl.multiple_of(own + (b - 1) * QB, WINDOW), 2 * WINDOW)]
    far = [(pl.multiple_of(starts[head, b * SEL + s], KB), KB) for s in range(SEL)]
    return near + far


def load_rows(keys, buffer, where):
    return jnp.concatenate([keys[buffer, pl.ds(start, size), :] for start, size in where], axis=0)


def mask_kernel(place, chosen, near_ref, far_ref, out_ref, *, heads, blocks):
    rows = blocks * QB
    tok, boundary = place[1], place[2]
    wide = 2 * WINDOW
    line = lax.broadcasted_iota(jnp.int32, (QB, wide), 1)
    column = lax.broadcasted_iota(jnp.int32, (QB, wide), 0)
    band = (line > column) & (line <= column + WINDOW)
    diagonal = line == column + WINDOW
    in_second = lambda position: jnp.where(position >= boundary, 1, 0)
    lane = lax.broadcasted_iota(jnp.int32, (1, SEL * KB), 1)
    for b in range(blocks):
        first = tok * rows + b * QB
        query_seq = in_second(first + lax.broadcasted_iota(jnp.int32, (QB, 1), 0))
        key = first - WINDOW + lax.broadcasted_iota(jnp.int32, (1, wide), 1)
        near = band & (diagonal | (near_ref[b : b + 1, :] > 0.0))
        near = jnp.where(near & (in_second(key) == query_seq), 0.0, negative)
        for head in range(heads):
            usable = jnp.zeros((1, SEL * KB), f32)
            token = lane & (KB - 1)
            for s in range(SEL):
                block = chosen[head, b * SEL + s]
                here = (lane >= s * KB) & (lane < (s + 1) * KB)
                early = block * KB + KB <= first - WINDOW
                usable = jnp.where(here & early, far_ref[pl.ds(block, 1), :], usable)
                token = token + jnp.where(here, block * KB, 0)
            far = (usable > 0.0) & (in_second(token) == query_seq)
            at = pl.ds(b * QB, QB)
            out_ref[head, at, :wide] = near
            out_ref[head, at, wide:] = jnp.where(far, 0.0, negative)


def masks(place, chosen, near_valid, far_valid, heads, rows):
    listed = 2 * WINDOW + SEL * KB
    return pl.pallas_call(
        functools.partial(mask_kernel, heads=heads, blocks=rows // QB),
        grid_spec=pltpu.PrefetchScalarGridSpec(
            num_scalar_prefetch=2,
            grid=(1,),
            in_specs=[whole(near_valid.shape), whole(far_valid.shape)],
            out_specs=whole((heads, rows, listed)),
        ),
        out_shape=jax.ShapeDtypeStruct((heads, rows, listed), f32),
        compiler_params=params(6),
        cost_estimate=cost(20 * heads * rows * listed, 4 * heads * rows * listed),
        name="masks",
    )(place, chosen, near_valid, far_valid)


def attend_kernel(place, starts, *refs, heads, blocks, parts):
    q_ref, w_ref, mask_ref = refs[:3]
    kv_parts = refs[3 : 3 + parts]
    mixed_ref, probs_ref = refs[3 + parts : 5 + parts]
    outs = refs[5 + parts : 9 + parts]
    keys, gathered, work, sems = refs[9 + parts :]
    rows = blocks * QB
    head, buffer = bring_blocks(kv_parts, keys, sems, heads, rows)
    blocks_at = [pl.ds(b * QB, QB) for b in range(blocks)]
    where = [listed_rows(place, starts, head, b, rows) for b in range(blocks)]
    for b, at in enumerate(blocks_at):
        kv = load_rows(keys, buffer, where[b])
        scores = lax.dot_general(q_ref[0, at, :], kv, ON_LANES, preferred_element_type=f32)
        work[at, :] = scores + mask_ref[0, at, :]
    scores = work[...]
    weights = jnp.exp(scores - jnp.max(scores, axis=-1, keepdims=True))
    weights = weights * (1.0 / jnp.sum(weights, axis=-1, keepdims=True))
    probs_ref[0] = weights.astype(bf16)
    for b, at in enumerate(blocks_at):
        kv = load_rows(keys, buffer, where[b])
        out = jnp.dot(probs_ref[0, at, :], kv, preferred_element_type=f32).astype(bf16)
        mixed_ref[0, at, :] = out
        gathered[head, at, :] = out

    @pl.when(head == heads - 1)
    def _():
        size = rows // 4
        for k in range(4):
            at = piece_rows(place, STEPS[k], size)
            mixed = jnp.concatenate([gathered[h, at, :] for h in range(heads)], axis=1)
            outs[k][...] = jnp.dot(mixed, w_ref[...], preferred_element_type=f32).astype(bf16)


def attend(place, starts, queries, w_out, mask, parts, count):
    heads, rows, _ = queries.shape
    quarter = rows // 4
    listed = mask.shape[2]
    per_head = lambda columns: pl.BlockSpec((1, rows, columns), lambda h, *_: (h, 0, 0))
    slots = count if len(parts) == 1 else len(parts)
    return pl.pallas_call(
        functools.partial(attend_kernel, heads=heads, blocks=rows // QB, parts=len(parts)),
        grid_spec=pltpu.PrefetchScalarGridSpec(
            num_scalar_prefetch=2,
            grid=(heads,),
            in_specs=[per_head(WIDE), whole(w_out.shape), per_head(listed)]
            + [pl.BlockSpec(memory_space=pl.ANY)] * len(parts),
            out_specs=[per_head(WIDE), per_head(listed)] + [whole((quarter, D))] * 4,
            scratch_shapes=[
                pltpu.VMEM((2, slots * rows, WIDE), bf16),
                pltpu.VMEM((heads, rows, WIDE), bf16),
                pltpu.VMEM((rows, listed), f32),
                pltpu.SemaphoreType.DMA((2, slots)),
            ],
        ),
        out_shape=[
            jax.ShapeDtypeStruct((heads, rows, WIDE), bf16),
            jax.ShapeDtypeStruct((heads, rows, listed), bf16),
        ]
        + [jax.ShapeDtypeStruct((quarter, D), bf16)] * 4,
        compiler_params=params(30 if len(parts) == 1 else 12),
        cost_estimate=cost(
            2 * rows * heads * WIDE * (D + 512), 2 * heads * WIDE * rows * (slots + 4)
        ),
        name="attend",
    )(place, starts, queries, w_out, mask, *parts)


def attend_back_kernel(place, starts, *refs, heads, count, blocks, parts):
    q_ref, probs_ref, w_ref = refs[:3]
    pieces = refs[3:7]
    kv_parts = refs[7 : 7 + parts]
    dq_ref, grad_ref = refs[7 + parts : 9 + parts]
    outs = refs[9 + parts : 9 + 2 * parts]
    keys, sums, mixed_ref, work, scores_ref, grads_ref, sems = refs[9 + 2 * parts :]
    rows = blocks * QB
    size = rows // 4
    head, buffer = bring_blocks(kv_parts, keys, sems, heads, rows)

    @pl.when(head == 0)
    def _():
        for k in range(4):
            grad_ref[piece_rows(place, STEPS[k], size), :] = pieces[k][...]

    sums[...] = jnp.zeros_like(sums)
    mixed_ref[...] = lax.dot_general(
        grad_ref[...], w_ref[...], ON_LANES, preferred_element_type=f32
    ).astype(bf16)
    blocks_at = [pl.ds(b * QB, QB) for b in range(blocks)]
    where = [listed_rows(place, starts, head, b, rows) for b in range(blocks)]
    for b, at in enumerate(blocks_at):
        kv = load_rows(keys, buffer, where[b])
        work[at, :] = lax.dot_general(
            mixed_ref[at, :], kv, ON_LANES, preferred_element_type=f32
        )
    weights = probs_ref[0].astype(f32)
    grad_probs = work[...]
    inner = jnp.sum(weights * grad_probs, axis=-1, keepdims=True)
    scores_ref[...] = (weights * (grad_probs - inner)).astype(bf16)
    for b, at in enumerate(blocks_at):
        kv = load_rows(keys, buffer, where[b])
        grad_q = jnp.dot(scores_ref[at, :], kv, preferred_element_type=f32)
        dq_ref[0, at, :] = (grad_q.astype(bf16).astype(f32) * scale).astype(bf16)
    for b, at in enumerate(blocks_at):
        grads_ref[b] = lax.dot_general(
            jnp.concatenate([scores_ref[at, :], probs_ref[0, at, :]], axis=0),
            jnp.concatenate([q_ref[0, at, :], mixed_ref[at, :]], axis=0),
            ON_ROWS,
            preferred_element_type=f32,
        )
    for b in range(blocks):
        done = 0
        for start, length in where[b]:
            sums[pl.ds(start, length), :] += grads_ref[b, done : done + length, :]
            done += length
    if parts == 1:
        for slot in range(count):
            outs[0][slot, 0] = sums[pl.ds(slot * rows, rows), :].astype(bf16)
    else:
        for slot in range(parts):
            outs[slot][0] = sums[pl.ds(slot * rows, rows), :].astype(bf16)


def attend_back(place, starts, queries, probs, w_out, pieces, parts, count):
    heads, rows, _ = queries.shape
    quarter = rows // 4
    listed = probs.shape[2]
    per_head = lambda columns: pl.BlockSpec((1, rows, columns), lambda h, *_: (h, 0, 0))
    slots = count if len(parts) == 1 else len(parts)
    if len(parts) == 1:
        out_specs = [pl.BlockSpec((count, 1, rows, WIDE), lambda h, *_: (0, h, 0, 0))]
    else:
        out_specs = [per_head(WIDE)] * len(parts)
    return pl.pallas_call(
        functools.partial(
            attend_back_kernel, heads=heads, count=count, blocks=rows // QB, parts=len(parts)
        ),
        grid_spec=pltpu.PrefetchScalarGridSpec(
            num_scalar_prefetch=2,
            grid=(heads,),
            in_specs=[
                per_head(WIDE),
                per_head(listed),
                pl.BlockSpec((WIDE, D), lambda h, *_: (h, 0)),
            ]
            + [whole((quarter, D))] * 4
            + [pl.BlockSpec(memory_space=pl.ANY)] * len(parts),
            out_specs=[per_head(WIDE), whole((rows, D))] + out_specs,
            scratch_shapes=[
                pltpu.VMEM((2, slots * rows, WIDE), bf16),
                pltpu.VMEM((slots * rows, WIDE), f32),
                pltpu.VMEM((rows, WIDE), bf16),
                pltpu.VMEM((rows, listed), f32),
                pltpu.VMEM((rows, listed), bf16),
                pltpu.VMEM((rows // QB, listed, WIDE), f32),
                pltpu.SemaphoreType.DMA((2, slots)),
            ],
        ),
        out_shape=[
            jax.ShapeDtypeStruct((heads, rows, WIDE), bf16),
            jax.ShapeDtypeStruct((rows, D), bf16),
        ]
        + [jax.ShapeDtypeStruct(part.shape, bf16) for part in parts],
        compiler_params=params(62 if len(parts) == 1 else 16),
        cost_estimate=cost(
            2 * rows * heads * WIDE * (D + 1536), 4 * heads * WIDE * rows * (slots + 4)
        ),
        name="attend_back",
    )(place, starts, queries, probs, w_out, *pieces, *parts)


def project_back_kernel(place, *refs, heads, terms):
    dq_ref, w_ref = refs[:2]
    kv_refs = refs[2 : 2 + terms]
    dkv_ref, bias_ref = refs[2 + terms : 4 + terms]
    outs = refs[4 + terms :]
    rows = dq_ref.shape[1]
    size = rows // 4
    for h in range(heads):
        total = kv_refs[0][h].astype(f32)
        for term in kv_refs[1:]:
            total = total + term[h].astype(f32)
        low = total.astype(bf16)
        dkv_ref[h] = low
        bias_ref[h : h + 1, :] = jnp.sum(dq_ref[h].astype(f32), axis=0, keepdims=True)
        bias_ref[heads + h : heads + h + 1, :] = jnp.sum(low.astype(f32), axis=0, keepdims=True)
    for k in range(4):
        at = piece_rows(place, STEPS[k], size)
        grads = jnp.concatenate(
            [dq_ref[h, at, :] for h in range(heads)] + [dkv_ref[h, at, :] for h in range(heads)],
            axis=1,
        )
        outs[k][...] = jnp.dot(grads, w_ref[...], preferred_element_type=f32).astype(bf16)


def project_back(place, dq, w_all, kv_terms):
    heads, rows, _ = dq.shape
    quarter = rows // 4
    return pl.pallas_call(
        functools.partial(project_back_kernel, heads=heads, terms=len(kv_terms)),
        grid_spec=pltpu.PrefetchScalarGridSpec(
            num_scalar_prefetch=1,
            grid=(1,),
            in_specs=[whole(dq.shape), whole(w_all.shape)] + [whole(dq.shape)] * len(kv_terms),
            out_specs=[whole(dq.shape), whole((2 * heads, WIDE))] + [whole((quarter, D))] * 4,
        ),
        out_shape=[
            jax.ShapeDtypeStruct(dq.shape, bf16),
            jax.ShapeDtypeStruct((2 * heads, WIDE), f32),
        ]
        + [jax.ShapeDtypeStruct((quarter, D), bf16)] * 4,
        compiler_params=params(12),
        cost_estimate=cost(4 * rows * D * heads * WIDE, 4 * D * heads * WIDE + 12 * rows * D),
        name="project_back",
    )(place, dq, w_all, *kv_terms)


def feed_kernel(place, *refs):
    pieces = refs[:4]
    up_ref, bias_ref, down_ref, kept_ref, slope_ref = refs[4:9]
    outs = refs[9:]
    size = pieces[0].shape[0]
    root = 0.7978845608028654
    cubic = 0.044715
    for k in range(4):
        at = pl.ds(k * size, size)
        normed = pieces[k][...]
        kept_ref[0, at, :] = normed
        inner = jnp.dot(normed, up_ref[...], preferred_element_type=f32) + bias_ref[...]
        square = inner * inner
        bend = jnp.tanh(root * inner * (1.0 + cubic * square))
        half = 0.5 * (1.0 + bend)
        hidden = (inner * half).astype(bf16)
        kept_ref[1, at, :] = hidden
        slope = half + 0.5 * inner * (1.0 - bend * bend) * (root * (1.0 + 3.0 * cubic * square))
        slope_ref[at, :] = slope.astype(bf16)
        outs[k][...] = jnp.dot(hidden, down_ref[...], preferred_element_type=f32).astype(bf16)


def feed(place, pieces, w_up, b_up, w_down):
    quarter = pieces[0].shape[0]
    rows = 4 * quarter
    units = w_up.shape[1]
    return pl.pallas_call(
        feed_kernel,
        grid_spec=pltpu.PrefetchScalarGridSpec(
            num_scalar_prefetch=1,
            grid=(1,),
            in_specs=[whole((quarter, D))] * 4
            + [whole(w_up.shape), whole(b_up.shape), whole(w_down.shape)],
            out_specs=[whole((2, rows, D)), whole((rows, units))] + [whole((quarter, D))] * 4,
        ),
        out_shape=[
            jax.ShapeDtypeStruct((2, rows, D), bf16),
            jax.ShapeDtypeStruct((rows, units), bf16),
        ]
        + [jax.ShapeDtypeStruct((quarter, D), bf16)] * 4,
        compiler_params=params(14),
        cost_estimate=cost(4 * rows * D * units, 4 * D * units + 10 * rows * D, rows * units),
        name="feed",
    )(place, *pieces, w_up, b_up, w_down)


def feed_back_kernel(place, *refs):
    pieces = refs[:4]
    down_ref, up_ref, slope_ref, kept_ref, bias_ref = refs[4:9]
    outs = refs[9:]
    size = pieces[0].shape[0]
    transposed = (((1,), (1,)), ((), ()))
    total = None
    for k in range(4):
        at = pl.ds(k * size, size)
        grad = pieces[k][...]
        kept_ref[1, at, :] = grad
        hidden = lax.dot_general(grad, down_ref[...], transposed, preferred_element_type=f32)
        inner = (hidden * slope_ref[at, :].astype(f32)).astype(bf16)
        kept_ref[0, at, :] = inner
        part = jnp.sum(inner.astype(f32), axis=0, keepdims=True)
        total = part if total is None else total + part
        outs[k][...] = lax.dot_general(
            inner, up_ref[...], transposed, preferred_element_type=f32
        ).astype(bf16)
    bias_ref[...] = total


def feed_back(place, pieces, w_up, w_down, slope):
    rows, units = slope.shape
    quarter = rows // 4
    if len(pieces) == 1:
        arrays = tuple(pieces) * 4
        specs = [
            pl.BlockSpec((quarter, D), lambda i, place, step=step: (place[0] ^ step, 0))
            for step in STEPS
        ]
    else:
        arrays = tuple(pieces)
        specs = [whole((quarter, D))] * 4
    return pl.pallas_call(
        feed_back_kernel,
        grid_spec=pltpu.PrefetchScalarGridSpec(
            num_scalar_prefetch=1,
            grid=(1,),
            in_specs=specs + [whole(w_down.shape), whole(w_up.shape), whole(slope.shape)],
            out_specs=[whole((2, rows, D)), whole((1, units))] + [whole((quarter, D))] * 4,
        ),
        out_shape=[
            jax.ShapeDtypeStruct((2, rows, D), bf16),
            jax.ShapeDtypeStruct((1, units), f32),
        ]
        + [jax.ShapeDtypeStruct((quarter, D), bf16)] * 4,
        compiler_params=params(14),
        cost_estimate=cost(4 * rows * D * units, 4 * D * units + 10 * rows * D),
        name="feed_back",
    )(place, *arrays, w_down, w_up, slope)


def add_norm_kernel(place, *refs, bias_row, norm_row):
    a, b, c, residual, param, valid = refs[:6]
    out_ref, low_ref, normed_ref, squares_ref = refs[6:]
    branch = a[...].astype(f32) + b[...].astype(f32) + c[...].astype(f32) + row(param, bias_row)
    total = residual[...].astype(f32) + branch
    out_ref[...] = total
    low = total.astype(bf16)
    low_ref[...] = low
    if norm_row is not None:
        unit, _ = normalise(low.astype(f32))
        gain, shift = row(param, GAIN + norm_row), row(param, SHIFT + norm_row)
        normed_ref[...] = (unit * gain + shift).astype(bf16)
    else:
        normed_ref[...] = low
    weight = valid[...]
    squares_ref[0:1, :] = jnp.sum(weight * branch * branch, axis=0, keepdims=True)
    squares_ref[1:2, :] = jnp.sum(weight * total * total, axis=0, keepdims=True)


def own_quarter(quarter):
    return pl.BlockSpec((quarter, D), lambda i, place: (place[0], 0))


def add_norm(place, terms, residual, param, valid, rows, bias_row, norm_row):
    quarter = rows // 4
    spec = whole((quarter, D))
    return pl.pallas_call(
        functools.partial(add_norm_kernel, bias_row=bias_row, norm_row=norm_row),
        grid_spec=pltpu.PrefetchScalarGridSpec(
            num_scalar_prefetch=1,
            grid=(1,),
            in_specs=[spec] * 3
            + [
                spec,
                whole((PARAM_ROWS, D)),
                whole(valid.shape),
            ],
            out_specs=[spec, spec, spec, whole((2, D))],
        ),
        out_shape=[
            jax.ShapeDtypeStruct((quarter, D), f32),
            jax.ShapeDtypeStruct((quarter, D), bf16),
            jax.ShapeDtypeStruct((quarter, D), bf16),
            jax.ShapeDtypeStruct((2, D), f32),
        ],
        compiler_params=params(4),
        cost_estimate=cost(20 * quarter * D, 18 * quarter * D),
        name="add_norm",
    )(place, *terms, residual, param, valid)


def norm_back_kernel(place, *refs, norm_row):
    a, b, c, source, gradient, param = refs[:6]
    out_ref, low_ref, sums_ref = refs[6:]
    grad_normed = a[...].astype(f32) + b[...].astype(f32) + c[...].astype(f32)
    unit, inverse = normalise(source[...].astype(f32))
    grad_unit = grad_normed * row(param, GAIN + norm_row)
    first = jnp.mean(grad_unit, axis=-1, keepdims=True)
    second = jnp.mean(grad_unit * unit, axis=-1, keepdims=True)
    total = gradient[...].astype(f32) + inverse * (grad_unit - first - unit * second)
    out_ref[...] = total
    low = total.astype(bf16)
    low_ref[...] = low
    sums_ref[0:1, :] = jnp.sum(grad_normed * unit, axis=0, keepdims=True)
    sums_ref[1:2, :] = jnp.sum(grad_normed, axis=0, keepdims=True)
    sums_ref[2:3, :] = jnp.sum(low.astype(f32), axis=0, keepdims=True)


def norm_back(place, terms, source, gradient, param, rows, norm_row):
    quarter = rows // 4
    spec = whole((quarter, D))
    pick = lambda array: spec if array.shape[0] == quarter else own_quarter(quarter)
    return pl.pallas_call(
        functools.partial(norm_back_kernel, norm_row=norm_row),
        grid_spec=pltpu.PrefetchScalarGridSpec(
            num_scalar_prefetch=1,
            grid=(1,),
            in_specs=[spec] * 3 + [pick(source), pick(gradient), whole((PARAM_ROWS, D))],
            out_specs=[spec, spec, whole((3, D))],
        ),
        out_shape=[
            jax.ShapeDtypeStruct((quarter, D), f32),
            jax.ShapeDtypeStruct((quarter, D), bf16),
            jax.ShapeDtypeStruct((3, D), f32),
        ],
        compiler_params=params(4),
        cost_estimate=cost(20 * quarter * D, 18 * quarter * D),
        name="norm_back",
    )(place, *terms, source, gradient, param)


def piece_slot(place, piece, order):
    away = piece ^ place[5]
    bit = lambda i: (away >> order[i]) & 1
    return bit(0), 2 * bit(1) + bit(2)


def put_piece(place, keep_ref, give_ref, piece, order, value):
    sent, k = piece_slot(place, piece, order)

    @pl.when(sent == 0)
    def _():
        keep_ref[k] = value

    @pl.when(sent == 1)
    def _():
        give_ref[k] = value


def take_pieces(place, keep_ref, give_ref, staged, order):
    for piece in range(8):
        sent, k = piece_slot(place, piece, order)

        @pl.when(sent == 0)
        def _():
            staged[piece] = keep_ref[k]

        @pl.when(sent == 1)
        def _():
            staged[piece] = give_ref[k]


def feed_grads_kernel(place, left_ref, right_ref, *outs):
    half = D // 2
    low = half // 2
    for w in range(2):
        for i in range(2):
            for j in range(2):
                value = lax.dot_general(
                    left_ref[w, :, i * half : (i + 1) * half],
                    right_ref[w, :, j * half : (j + 1) * half],
                    ON_ROWS,
                    preferred_element_type=f32,
                ).astype(bf16)
                for part in range(2):
                    put_piece(
                        place,
                        outs[2 * w],
                        outs[2 * w + 1],
                        4 * i + 2 * j + part,
                        ORDERS[w],
                        value[part * low : (part + 1) * low],
                    )


def pieces_call(kernel, name, place, arrays, shape, flops):
    results = pl.pallas_call(
        kernel,
        grid_spec=pltpu.PrefetchScalarGridSpec(
            num_scalar_prefetch=1,
            grid=(1,),
            in_specs=[whole(array.shape) for array in arrays],
            out_specs=[whole((4,) + shape)] * 4,
        ),
        out_shape=[jax.ShapeDtypeStruct((4,) + shape, bf16)] * 4,
        compiler_params=params(14),
        cost_estimate=cost(flops, 2 * sum(array.size for array in arrays)),
        name=name,
    )(place, *arrays)
    return [results[:2], results[2:]]


def feed_grads(place, left, right):
    rows = left.shape[1]
    return pieces_call(
        feed_grads_kernel, "feed_grads", place, (left, right), (D // 4, D // 2), 4 * rows * D * D
    )


def mix_grads_kernel(place, normed_ref, dq_ref, dkv_ref, mixed_ref, grad_ref, *outs):
    heads = dq_ref.shape[0]
    half = D // 2
    low = heads * HD // 2
    for j in range(2):
        at = slice(j * half, (j + 1) * half)
        product = lambda left, right: [
            lax.dot_general(
                left[h], right[:, at], ON_ROWS, preferred_element_type=f32
            ).astype(bf16)
            for h in range(heads)
        ]
        join_heads = lambda parts, first: jnp.concatenate(
            [part[first : first + HD] for part in parts], axis=0
        )
        queries = product(dq_ref, normed_ref)
        pairs = product(dkv_ref, normed_ref)
        mixes = product(mixed_ref, grad_ref)
        values = (
            join_heads(queries, 0),
            join_heads(pairs, 0),
            join_heads(pairs, HD),
            join_heads(mixes, HD),
        )
        for g, value in enumerate(values):
            for part in range(2):
                put_piece(
                    place,
                    outs[2 * j],
                    outs[2 * j + 1],
                    2 * g + part,
                    ORDERS[j],
                    value[part * low : (part + 1) * low],
                )


def mix_grads(place, normed, dq, dkv, mixed, grad):
    heads, rows, _ = dq.shape
    return pieces_call(
        mix_grads_kernel,
        "mix_grads",
        place,
        (normed, dq, dkv, mixed, grad),
        (heads * HD // 2, D // 2),
        6 * rows * D * heads * WIDE,
    )


def feed_place_kernel(place, *refs):
    up_ref, down_ref, staged = refs[-3:]
    half = D // 2
    low = half // 2
    for w, out in enumerate((up_ref, down_ref)):
        take_pieces(place, refs[2 * w], refs[2 * w + 1], staged, ORDERS[w])
        for piece in range(8):
            i, j, part = piece // 4, (piece // 2) % 2, piece % 2
            top = i * half + part * low
            out[0, top : top + low, j * half : (j + 1) * half] = staged[piece].astype(f32)


def mix_place_kernel(place, *refs):
    qkv_ref, out_ref, staged = refs[-3:]
    half = D // 2
    low = staged.shape[1]
    for j in range(2):
        take_pieces(place, refs[2 * j], refs[2 * j + 1], staged, ORDERS[j])
        at = slice(j * half, (j + 1) * half)
        for piece in range(8):
            g, part = piece // 2, piece % 2
            rows = slice(part * low, (part + 1) * low)
            value = staged[piece].astype(f32)
            if g < 3:
                qkv_ref[0, g, rows, at] = value
            else:
                out_ref[0, rows, at] = value


def place_call(kernel, name, place, halves, earlier, shapes, layer):
    arrays = [array for half in halves for array in half]
    specs = [
        pl.BlockSpec((1,) + shape, lambda *_, rank=len(shape): (layer,) + (0,) * rank)
        for shape in shapes
    ]
    kept = [pl.BlockSpec(memory_space=pl.ANY)] * len(earlier)
    return pl.pallas_call(
        kernel,
        grid_spec=pltpu.PrefetchScalarGridSpec(
            num_scalar_prefetch=1,
            grid=(1,),
            in_specs=[whole(array.shape) for array in arrays] + kept,
            out_specs=specs,
            scratch_shapes=[pltpu.VMEM((8,) + arrays[0].shape[1:], bf16)],
        ),
        out_shape=[jax.ShapeDtypeStruct((LAYERS,) + shape, f32) for shape in shapes],
        input_output_aliases={5 + i: i for i in range(len(earlier))},
        compiler_params=params(18),
        cost_estimate=cost(4 * arrays[0].size, 24 * arrays[0].size),
        name=name,
    )(place, *arrays, *earlier)


def columns_kernel(place, *refs):
    pieces, out = refs[:4], refs[4]
    size = pieces[0].shape[0]
    width = out.shape[0]
    for p in range(4):

        @pl.when(place[0] == p)
        def _():
            for k in range(4):
                part = pieces[k][:, p * width : (p + 1) * width].astype(f32)
                q = p ^ STEPS[k]
                out[:, q * size : (q + 1) * size] = jnp.transpose(part).astype(bf16)


def columns(place, pieces):
    quarter = pieces[0].shape[0]
    return pl.pallas_call(
        columns_kernel,
        grid_spec=pltpu.PrefetchScalarGridSpec(
            num_scalar_prefetch=1,
            grid=(1,),
            in_specs=[whole((quarter, D))] * 4,
            out_specs=whole((D // 4, 4 * quarter)),
        ),
        out_shape=jax.ShapeDtypeStruct((D // 4, 4 * quarter), bf16),
        compiler_params=params(4),
        cost_estimate=cost(quarter * D, 16 * quarter * D),
        name="columns",
    )(place, *pieces)


def on_device(
    residual_in,
    cotangent,
    w_qkv,
    b_qv,
    w_out,
    b_out,
    w_up,
    b_up,
    w_down,
    b_down,
    ln_gain,
    ln_bias,
    selection,
    lengths,
    valid,
):
    rows = residual_in.shape[0]
    heads = selection.shape[0]
    blocks = rows // QB
    quarter = rows // 4
    count = lax.axis_size("tok")
    position = lax.axis_index("tok")
    member = lax.axis_index("head")
    width = D // 4
    first_row = position * rows
    chosen = lax.dynamic_slice_in_dim(selection, position * blocks, blocks, 1).reshape(heads, -1)
    per_device = rows // KB
    starts = slot_of(chosen // per_device, position, count) * rows + (chosen % per_device) * KB
    place = jnp.stack(
        [
            member,
            position,
            lengths[0],
            slot_of(position, position, count) * rows,
            slot_of(jnp.maximum(position - 1, 0), position, count) * rows,
            position if ring_form(count) else 0,
        ]
    ).astype(jnp.int32)

    first_pieces = share_quarters(residual_in.T)
    small = jnp.concatenate(
        [ln_gain.reshape(-1, width), ln_bias.reshape(-1, width), b_out, b_down], axis=0
    )
    small = jnp.pad(small, ((0, 128 - small.shape[0]), (0, 0)))
    param_pieces = share_quarters(small.T)

    split = jnp.transpose(w_qkv, (0, 2, 3, 1)).reshape(LAYERS, 3, heads, HD, D)
    w_all = jnp.concatenate(
        [
            jnp.pad(split[:, 0], ((0, 0), (0, 0), (0, WIDE - HD), (0, 0))),
            jnp.concatenate([split[:, 1], split[:, 2]], axis=2),
        ],
        axis=1,
    ).reshape(LAYERS, 2 * heads * WIDE, D)
    b_split = b_qv.reshape(LAYERS, 2, heads, HD)
    b_all = (
        jnp.concatenate(
            [
                jnp.pad(b_split[:, 0], ((0, 0), (0, 0), (0, HD))),
                jnp.pad(b_split[:, 1], ((0, 0), (0, 0), (HD, 0))),
            ],
            axis=1,
        )
        .reshape(LAYERS, 1, 2 * heads * WIDE)
        .astype(f32)
    )
    w_mix = jnp.pad(
        w_out.reshape(LAYERS, heads, HD, D), ((0, 0), (0, 0), (HD, 0), (0, 0))
    ).reshape(LAYERS, heads * WIDE, D)
    b_inner = b_up.astype(f32)

    far_valid = jnp.tile(valid.reshape(-1, KB), (1, SEL)).astype(f32)
    padded = jnp.concatenate([jnp.zeros((WINDOW,), jnp.int32), valid])
    near = lax.dynamic_slice_in_dim(padded, first_row, rows + WINDOW).reshape(-1, WINDOW)
    near_valid = jnp.concatenate([near[:-1], near[1:]], axis=1).astype(f32)
    own_valid = lax.dynamic_slice_in_dim(valid, first_row + member * quarter, quarter)
    own_valid = own_valid.astype(f32)[:, None]
    mask = masks(place, chosen, near_valid, far_valid, heads, rows)

    pieces = first_pieces
    lows = []
    kept = []
    squares = []
    for l in range(LAYERS):
        normed, queries, own_kv, *first = project(
            place, pieces, None if l else param_pieces, w_all[l], b_all[l], rows, heads
        )
        if l == 0:
            low_first, param = first
            residual = low_first
        parts = gather_blocks(own_kv)
        mixed, probs, *pieces = attend(place, starts, queries, w_mix[l], mask, parts, count)
        residual, low_second, normed_own, branch_squares = add_norm(
            place, sum_quarters(pieces), residual, param, own_valid, rows, B_OUT + l, 2 * l + 1
        )
        fed, slope, *pieces = feed(
            place, share_quarters(normed_own), w_up[l], b_inner[l : l + 1], w_down[l]
        )
        residual, low_next, normed_own, second_squares = add_norm(
            place,
            sum_quarters(pieces),
            residual,
            param,
            own_valid,
            rows,
            B_DOWN + l,
            2 * l + 2 if l + 1 < LAYERS else None,
        )
        squares.append((second_squares[1], branch_squares[0], second_squares[0]))
        kept.append((normed, queries, parts, mixed, probs, low_second, fed, slope))
        lows.append(low_next)
        if l + 1 < LAYERS:
            pieces = share_quarters(normed_own)
    residual_out = columns(place, share_quarters(lows[-1])).T

    gradient, sums_down = turn(place, share_quarters(cotangent.T))
    sums_down = sums_down[0]
    grad_pieces = (gradient,)
    grads = [None] * LAYERS
    placed_feed = placed_mix = ()
    shapes_feed = ((D, D), (D, D))
    shapes_mix = ((3, heads * HD, D), (heads * HD, D))
    mix_bundle = None
    feed_bundle = None
    nothing = lambda other: other
    for l in reversed(range(LAYERS)):
        normed, queries, parts, mixed, probs, low_second, fed, slope = kept[l]
        last_feed = feed_bundle.advance if feed_bundle else nothing
        last_mix = mix_bundle.advance if mix_bundle else nothing
        fed_back, grad_b_up, *pieces = feed_back(place, grad_pieces, w_up[l], w_down[l], slope)
        halves = feed_grads(place, fed, fed_back)
        terms, halves = lax.optimization_barrier((sum_quarters(pieces), halves))
        terms = last_feed(last_mix(terms))
        feed_bundle = Bundle(halves)
        gradient, low, second_sums = norm_back(
            place, terms, low_second, gradient, param, rows, 2 * l + 1
        )
        pieces = last_feed(last_mix(share_quarters(low)))
        if l + 1 < LAYERS:
            placed_feed = place_call(
                feed_place_kernel,
                "feed_place",
                place,
                old_feed.result,
                placed_feed,
                shapes_feed,
                l + 1,
            )
        dq, branch_full, *kv_grads = attend_back(
            place, starts, queries, probs, w_mix[l], pieces, parts, count
        )
        kv_grads = feed_bundle.advance(last_mix(kv_grads))
        kv_terms = return_blocks(
            kv_grads, lambda other: feed_bundle.advance(other)
        )
        kv_terms = feed_bundle.advance(last_mix(kv_terms))
        dkv, bias_sums, *pieces = project_back(place, dq, w_all[l], kv_terms)
        halves = mix_grads(place, normed, dq, dkv, mixed, branch_full)
        terms, halves = lax.optimization_barrier((sum_quarters(pieces), halves))
        terms = feed_bundle.advance(last_mix(terms))
        if l + 1 < LAYERS:
            placed_mix = place_call(
                mix_place_kernel, "mix_place", place, mix_bundle.result, placed_mix, shapes_mix, l + 1
            )
        mix_bundle = Bundle(halves)
        gradient, low, first_sums = norm_back(
            place, terms, lows[l - 1] if l else low_first, gradient, param, rows, 2 * l
        )
        pieces = share_quarters(low)
        if l:
            grad_pieces = mix_bundle.advance(pieces)
            old_feed = feed_bundle
        grads[l] = (
            None,
            grad_b_up[0],
            jnp.concatenate(
                [
                    bias_sums[:heads, :HD].reshape(-1),
                    bias_sums[heads:, HD:].reshape(-1),
                    jnp.zeros((D - 2 * heads * HD,), f32),
                ]
            ),
            jnp.stack([first_sums[0], second_sums[0]]),
            jnp.stack([first_sums[1], second_sums[1]]),
            second_sums[2],
            sums_down,
        )
        sums_down = first_sums[2]
    grad_residual = columns(place, pieces).T
    for bundle in (feed_bundle, mix_bundle):
        while bundle.ring and bundle.step < 6:
            bundle.advance(())
    placed_feed = place_call(
        feed_place_kernel, "feed_place", place, feed_bundle.result, placed_feed, shapes_feed, 0
    )
    placed_mix = place_call(
        mix_place_kernel, "mix_place", place, mix_bundle.result, placed_mix, shapes_mix, 0
    )

    over_all = jnp.concatenate(
        [grads[l][3] for l in range(LAYERS)]
        + [grads[l][4] for l in range(LAYERS)]
        + [jnp.stack([grads[l][5] for l in range(LAYERS)])]
        + [jnp.stack([grads[l][6] for l in range(LAYERS)])]
        + [jnp.stack([vector for layer in squares for vector in layer])],
        axis=0,
    )
    over_tok = jnp.stack(
        [grads[l][1] for l in range(LAYERS)] + [grads[l][2] for l in range(LAYERS)]
    )
    packed = small_sum(
        jnp.concatenate([small_sum(over_all, ("head",)), over_tok], axis=0), ("tok",)
    )
    stat_row = 4 * LAYERS + 2 * LAYERS
    tok_row = stat_row + 3 * LAYERS
    mine = lax.dynamic_slice_in_dim(packed[:stat_row], member * width, width, 1)
    grad_ln_gain = mine[: 2 * LAYERS].reshape(LAYERS, 2, width)
    grad_ln_bias = mine[2 * LAYERS : 4 * LAYERS].reshape(LAYERS, 2, width)
    grad_b_out = mine[4 * LAYERS : 5 * LAYERS]
    grad_b_down = mine[5 * LAYERS : 6 * LAYERS]
    square_sums = jnp.sum(packed[stat_row:tok_row], axis=-1).reshape(LAYERS, 3)
    valid_count = jnp.maximum(jnp.sum(valid.astype(f32)), 1.0)
    statistics = jnp.sqrt(square_sums / (valid_count * D))
    grad_b_up = packed[tok_row : tok_row + LAYERS]
    grad_b_qv = packed[tok_row + LAYERS :, : 2 * heads * HD].reshape(LAYERS, 2, heads * HD)
    return (
        residual_out,
        grad_residual,
        jnp.transpose(placed_mix[0], (0, 3, 1, 2)),
        grad_b_qv,
        placed_mix[1],
        grad_b_out,
        placed_feed[0],
        grad_b_up,
        placed_feed[1],
        grad_b_down,
        grad_ln_gain,
        grad_ln_bias,
        statistics,
    )


def solution(mesh):
    in_specs = (
        P("tok", "head"),
        P("tok", "head"),
        P(None, None, None, "head"),
        P(None, None, "head"),
        P(None, "head", None),
        P(None, "head"),
        P(None, None, "head"),
        P(None, "head"),
        P(None, "head", None),
        P(None, "head"),
        P(None, None, "head"),
        P(None, None, "head"),
        P("head", None, None),
        P(),
        P(),
    )
    out_specs = (
        P("tok", "head"),
        P("tok", "head"),
        P(None, None, None, "head"),
        P(None, None, "head"),
        P(None, "head", None),
        P(None, "head"),
        P(None, None, "head"),
        P(None, "head"),
        P(None, "head", None),
        P(None, "head"),
        P(None, None, "head"),
        P(None, None, "head"),
        P(),
    )
    return jax.shard_map(
        on_device, mesh=mesh, in_specs=in_specs, out_specs=out_specs, check_vma=False
    )
```

```python
import functools

import jax
import jax.numpy as jnp
from jax import lax
from jax.experimental import pallas as pl
from jax.experimental.pallas import tpu as pltpu
from jax.sharding import PartitionSpec as P

D = 768
HD = 64
LAYERS = 2
WINDOW = 64
KB = 16
SEL = 4
QB = 64
WIDE = 2 * HD

epsilon = 1e-05
negative = -1e30
scale = HD ** (-0.5)
bf16 = jnp.bfloat16
f32 = jnp.float32

STEPS = (0, 2, 1, 3)
GAIN, SHIFT, B_OUT, B_DOWN, PARAM_ROWS = 0, 4, 8, 10, 16


def params(megabytes):
    return pltpu.CompilerParams(vmem_limit_bytes=megabytes * 2**20)


def cost(flops, moved, special=0):
    return pl.CostEstimate(flops=int(flops), bytes_accessed=int(moved), transcendentals=int(special))


def swap(value, axis, step):
    return lax.ppermute(value, axis, [(i, i ^ step) for i in range(lax.axis_size(axis))])


def rotate(value, axis, step):
    count = lax.axis_size(axis)
    return lax.ppermute(value, axis, [(i, (i + step) % count) for i in range(count)])


def share_features(own):
    across = swap(own, "head", 2)
    beside = swap(own, "head", 1)
    both = swap(across, "head", 1)
    return own, across, beside, both


def share_rows(own):
    return own, swap(own, "head", 1)


def sum_rows(pieces):
    own, other = pieces
    chip = (own.astype(f32) + swap(other, "head", 1).astype(f32)).astype(bf16)
    return chip, swap(chip, "head", 2)


def small_sum(value, axis):
    step = 1
    while step < lax.axis_size(axis):
        value = value + swap(value, axis, step)
        step *= 2
    return value


def finish_in_turn(other, *bundles):
    if not bundles[0].ring:
        return
    turns = {True: [], False: []}
    for index in TURNS:
        bundle = bundles[index]
        if bundle.step == 6:
            continue
        stage = bundle.step if bundle.step < 3 else 5 - bundle.step
        queue = turns[bundle.order[stage] == 0]
        depth = COLUMN_DEPTH if bundle.order[stage] == 0 else Z_DEPTH
        bundle.send(queue[-depth] if len(queue) >= depth else other)
        queue.append(bundle.coming)


def ring_form(count):
    return count == 8


COLUMN_FIRST = (0, 1, 2)

TURNS = (0, 1, 2, 5, 3, 0, 2, 4, 1, 3, 2, 5, 3, 2, 4, 3, 5, 3, 4, 4, 4, 5, 5, 5)
COLUMN_DEPTH, Z_DEPTH = 2, 3


def after(value, other):
    return lax.optimization_barrier((value, other))[0]


class Bundle:
    def __init__(self, pieces, order):
        self.ring = ring_form(lax.axis_size("tok"))
        self.step, self.order = 0, order
        self.kept, self.out = pieces
        if not self.ring:
            self.result = lax.psum(tuple(pieces), "tok")

    def send(self, other=None):
        if not self.ring or self.step == 6:
            return
        if self.step:
            kept, came = self.kept, self.coming
            if other is not None:
                kept, came = after((kept, came), other)
            if self.step < 3:
                self.kept, self.out = merge("split", kept, came)
            else:
                (self.kept,) = merge("add" if self.step == 3 else "join", kept, came)
                self.out = self.kept
        stage = self.step if self.step < 3 else 5 - self.step
        self.coming = swap(self.out, "tok", 1 << self.order[stage])
        self.step += 1

    def take(self, other):
        if not self.ring:
            return other
        self.coming, other = lax.optimization_barrier((self.coming, other))
        return other

    def finish(self):
        while self.ring and self.step < 6:
            self.send()
        if self.ring:
            self.result = (self.kept, self.coming)
        return self.result


def gather_blocks(chunks):
    count = lax.axis_size("tok")
    if not ring_form(count):
        return [lax.all_gather(chunk, "tok") for chunk in chunks]
    parts = [None] * (2 * count)
    for k, current in enumerate(chunks):
        for hop in range(count // 2):
            other = swap(current, "tok", 1)
            after = None
            if hop < count // 2 - 1:
                after = rotate(current, "tok", 2)
                current, other, after = lax.optimization_barrier((current, other, after))
            parts[4 * hop + k] = current
            parts[4 * hop + 2 + k] = other
            current = after
    return parts


def return_blocks(parts, meanwhile):
    count = lax.axis_size("tok")
    if not ring_form(count):
        return [
            [lax.psum_scatter(part, "tok", scatter_dimension=0, tiled=False)] for part in parts
        ]
    running = [None, None]
    own = [None, None]
    got = [None, None]
    for d in range(count // 2 - 1, -1, -1):
        for k in range(2):
            mine, other = parts[4 * d + k], parts[4 * d + 2 + k]
            if got[k] is not None:
                other, got[k] = lax.optimization_barrier((other, got[k]))
                total = own[k].astype(f32) + got[k].astype(f32)
                if running[k] is not None:
                    total = total + running[k].astype(f32)
                running[k] = rotate(total.astype(bf16), "tok", -2)
            own[k], got[k] = mine, swap(other, "tok", 1)
        if d == 1:
            running = meanwhile(running)
    return [[own[k], got[k], running[k]] for k in range(2)]


def slot_of(block, tok, count):
    if not ring_form(count):
        return block
    away = (tok >> 1) - (block >> 1)
    return 2 * jnp.maximum(away, 0) + ((tok ^ block) & 1)


ON_LANES = (((1,), (1,)), ((), ()))
ON_ROWS = (((0,), (0,)), ((), ()))


def normalise(rows):
    average = jnp.mean(rows, axis=-1, keepdims=True)
    centred = rows - average
    spread = jnp.mean(centred * centred, axis=-1, keepdims=True)
    inverse = lax.rsqrt(spread + epsilon)
    return centred * inverse, inverse


def row(ref, index):
    return ref[index : index + 1, :].astype(f32)


def piece_rows(place, step, size):
    return pl.ds(pl.multiple_of((place[0] ^ step) * size, size), size)


def half_rows(place, k, size):
    return pl.ds(pl.multiple_of(((place[0] & 1) ^ k) * size, size), size)


def project_kernel(place, *refs, heads, first):
    if first:
        pieces, param_pieces = refs[:4], refs[4:8]
        w_ref, bias_ref, normed_ref, q_ref = refs[8:12]
        kv_refs = refs[12:14]
        low_ref, param_ref, staged, turned = refs[14:]
        width = staged.shape[0] // 4
        for k in range(4):
            staged[piece_rows(place, STEPS[k], width), :] = pieces[k][...]
            turned[piece_rows(place, STEPS[k], width), :] = param_pieces[k][...].astype(f32)
        param_ref[...] = jnp.transpose(turned[...])[:PARAM_ROWS]
    else:
        pieces = refs[:2]
        w_ref, bias_ref, normed_ref, q_ref = refs[2:6]
        kv_refs = refs[6:]
    size = normed_ref.shape[0] // 2
    for k in range(2):
        rows = half_rows(place, k, size)
        if first:
            part = jnp.transpose(staged[:, rows].astype(f32))
            if k == 0:
                low_ref[...] = part.astype(bf16)
            unit, _ = normalise(part)
            normed = (unit * row(param_ref, GAIN) + row(param_ref, SHIFT)).astype(bf16)
        else:
            normed = pieces[k][...]
        normed_ref[rows, :] = normed
        projected = lax.dot_general(normed, w_ref[...], ON_LANES, preferred_element_type=f32)
        projected = projected + bias_ref[...]
        for h in range(heads):
            q_ref[h, rows, :] = (projected[:, h * WIDE : (h + 1) * WIDE] * scale).astype(bf16)
            at = (heads + h) * WIDE
            kv_refs[k][h] = projected[:, at : at + WIDE].astype(bf16)


def whole(shape):
    return pl.BlockSpec(shape, lambda *_: (0,) * len(shape))


def project(place, pieces, param_pieces, w_all, bias_all, rows, heads):
    first = param_pieces is not None
    arrays = tuple(pieces) + (tuple(param_pieces) if first else ())
    columns = w_all.shape[0]
    out_shapes = [
        jax.ShapeDtypeStruct((rows, D), bf16),
        jax.ShapeDtypeStruct((heads, rows, WIDE), bf16),
        jax.ShapeDtypeStruct((heads, rows // 2, WIDE), bf16),
        jax.ShapeDtypeStruct((heads, rows // 2, WIDE), bf16),
    ]
    scratch = []
    if first:
        out_shapes += [
            jax.ShapeDtypeStruct((rows // 2, D), bf16),
            jax.ShapeDtypeStruct((PARAM_ROWS, D), f32),
        ]
        scratch = [pltpu.VMEM((D, rows), bf16), pltpu.VMEM((D, 128), f32)]
    return pl.pallas_call(
        functools.partial(project_kernel, heads=heads, first=first),
        grid_spec=pltpu.PrefetchScalarGridSpec(
            num_scalar_prefetch=1,
            grid=(1,),
            in_specs=[whole(array.shape) for array in arrays + (w_all, bias_all)],
            out_specs=[whole(shape.shape) for shape in out_shapes],
            scratch_shapes=scratch,
        ),
        out_shape=out_shapes,
        compiler_params=params(12),
        cost_estimate=cost(2 * rows * D * columns, 2 * D * columns + 8 * rows * D),
        name="project",
    )(place, *arrays, w_all, bias_all)


def turn_kernel(place, *refs):
    pieces = refs[:4]
    out_ref, sums_ref, staged = refs[4:]
    width = staged.shape[0] // 4
    size = out_ref.shape[0] // 2
    for k in range(4):
        staged[piece_rows(place, STEPS[k], width), :] = pieces[k][...]
    for k in range(2):
        part = jnp.transpose(staged[:, k * size : (k + 1) * size].astype(f32))
        out_ref[k * size : (k + 1) * size, :] = part.astype(bf16)

        @pl.when((place[0] & 1) == k)
        def _():
            sums_ref[...] = jnp.sum(part, axis=0, keepdims=True)


def turn(place, pieces):
    width, rows = pieces[0].shape
    return pl.pallas_call(
        turn_kernel,
        grid_spec=pltpu.PrefetchScalarGridSpec(
            num_scalar_prefetch=1,
            grid=(1,),
            in_specs=[whole((width, rows))] * 4,
            out_specs=[whole((rows, D)), whole((1, D))],
            scratch_shapes=[pltpu.VMEM((D, rows), bf16)],
        ),
        out_shape=[jax.ShapeDtypeStruct((rows, D), bf16), jax.ShapeDtypeStruct((1, D), f32)],
        compiler_params=params(6),
        cost_estimate=cost(rows * D, 4 * rows * D),
        name="turn",
    )(place, *pieces)


def merge_kernel(kept, came, *outs, act):
    count = kept.shape[0]
    if act == "join":
        outs[0][:count] = kept[...]
        outs[0][count:] = came[...]
        return
    each = count // len(outs)
    for i, out in enumerate(outs):
        at = slice(i * each, (i + 1) * each)
        out[...] = (kept[at].astype(f32) + came[at].astype(f32)).astype(bf16)


def merge(act, kept, came):
    count = kept.shape[0]
    counts = {"add": [count], "split": [count // 2] * 2, "join": [2 * count]}[act]
    shapes = [(n,) + kept.shape[1:] for n in counts]
    return pl.pallas_call(
        functools.partial(merge_kernel, act=act),
        grid=(1,),
        in_specs=[whole(kept.shape)] * 2,
        out_specs=[whole(shape) for shape in shapes],
        out_shape=[jax.ShapeDtypeStruct(shape, bf16) for shape in shapes],
        compiler_params=params(8),
        cost_estimate=cost(kept.size, 8 * kept.size),
        name="merge",
    )(kept, came)


def chunk_rows(place, slot, k, rows):
    return pl.ds(pl.multiple_of(slot * rows + ((place[0] & 1) ^ k) * (rows // 2), rows // 2), rows // 2)


def copies(place, parts, scratch, sems, head, buffer, rows):
    if len(parts) == 2:
        sources = [parts[k].at[slot, head] for slot in range(parts[0].shape[0]) for k in range(2)]
    else:
        sources = [part.at[head] for part in parts]
    return [
        pltpu.make_async_copy(
            source,
            scratch.at[buffer, chunk_rows(place, i // 2, i % 2, rows), :],
            sems.at[buffer, i],
        )
        for i, source in enumerate(sources)
    ]


def bring_blocks(place, parts, scratch, sems, heads, rows):
    head = pl.program_id(0)
    buffer = lax.rem(head, 2)

    @pl.when(head == 0)
    def _():
        for copy in copies(place, parts, scratch, sems, 0, 0, rows):
            copy.start()

    @pl.when(head + 1 < heads)
    def _():
        for copy in copies(place, parts, scratch, sems, head + 1, 1 - buffer, rows):
            copy.start()

    for copy in copies(place, parts, scratch, sems, head, buffer, rows):
        copy.wait()
    return head, buffer


def listed_rows(place, starts, head, b, rows):
    own, before = place[3], place[4]
    if b == 0:
        near = [
            (pl.multiple_of(before + rows - WINDOW, WINDOW), WINDOW),
            (pl.multiple_of(own, WINDOW), WINDOW),
        ]
    else:
        near = [(pl.multiple_of(own + (b - 1) * QB, WINDOW), 2 * WINDOW)]
    far = [(pl.multiple_of(starts[head, b * SEL + s], KB), KB) for s in range(SEL)]
    return near + far


def load_rows(keys, buffer, where):
    return jnp.concatenate([keys[buffer, pl.ds(start, size), :] for start, size in where], axis=0)


def mask_kernel(place, chosen, near_ref, far_ref, out_ref, *, heads, blocks):
    rows = blocks * QB
    tok, boundary = place[1], place[2]
    wide = 2 * WINDOW
    line = lax.broadcasted_iota(jnp.int32, (QB, wide), 1)
    column = lax.broadcasted_iota(jnp.int32, (QB, wide), 0)
    band = (line > column) & (line <= column + WINDOW)
    diagonal = line == column + WINDOW
    in_second = lambda position: jnp.where(position >= boundary, 1, 0)
    lane = lax.broadcasted_iota(jnp.int32, (1, SEL * KB), 1)
    for b in range(blocks):
        first = tok * rows + b * QB
        query_seq = in_second(first + lax.broadcasted_iota(jnp.int32, (QB, 1), 0))
        key = first - WINDOW + lax.broadcasted_iota(jnp.int32, (1, wide), 1)
        near = band & (diagonal | (near_ref[b : b + 1, :] > 0.0))
        near = jnp.where(near & (in_second(key) == query_seq), 0.0, negative)
        for head in range(heads):
            usable = jnp.zeros((1, SEL * KB), f32)
            token = lane & (KB - 1)
            for s in range(SEL):
                block = chosen[head, b * SEL + s]
                here = (lane >= s * KB) & (lane < (s + 1) * KB)
                early = block * KB + KB <= first - WINDOW
                usable = jnp.where(here & early, far_ref[pl.ds(block, 1), :], usable)
                token = token + jnp.where(here, block * KB, 0)
            far = (usable > 0.0) & (in_second(token) == query_seq)
            at = pl.ds(b * QB, QB)
            out_ref[head, at, :wide] = near
            out_ref[head, at, wide:] = jnp.where(far, 0.0, negative)


def masks(place, chosen, near_valid, far_valid, heads, rows):
    listed = 2 * WINDOW + SEL * KB
    return pl.pallas_call(
        functools.partial(mask_kernel, heads=heads, blocks=rows // QB),
        grid_spec=pltpu.PrefetchScalarGridSpec(
            num_scalar_prefetch=2,
            grid=(1,),
            in_specs=[whole(near_valid.shape), whole(far_valid.shape)],
            out_specs=whole((heads, rows, listed)),
        ),
        out_shape=jax.ShapeDtypeStruct((heads, rows, listed), f32),
        compiler_params=params(6),
        cost_estimate=cost(20 * heads * rows * listed, 4 * heads * rows * listed),
        name="masks",
    )(place, chosen, near_valid, far_valid)


def attend_kernel(place, starts, *refs, heads, blocks, parts):
    q_ref, w_ref, mask_ref = refs[:3]
    kv_parts = refs[3 : 3 + parts]
    mixed_ref, probs_ref = refs[3 + parts : 5 + parts]
    outs = refs[5 + parts : 7 + parts]
    keys, gathered, work, sems = refs[7 + parts :]
    rows = blocks * QB
    head, buffer = bring_blocks(place, kv_parts, keys, sems, heads, rows)
    blocks_at = [pl.ds(b * QB, QB) for b in range(blocks)]
    where = [listed_rows(place, starts, head, b, rows) for b in range(blocks)]
    for b, at in enumerate(blocks_at):
        kv = load_rows(keys, buffer, where[b])
        scores = lax.dot_general(q_ref[0, at, :], kv, ON_LANES, preferred_element_type=f32)
        work[at, :] = scores + mask_ref[0, at, :]
    scores = work[...]
    weights = jnp.exp(scores - jnp.max(scores, axis=-1, keepdims=True))
    weights = weights * (1.0 / jnp.sum(weights, axis=-1, keepdims=True))
    probs_ref[0] = weights.astype(bf16)
    for b, at in enumerate(blocks_at):
        kv = load_rows(keys, buffer, where[b])
        out = jnp.dot(probs_ref[0, at, :], kv, preferred_element_type=f32).astype(bf16)
        mixed_ref[0, at, :] = out
        gathered[head, at, :] = out

    @pl.when(head == heads - 1)
    def _():
        size = rows // 2
        for k in range(2):
            at = half_rows(place, k, size)
            mixed = jnp.concatenate([gathered[h, at, :] for h in range(heads)], axis=1)
            outs[k][...] = jnp.dot(mixed, w_ref[...], preferred_element_type=f32).astype(bf16)


def attend(place, starts, queries, w_out, mask, parts, count):
    heads, rows, _ = queries.shape
    listed = mask.shape[2]
    per_head = lambda columns: pl.BlockSpec((1, rows, columns), lambda h, *_: (h, 0, 0))
    slots = count if len(parts) == 2 else len(parts) // 2
    return pl.pallas_call(
        functools.partial(attend_kernel, heads=heads, blocks=rows // QB, parts=len(parts)),
        grid_spec=pltpu.PrefetchScalarGridSpec(
            num_scalar_prefetch=2,
            grid=(heads,),
            in_specs=[per_head(WIDE), whole(w_out.shape), per_head(listed)]
            + [pl.BlockSpec(memory_space=pl.ANY)] * len(parts),
            out_specs=[per_head(WIDE), per_head(listed)] + [whole((rows // 2, D))] * 2,
            scratch_shapes=[
                pltpu.VMEM((2, slots * rows, WIDE), bf16),
                pltpu.VMEM((heads, rows, WIDE), bf16),
                pltpu.VMEM((rows, listed), f32),
                pltpu.SemaphoreType.DMA((2, 2 * slots)),
            ],
        ),
        out_shape=[
            jax.ShapeDtypeStruct((heads, rows, WIDE), bf16),
            jax.ShapeDtypeStruct((heads, rows, listed), bf16),
        ]
        + [jax.ShapeDtypeStruct((rows // 2, D), bf16)] * 2,
        compiler_params=params(30 if len(parts) == 2 else 12),
        cost_estimate=cost(
            2 * rows * heads * WIDE * (D + 512), 2 * heads * WIDE * rows * (slots + 4)
        ),
        name="attend",
    )(place, starts, queries, w_out, mask, *parts)


def attend_back_kernel(place, starts, *refs, heads, count, blocks, parts):
    q_ref, probs_ref, w_ref = refs[:3]
    pieces = refs[3:5]
    kv_parts = refs[5 : 5 + parts]
    dq_ref, grad_ref = refs[5 + parts : 7 + parts]
    outs = refs[7 + parts : 7 + 2 * parts]
    keys, sums, mixed_ref, work, scores_ref, grads_ref, sems = refs[7 + 2 * parts :]
    rows = blocks * QB
    size = rows // 2
    head, buffer = bring_blocks(place, kv_parts, keys, sems, heads, rows)

    @pl.when(head == 0)
    def _():
        for k in range(2):
            grad_ref[half_rows(place, k, size), :] = pieces[k][...]

    sums[...] = jnp.zeros_like(sums)
    mixed_ref[...] = lax.dot_general(
        grad_ref[...], w_ref[...], ON_LANES, preferred_element_type=f32
    ).astype(bf16)
    blocks_at = [pl.ds(b * QB, QB) for b in range(blocks)]
    where = [listed_rows(place, starts, head, b, rows) for b in range(blocks)]
    for b, at in enumerate(blocks_at):
        kv = load_rows(keys, buffer, where[b])
        work[at, :] = lax.dot_general(
            mixed_ref[at, :], kv, ON_LANES, preferred_element_type=f32
        )
    weights = probs_ref[0].astype(f32)
    grad_probs = work[...]
    inner = jnp.sum(weights * grad_probs, axis=-1, keepdims=True)
    scores_ref[...] = (weights * (grad_probs - inner)).astype(bf16)
    for b, at in enumerate(blocks_at):
        kv = load_rows(keys, buffer, where[b])
        grad_q = jnp.dot(scores_ref[at, :], kv, preferred_element_type=f32)
        dq_ref[0, at, :] = (grad_q.astype(bf16).astype(f32) * scale).astype(bf16)
    for b, at in enumerate(blocks_at):
        grads_ref[b] = lax.dot_general(
            jnp.concatenate([scores_ref[at, :], probs_ref[0, at, :]], axis=0),
            jnp.concatenate([q_ref[0, at, :], mixed_ref[at, :]], axis=0),
            ON_ROWS,
            preferred_element_type=f32,
        )
    for b in range(blocks):
        done = 0
        for start, length in where[b]:
            sums[pl.ds(start, length), :] += grads_ref[b, done : done + length, :]
            done += length
    for i in range(2 * count if parts == 2 else parts):
        chunk = sums[chunk_rows(place, i // 2, i % 2, rows), :].astype(bf16)
        if parts == 2:
            outs[i % 2][i // 2, 0] = chunk
        else:
            outs[i][0] = chunk


def attend_back(place, starts, queries, probs, w_out, pieces, parts, count):
    heads, rows, _ = queries.shape
    listed = probs.shape[2]
    per_head = lambda columns: pl.BlockSpec((1, rows, columns), lambda h, *_: (h, 0, 0))
    slots = count if len(parts) == 2 else len(parts) // 2
    if len(parts) == 2:
        out_specs = [pl.BlockSpec((count, 1, rows // 2, WIDE), lambda h, *_: (0, h, 0, 0))] * 2
    else:
        out_specs = [pl.BlockSpec((1, rows // 2, WIDE), lambda h, *_: (h, 0, 0))] * len(parts)
    return pl.pallas_call(
        functools.partial(
            attend_back_kernel, heads=heads, count=count, blocks=rows // QB, parts=len(parts)
        ),
        grid_spec=pltpu.PrefetchScalarGridSpec(
            num_scalar_prefetch=2,
            grid=(heads,),
            in_specs=[
                per_head(WIDE),
                per_head(listed),
                pl.BlockSpec((WIDE, D), lambda h, *_: (h, 0)),
            ]
            + [whole((rows // 2, D))] * 2
            + [pl.BlockSpec(memory_space=pl.ANY)] * len(parts),
            out_specs=[per_head(WIDE), whole((rows, D))] + out_specs,
            scratch_shapes=[
                pltpu.VMEM((2, slots * rows, WIDE), bf16),
                pltpu.VMEM((slots * rows, WIDE), f32),
                pltpu.VMEM((rows, WIDE), bf16),
                pltpu.VMEM((rows, listed), f32),
                pltpu.VMEM((rows, listed), bf16),
                pltpu.VMEM((rows // QB, listed, WIDE), f32),
                pltpu.SemaphoreType.DMA((2, 2 * slots)),
            ],
        ),
        out_shape=[
            jax.ShapeDtypeStruct((heads, rows, WIDE), bf16),
            jax.ShapeDtypeStruct((rows, D), bf16),
        ]
        + [jax.ShapeDtypeStruct(part.shape, bf16) for part in parts],
        compiler_params=params(62 if len(parts) == 2 else 16),
        cost_estimate=cost(
            2 * rows * heads * WIDE * (D + 1536), 4 * heads * WIDE * rows * (slots + 4)
        ),
        name="attend_back",
    )(place, starts, queries, probs, w_out, *pieces, *parts)


def project_back_kernel(place, *refs, heads, terms, norm_row):
    dq_ref, w_ref, normed_ref, param = refs[:4]
    kv_refs = refs[4 : 4 + 2 * terms]
    dkv_ref, bias_ref, sums_ref = refs[4 + 2 * terms : 7 + 2 * terms]
    outs = refs[7 + 2 * terms :]
    gain, shift = row(param, GAIN + norm_row), row(param, SHIFT + norm_row)
    sums_ref[...] = jnp.zeros_like(sums_ref)
    rows = dq_ref.shape[1]
    size = rows // 2
    for h in range(heads):
        bias_ref[h : h + 1, :] = jnp.sum(dq_ref[h].astype(f32), axis=0, keepdims=True)
        over_rows = jnp.zeros((1, WIDE), f32)
        for k in range(2):
            total = kv_refs[k * terms][h].astype(f32)
            for term in kv_refs[k * terms + 1 : (k + 1) * terms]:
                total = total + term[h].astype(f32)
            low = total.astype(bf16)
            dkv_ref[h, half_rows(place, k, size), :] = low
            over_rows = over_rows + jnp.sum(low.astype(f32), axis=0, keepdims=True)
        bias_ref[heads + h : heads + h + 1, :] = over_rows
    for k in range(2):
        at = half_rows(place, k, size)
        grads = jnp.concatenate(
            [dq_ref[h, at, :] for h in range(heads)] + [dkv_ref[h, at, :] for h in range(heads)],
            axis=1,
        )
        grad_normed = jnp.dot(grads, w_ref[...], preferred_element_type=f32)
        outs[k][...] = grad_normed.astype(bf16)
        unit = (normed_ref[at, :].astype(f32) - shift) / gain
        sums_ref[0:1, :] += jnp.sum(grad_normed * unit, axis=0, keepdims=True)
        sums_ref[1:2, :] += jnp.sum(grad_normed, axis=0, keepdims=True)


def project_back(place, dq, w_all, normed, param, kv_terms, norm_row):
    heads, rows, _ = dq.shape
    half = rows // 2
    return pl.pallas_call(
        functools.partial(
            project_back_kernel, heads=heads, terms=len(kv_terms[0]), norm_row=norm_row
        ),
        grid_spec=pltpu.PrefetchScalarGridSpec(
            num_scalar_prefetch=1,
            grid=(1,),
            in_specs=[whole(array.shape) for array in (dq, w_all, normed, param)]
            + [whole((heads, half, WIDE))] * (2 * len(kv_terms[0])),
            out_specs=[whole(dq.shape), whole((2 * heads, WIDE)), whole((2, D))]
            + [whole((half, D))] * 2,
        ),
        out_shape=[
            jax.ShapeDtypeStruct(dq.shape, bf16),
            jax.ShapeDtypeStruct((2 * heads, WIDE), f32),
            jax.ShapeDtypeStruct((2, D), f32),
        ]
        + [jax.ShapeDtypeStruct((half, D), bf16)] * 2,
        compiler_params=params(12),
        cost_estimate=cost(4 * rows * D * heads * WIDE, 4 * D * heads * WIDE + 12 * rows * D),
        name="project_back",
    )(place, dq, w_all, normed, param, *kv_terms[0], *kv_terms[1])


def feed_kernel(place, *refs):
    pieces = refs[:2]
    up_ref, bias_ref, down_ref, kept_ref, slope_ref = refs[2:7]
    outs = refs[7:]
    size = pieces[0].shape[0]
    root = 0.7978845608028654
    cubic = 0.044715
    for k in range(2):
        at = pl.ds(k * size, size)
        normed = pieces[k][...]
        kept_ref[0, at, :] = normed
        inner = jnp.dot(normed, up_ref[...], preferred_element_type=f32) + bias_ref[...]
        square = inner * inner
        bend = jnp.tanh(root * inner * (1.0 + cubic * square))
        half = 0.5 * (1.0 + bend)
        hidden = (inner * half).astype(bf16)
        kept_ref[1, at, :] = hidden
        slope = half + 0.5 * inner * (1.0 - bend * bend) * (root * (1.0 + 3.0 * cubic * square))
        slope_ref[at, :] = slope.astype(bf16)
        outs[k][...] = jnp.dot(hidden, down_ref[...], preferred_element_type=f32).astype(bf16)


def feed(place, pieces, w_up, b_up, w_down):
    half = pieces[0].shape[0]
    rows = 2 * half
    units = w_up.shape[1]
    return pl.pallas_call(
        feed_kernel,
        grid_spec=pltpu.PrefetchScalarGridSpec(
            num_scalar_prefetch=1,
            grid=(1,),
            in_specs=[whole((half, D))] * 2
            + [whole(w_up.shape), whole(b_up.shape), whole(w_down.shape)],
            out_specs=[whole((2, rows, D)), whole((rows, units))] + [whole((half, D))] * 2,
        ),
        out_shape=[
            jax.ShapeDtypeStruct((2, rows, D), bf16),
            jax.ShapeDtypeStruct((rows, units), bf16),
        ]
        + [jax.ShapeDtypeStruct((half, D), bf16)] * 2,
        compiler_params=params(14),
        cost_estimate=cost(4 * rows * D * units, 4 * D * units + 10 * rows * D, rows * units),
        name="feed",
    )(place, *pieces, w_up, b_up, w_down)


def feed_back_kernel(place, *refs):
    pieces = refs[:2]
    down_ref, up_ref, slope_ref, inner_ref, bias_ref = refs[2:7]
    outs = refs[7:]
    size = pieces[0].shape[0]
    transposed = (((1,), (1,)), ((), ()))
    total = None
    for k in range(2):
        at = pl.ds(k * size, size)
        grad = pieces[k][...]
        hidden = lax.dot_general(grad, down_ref[...], transposed, preferred_element_type=f32)
        inner = (hidden * slope_ref[at, :].astype(f32)).astype(bf16)
        inner_ref[at, :] = inner
        part = jnp.sum(inner.astype(f32), axis=0, keepdims=True)
        total = part if total is None else total + part
        outs[k][...] = lax.dot_general(
            inner, up_ref[...], transposed, preferred_element_type=f32
        ).astype(bf16)
    bias_ref[...] = total


def halves_of(pieces, half):
    if len(pieces) == 2:
        return tuple(pieces), [whole((half, D))] * 2
    specs = [
        pl.BlockSpec((half, D), lambda i, place, k=k: ((place[0] & 1) ^ k, 0)) for k in range(2)
    ]
    return tuple(pieces) * 2, specs


def feed_back(place, pieces, w_up, w_down, slope):
    rows, units = slope.shape
    half = rows // 2
    arrays, specs = halves_of(pieces, half)
    return pl.pallas_call(
        feed_back_kernel,
        grid_spec=pltpu.PrefetchScalarGridSpec(
            num_scalar_prefetch=1,
            grid=(1,),
            in_specs=specs + [whole(w_down.shape), whole(w_up.shape), whole(slope.shape)],
            out_specs=[whole((rows, units)), whole((1, units))] + [whole((half, D))] * 2,
        ),
        out_shape=[
            jax.ShapeDtypeStruct((rows, units), bf16),
            jax.ShapeDtypeStruct((1, units), f32),
        ]
        + [jax.ShapeDtypeStruct((half, D), bf16)] * 2,
        compiler_params=params(14),
        cost_estimate=cost(4 * rows * D * units, 4 * D * units + 10 * rows * D),
        name="feed_back",
    )(place, *arrays, w_down, w_up, slope)


def add_norm_kernel(place, *refs, bias_row, norm_row):
    a, b, residual, param, valid = refs[:5]
    out_ref, low_ref, normed_ref, squares_ref = refs[5:]
    branch = a[...].astype(f32) + b[...].astype(f32) + row(param, bias_row)
    total = residual[...].astype(f32) + branch
    out_ref[...] = total
    low = total.astype(bf16)
    low_ref[...] = low
    if norm_row is not None:
        unit, _ = normalise(low.astype(f32))
        gain, shift = row(param, GAIN + norm_row), row(param, SHIFT + norm_row)
        normed_ref[...] = (unit * gain + shift).astype(bf16)
    else:
        normed_ref[...] = low
    weight = valid[...]
    squares_ref[0:1, :] = jnp.sum(weight * branch * branch, axis=0, keepdims=True)
    squares_ref[1:2, :] = jnp.sum(weight * total * total, axis=0, keepdims=True)


def own_half(half):
    return pl.BlockSpec((half, D), lambda i, place: (place[0] & 1, 0))


def add_norm(place, terms, residual, param, valid, rows, bias_row, norm_row):
    half = rows // 2
    spec = whole((half, D))
    return pl.pallas_call(
        functools.partial(add_norm_kernel, bias_row=bias_row, norm_row=norm_row),
        grid_spec=pltpu.PrefetchScalarGridSpec(
            num_scalar_prefetch=1,
            grid=(1,),
            in_specs=[spec] * 2
            + [
                spec,
                whole((PARAM_ROWS, D)),
                whole(valid.shape),
            ],
            out_specs=[spec, spec, spec, whole((2, D))],
        ),
        out_shape=[
            jax.ShapeDtypeStruct((half, D), f32),
            jax.ShapeDtypeStruct((half, D), bf16),
            jax.ShapeDtypeStruct((half, D), bf16),
            jax.ShapeDtypeStruct((2, D), f32),
        ],
        compiler_params=params(8),
        cost_estimate=cost(20 * half * D, 18 * half * D),
        name="add_norm",
    )(place, *terms, residual, param, valid)


def norm_back_kernel(place, *refs, norm_row):
    a, b, source, gradient, param = refs[:5]
    out_ref, low_ref, sums_ref = refs[5:]
    grad_normed = a[...].astype(f32) + b[...].astype(f32)
    unit, inverse = normalise(source[...].astype(f32))
    grad_unit = grad_normed * row(param, GAIN + norm_row)
    first = jnp.mean(grad_unit, axis=-1, keepdims=True)
    second = jnp.mean(grad_unit * unit, axis=-1, keepdims=True)
    total = gradient[...].astype(f32) + inverse * (grad_unit - first - unit * second)
    out_ref[...] = total
    low = total.astype(bf16)
    low_ref[...] = low
    sums_ref[0:1, :] = jnp.sum(grad_normed * unit, axis=0, keepdims=True)
    sums_ref[1:2, :] = jnp.sum(grad_normed, axis=0, keepdims=True)
    sums_ref[2:3, :] = jnp.sum(low.astype(f32), axis=0, keepdims=True)


def norm_back(place, terms, source, gradient, param, rows, norm_row):
    half = rows // 2
    spec = whole((half, D))
    pick = lambda array: spec if array.shape[0] == half else own_half(half)
    return pl.pallas_call(
        functools.partial(norm_back_kernel, norm_row=norm_row),
        grid_spec=pltpu.PrefetchScalarGridSpec(
            num_scalar_prefetch=1,
            grid=(1,),
            in_specs=[spec] * 2 + [pick(source), pick(gradient), whole((PARAM_ROWS, D))],
            out_specs=[spec, spec, whole((3, D))],
        ),
        out_shape=[
            jax.ShapeDtypeStruct((half, D), f32),
            jax.ShapeDtypeStruct((half, D), bf16),
            jax.ShapeDtypeStruct((3, D), f32),
        ],
        compiler_params=params(8),
        cost_estimate=cost(20 * half * D, 18 * half * D),
        name="norm_back",
    )(place, *terms, source, gradient, param)


def piece_slot(place, piece, order):
    away = piece ^ place[5]
    bit = lambda i: (away >> order[i]) & 1
    return bit(0), 2 * bit(1) + bit(2)


def put_piece(place, outs, order, part, piece, value):
    low = value.shape[0]
    at = slice(part * low, (part + 1) * low)
    sent, k = piece_slot(place, piece, order)

    @pl.when(sent == 0)
    def _():
        outs[0][k, at] = value

    @pl.when(sent == 1)
    def _():
        outs[1][k, at] = value


def take_pieces(place, refs, order, staged):
    for piece in range(8):
        sent, k = piece_slot(place, piece, order)

        @pl.when(sent == 0)
        def _():
            staged[piece] = refs[0][k]

        @pl.when(sent == 1)
        def _():
            staged[piece] = refs[1][k]


def square_grads_kernel(place, left_ref, *refs, order, terms):
    rights, outs = refs[:terms], refs[terms:]
    half = D // 2
    low = half // 2
    size = left_ref.shape[1] // terms
    for i in range(2):
        for j in range(2):
            value = sum(
                lax.dot_general(
                    left_ref[0, k * size : (k + 1) * size, i * half : (i + 1) * half],
                    right[:, j * half : (j + 1) * half],
                    ON_ROWS,
                    preferred_element_type=f32,
                )
                for k, right in enumerate(rights)
            ).astype(bf16)
            for part in range(2):
                piece = 4 * i + 2 * j + part
                put_piece(place, outs, order, 0, piece, value[part * low : (part + 1) * low])


def square_grads(place, fed, which, rights, order):
    rows = fed.shape[1]
    if which:
        arrays, specs = halves_of(rights, rows // 2)
    else:
        arrays, specs = tuple(rights), [whole(rights[0].shape)]
    left = pl.BlockSpec((1, rows, D), lambda *_: (which, 0, 0))
    return pieces_call(
        functools.partial(square_grads_kernel, order=order, terms=len(arrays)),
        "down_grads" if which else "up_grads",
        place,
        (fed, *arrays),
        (D // 4, D // 2),
        2 * rows * D * D,
        [left, *specs],
    )


def pieces_call(kernel, name, place, arrays, shape, flops, specs=None):
    return pl.pallas_call(
        kernel,
        grid_spec=pltpu.PrefetchScalarGridSpec(
            num_scalar_prefetch=1,
            grid=(1,),
            in_specs=specs or [whole(array.shape) for array in arrays],
            out_specs=[whole((4,) + shape)] * 2,
        ),
        out_shape=[jax.ShapeDtypeStruct((4,) + shape, bf16)] * 2,
        compiler_params=params(14),
        cost_estimate=cost(flops, 2 * sum(array.size for array in arrays)),
        name=name,
    )(place, *arrays)


def mix_grads_kernel(place, *refs, arrays, groups, order):
    sources, outs = refs[:arrays], refs[arrays:]
    half = D // 2
    parts = 8 // len(groups)
    for j in range(2):
        at = slice(j * half, (j + 1) * half)
        products = {}
        for g, (left, right, first) in enumerate(groups):
            if left not in products:
                heads = sources[left].shape[0]
                products[left] = [
                    lax.dot_general(
                        sources[left][h],
                        sources[right][:, at],
                        ON_ROWS,
                        preferred_element_type=f32,
                    ).astype(bf16)
                    for h in range(heads)
                ]
            value = jnp.concatenate(
                [product[first : first + HD] for product in products[left]], axis=0
            )
            low = value.shape[0] // parts
            for part in range(parts):
                piece = parts * g + part
                put_piece(place, outs, order, j, piece, value[part * low : (part + 1) * low])


def mix_grads(place, arrays, groups, order):
    heads, rows, _ = arrays[0].shape
    return pieces_call(
        functools.partial(mix_grads_kernel, arrays=len(arrays), groups=groups, order=order),
        "mix_grads",
        place,
        arrays,
        (heads * HD * len(groups) // 4, D // 2),
        2 * len(groups) * rows * D * heads * WIDE,
    )


def square_place_kernel(place, *refs, order):
    out, staged = refs[-2:]
    half = D // 2
    low = half // 2
    take_pieces(place, refs[:2], order, staged)
    for piece in range(8):
        i, j, part = piece // 4, (piece // 2) % 2, piece % 2
        top = i * half + part * low
        out[0, top : top + low, j * half : (j + 1) * half] = staged[piece].astype(f32)


def mix_place_kernel(place, *refs, bundles):
    first_staged = len(refs) - len(bundles)
    qkv_ref, out_ref = refs[first_staged - 2 : first_staged]
    half = D // 2
    for i, (order, groups) in enumerate(bundles):
        staged = refs[first_staged + i]
        take_pieces(place, refs[2 * i : 2 * i + 2], order, staged)
        parts = 8 // len(groups)
        low = staged.shape[1] // 2
        for j in range(2):
            columns_at = slice(j * half, (j + 1) * half)
            for piece in range(8):
                g, part = groups[piece // parts], piece % parts
                rows = slice(part * low, (part + 1) * low)
                value = staged[piece, j * low : (j + 1) * low].astype(f32)
                if g < 3:
                    qkv_ref[0, g, rows, columns_at] = value
                else:
                    out_ref[0, rows, columns_at] = value


def place_call(kernel, name, place, bundles, earlier, shapes, layer):
    arrays = [array for bundle in bundles for array in bundle]
    specs = [
        pl.BlockSpec((1,) + shape, lambda *_, rank=len(shape): (layer,) + (0,) * rank)
        for shape in shapes
    ]
    kept = [pl.BlockSpec(memory_space=pl.ANY)] * len(earlier)
    size = sum(array.size for array in arrays)
    return pl.pallas_call(
        kernel,
        grid_spec=pltpu.PrefetchScalarGridSpec(
            num_scalar_prefetch=1,
            grid=(1,),
            in_specs=[whole(array.shape) for array in arrays] + kept,
            out_specs=specs,
            scratch_shapes=[pltpu.VMEM((8,) + bundle[0].shape[1:], bf16) for bundle in bundles],
        ),
        out_shape=[jax.ShapeDtypeStruct((LAYERS,) + shape, f32) for shape in shapes],
        input_output_aliases={1 + len(arrays) + i: i for i in range(len(earlier))},
        compiler_params=params(18),
        cost_estimate=cost(size, 6 * size),
        name=name,
    )(place, *arrays, *earlier)


def columns_kernel(place, *refs):
    pieces, out = refs[:2], refs[2]
    size = pieces[0].shape[0]
    width = out.shape[0]
    for p in range(4):

        @pl.when(place[0] == p)
        def _():
            for k in range(2):
                part = pieces[k][:, p * width : (p + 1) * width].astype(f32)
                q = (p & 1) ^ k
                out[:, q * size : (q + 1) * size] = jnp.transpose(part).astype(bf16)


def columns(place, pieces):
    half = pieces[0].shape[0]
    return pl.pallas_call(
        columns_kernel,
        grid_spec=pltpu.PrefetchScalarGridSpec(
            num_scalar_prefetch=1,
            grid=(1,),
            in_specs=[whole((half, D))] * 2,
            out_specs=whole((D // 4, 2 * half)),
        ),
        out_shape=jax.ShapeDtypeStruct((D // 4, 2 * half), bf16),
        compiler_params=params(8),
        cost_estimate=cost(half * D, 8 * half * D),
        name="columns",
    )(place, *pieces)


def on_device(
    residual_in,
    cotangent,
    w_qkv,
    b_qv,
    w_out,
    b_out,
    w_up,
    b_up,
    w_down,
    b_down,
    ln_gain,
    ln_bias,
    selection,
    lengths,
    valid,
):
    rows = residual_in.shape[0]
    heads = selection.shape[0]
    blocks = rows // QB
    half = rows // 2
    count = lax.axis_size("tok")
    position = lax.axis_index("tok")
    member = lax.axis_index("head")
    width = D // 4
    first_row = position * rows
    chosen = lax.dynamic_slice_in_dim(selection, position * blocks, blocks, 1).reshape(heads, -1)
    per_device = rows // KB
    starts = slot_of(chosen // per_device, position, count) * rows + (chosen % per_device) * KB
    place = jnp.stack(
        [
            member,
            position,
            lengths[0],
            slot_of(position, position, count) * rows,
            slot_of(jnp.maximum(position - 1, 0), position, count) * rows,
            position if ring_form(count) else 0,
        ]
    ).astype(jnp.int32)

    first_pieces = share_features(residual_in.T)
    small = jnp.concatenate(
        [ln_gain.reshape(-1, width), ln_bias.reshape(-1, width), b_out, b_down], axis=0
    )
    small = jnp.pad(small, ((0, 128 - small.shape[0]), (0, 0)))
    param_pieces = share_features(small.T)

    split = jnp.transpose(w_qkv, (0, 2, 3, 1)).reshape(LAYERS, 3, heads, HD, D)
    w_all = jnp.concatenate(
        [
            jnp.pad(split[:, 0], ((0, 0), (0, 0), (0, WIDE - HD), (0, 0))),
            jnp.concatenate([split[:, 1], split[:, 2]], axis=2),
        ],
        axis=1,
    ).reshape(LAYERS, 2 * heads * WIDE, D)
    b_split = b_qv.reshape(LAYERS, 2, heads, HD)
    b_all = (
        jnp.concatenate(
            [
                jnp.pad(b_split[:, 0], ((0, 0), (0, 0), (0, HD))),
                jnp.pad(b_split[:, 1], ((0, 0), (0, 0), (HD, 0))),
            ],
            axis=1,
        )
        .reshape(LAYERS, 1, 2 * heads * WIDE)
        .astype(f32)
    )
    w_mix = jnp.pad(
        w_out.reshape(LAYERS, heads, HD, D), ((0, 0), (0, 0), (HD, 0), (0, 0))
    ).reshape(LAYERS, heads * WIDE, D)
    b_inner = b_up.astype(f32)

    far_valid = jnp.tile(valid.reshape(-1, KB), (1, SEL)).astype(f32)
    padded = jnp.concatenate([jnp.zeros((WINDOW,), jnp.int32), valid])
    near = lax.dynamic_slice_in_dim(padded, first_row, rows + WINDOW).reshape(-1, WINDOW)
    near_valid = jnp.concatenate([near[:-1], near[1:]], axis=1).astype(f32)
    own_valid = lax.dynamic_slice_in_dim(valid, first_row + (member & 1) * half, half)
    own_valid = own_valid.astype(f32)[:, None]
    mask = masks(place, chosen, near_valid, far_valid, heads, rows)

    pieces = first_pieces
    lows = []
    kept = []
    squares = []
    for l in range(LAYERS):
        normed, queries, *own_kv = project(
            place, pieces, None if l else param_pieces, w_all[l], b_all[l], rows, heads
        )
        if l == 0:
            own_kv, (low_first, param) = own_kv[:2], own_kv[2:]
            residual = low_first
        parts = gather_blocks(own_kv)
        mixed, probs, *pieces = attend(place, starts, queries, w_mix[l], mask, parts, count)
        residual, low_second, normed_own, branch_squares = add_norm(
            place, sum_rows(pieces), residual, param, own_valid, rows, B_OUT + l, 2 * l + 1
        )
        fed, slope, *pieces = feed(
            place, share_rows(normed_own), w_up[l], b_inner[l : l + 1], w_down[l]
        )
        residual, low_next, normed_own, second_squares = add_norm(
            place,
            sum_rows(pieces),
            residual,
            param,
            own_valid,
            rows,
            B_DOWN + l,
            2 * l + 2 if l + 1 < LAYERS else None,
        )
        squares.append((second_squares[1], branch_squares[0], second_squares[0]))
        kept.append((normed, queries, parts, mixed, probs, low_second, fed, slope))
        lows.append(low_next)
        if l + 1 < LAYERS:
            pieces = share_rows(normed_own)
    residual_out = columns(place, share_rows(lows[-1])).T

    gradient, sums_down = turn(place, share_features(cotangent.T))
    sums_down = sums_down[0]
    grad_pieces = (gradient,)
    grads = [None] * LAYERS
    placed_up = placed_down = placed_mix = ()
    shapes_mix = ((3, heads * HD, D), (heads * HD, D))
    for l in reversed(range(LAYERS)):
        last = l == 0
        normed, queries, parts, mixed, probs, low_second, fed, slope = kept[l]
        down = Bundle(square_grads(place, fed, 1, grad_pieces, COLUMN_FIRST), COLUMN_FIRST)
        down.send()
        inner, grad_b_up, *pieces = feed_back(place, grad_pieces, w_up[l], w_down[l], slope)
        up = Bundle(square_grads(place, fed, 0, (inner,), COLUMN_FIRST), COLUMN_FIRST)
        up.send()
        terms, _, _ = lax.optimization_barrier((sum_rows(pieces), up.out, down.out))
        terms = down.take(terms)
        if last:
            terms = mix_before.take(up_before.take(down_before.take(terms)))
            down_before.send()
            up_before.send()
        gradient, low, second_sums = norm_back(
            place, terms, low_second, gradient, param, rows, 2 * l + 1
        )
        pieces = share_rows(low)
        dq, branch_full, *kv_grads = attend_back(
            place, starts, queries, probs, w_mix[l], pieces, parts, count
        )
        kv_grads = up.take(kv_grads)
        if last:
            kv_grads = up_before.take(down_before.take(kv_grads))
        kv_terms = return_blocks(kv_grads, lambda other: other)
        if last:
            kv_terms, residual_out = lax.optimization_barrier((kv_terms, residual_out))
        dkv, bias_sums, first_sums, *pieces = project_back(
            place, dq, w_all[l], normed, param, kv_terms, 2 * l
        )
        if not last:
            down.send(dkv)
            up.send(dkv)
        groups = ((0, 3, 0), (1, 3, 0), (1, 3, HD), (2, 4, HD))
        mix_pieces = mix_grads(
            place, (dq, dkv, mixed, normed, branch_full), groups, COLUMN_FIRST
        )
        mix = Bundle(mix_pieces, COLUMN_FIRST)
        if last:
            finish_in_turn(dkv, down_before, up_before, mix_before, down, up, mix)
        else:
            mix.send()
        terms, _ = lax.optimization_barrier((sum_rows(pieces), mix_pieces))
        if not last:
            terms = up.take(down.take(terms))
            down.send()
            up.send()
            down_before, up_before, mix_before = down, up, mix
        gradient, low, low_sums = norm_back(
            place, terms, lows[l - 1] if l else low_first, gradient, param, rows, 2 * l
        )
        pieces = share_rows(low)
        if not last:
            pieces = mix.take(pieces)
            mix.send()
        grad_pieces = pieces
        grads[l] = (
            None,
            grad_b_up[0],
            jnp.concatenate(
                [
                    bias_sums[:heads, :HD].reshape(-1),
                    bias_sums[heads:, HD:].reshape(-1),
                    jnp.zeros((D - 2 * heads * HD,), f32),
                ]
            ),
            None,
            None,
            second_sums[2],
            sums_down,
            first_sums,
            second_sums,
        )
        sums_down = low_sums[2]
    grad_residual = columns(place, pieces).T
    for l, bundles in ((1, (down_before, up_before, mix_before)), (0, (down, up, mix))):
        placed_down, placed_up = [
            place_call(
                functools.partial(square_place_kernel, order=COLUMN_FIRST),
                name,
                place,
                [bundle.finish()],
                placed,
                ((D, D),),
                l,
            )
            for name, bundle, placed in (
                ("down_place", bundles[0], placed_down),
                ("up_place", bundles[1], placed_up),
            )
        ]
        done = bundles[2].finish()
        if l == 0:
            done, placed_down, placed_up, placed_mix = lax.optimization_barrier(
                (done, placed_down, placed_up, placed_mix)
            )
        placed_mix = place_call(
            functools.partial(mix_place_kernel, bundles=((COLUMN_FIRST, (0, 1, 2, 3)),)),
            "mix_place",
            place,
            [done],
            placed_mix,
            shapes_mix,
            l,
        )

    first = jnp.concatenate([grads[l][7] for l in range(LAYERS)], axis=0)
    first = first + swap(first, "head", 2)
    over_all = jnp.concatenate(
        [first]
        + [grads[l][8][:2] for l in range(LAYERS)]
        + [jnp.stack([grads[l][5] for l in range(LAYERS)])]
        + [jnp.stack([grads[l][6] for l in range(LAYERS)])]
        + [jnp.stack([vector for layer in squares for vector in layer])],
        axis=0,
    )
    over_tok = jnp.stack(
        [grads[l][1] for l in range(LAYERS)] + [grads[l][2] for l in range(LAYERS)]
    )
    packed = small_sum(
        jnp.concatenate([over_all + swap(over_all, "head", 1), over_tok], axis=0), "tok"
    )
    stat_row = 4 * LAYERS + 2 * LAYERS
    tok_row = stat_row + 3 * LAYERS
    mine = lax.dynamic_slice_in_dim(packed[:stat_row], member * width, width, 1)
    norms = mine[: 4 * LAYERS].reshape(2, LAYERS, 2, width)
    grad_ln_gain = jnp.stack([norms[0, :, 0], norms[1, :, 0]], axis=1)
    grad_ln_bias = jnp.stack([norms[0, :, 1], norms[1, :, 1]], axis=1)
    grad_b_out = mine[4 * LAYERS : 5 * LAYERS]
    grad_b_down = mine[5 * LAYERS : 6 * LAYERS]
    square_sums = jnp.sum(packed[stat_row:tok_row], axis=-1).reshape(LAYERS, 3)
    valid_count = jnp.maximum(jnp.sum(valid.astype(f32)), 1.0)
    statistics = jnp.sqrt(square_sums / (valid_count * D))
    grad_b_up = packed[tok_row : tok_row + LAYERS]
    grad_b_qv = packed[tok_row + LAYERS :, : 2 * heads * HD].reshape(LAYERS, 2, heads * HD)
    return (
        residual_out,
        grad_residual,
        jnp.transpose(placed_mix[0], (0, 3, 1, 2)),
        grad_b_qv,
        placed_mix[1],
        grad_b_out,
        placed_up[0],
        grad_b_up,
        placed_down[0],
        grad_b_down,
        grad_ln_gain,
        grad_ln_bias,
        statistics,
    )


def solution(mesh):
    in_specs = (
        P("tok", "head"),
        P("tok", "head"),
        P(None, None, None, "head"),
        P(None, None, "head"),
        P(None, "head", None),
        P(None, "head"),
        P(None, None, "head"),
        P(None, "head"),
        P(None, "head", None),
        P(None, "head"),
        P(None, None, "head"),
        P(None, None, "head"),
        P("head", None, None),
        P(),
        P(),
    )
    out_specs = (
        P("tok", "head"),
        P("tok", "head"),
        P(None, None, None, "head"),
        P(None, None, "head"),
        P(None, "head", None),
        P(None, "head"),
        P(None, None, "head"),
        P(None, "head"),
        P(None, "head", None),
        P(None, "head"),
        P(None, None, "head"),
        P(None, None, "head"),
        P(),
    )
    return jax.shard_map(
        on_device, mesh=mesh, in_specs=in_specs, out_specs=out_specs, check_vma=False
    )
```

```python
import functools

import jax
import jax.numpy as jnp
from jax import lax
from jax.experimental import pallas as pl
from jax.experimental.pallas import tpu as pltpu
from jax.sharding import PartitionSpec as P

D = 768
HD = 64
LAYERS = 2
WINDOW = 64
KB = 16
SEL = 4
QB = 64
WIDE = 2 * HD

epsilon = 1e-05
negative = -1e30
scale = HD ** (-0.5)
bf16 = jnp.bfloat16
f32 = jnp.float32

STEPS = (0, 2, 1, 3)
GAIN, SHIFT, B_OUT, B_DOWN, PARAM_ROWS = 0, 4, 8, 10, 16


def params(megabytes):
    return pltpu.CompilerParams(vmem_limit_bytes=megabytes * 2**20)


def cost(flops, moved, special=0):
    return pl.CostEstimate(flops=int(flops), bytes_accessed=int(moved), transcendentals=int(special))


def swap(value, axis, step):
    return lax.ppermute(value, axis, [(i, i ^ step) for i in range(lax.axis_size(axis))])


def rotate(value, axis, step):
    count = lax.axis_size(axis)
    return lax.ppermute(value, axis, [(i, (i + step) % count) for i in range(count)])


def share_features(own):
    across = swap(own, "head", 2)
    beside = swap(own, "head", 1)
    both = swap(across, "head", 1)
    return own, across, beside, both


def share_rows(own):
    return own, swap(own, "head", 1)


def sum_rows(pieces):
    own, other = pieces
    chip = (own.astype(f32) + swap(other, "head", 1).astype(f32)).astype(bf16)
    return chip, swap(chip, "head", 2)


def small_sum(value, axis):
    step = 1
    while step < lax.axis_size(axis):
        value = value + swap(value, axis, step)
        step *= 2
    return value


def finish_in_turn(other, *bundles):
    if not bundles[0].ring:
        return
    turns = {True: [], False: []}
    started = []
    for index in TURNS:
        bundle = bundles[index]
        if bundle.step == 6:
            continue
        stage = bundle.step if bundle.step < 3 else 5 - bundle.step
        queue = turns[bundle.order[stage] == 0]
        depth = COLUMN_DEPTH if bundle.order[stage] == 0 else Z_DEPTH
        wait = [other]
        if len(queue) >= depth:
            wait.append(queue[-depth])
        if len(started) >= LAG:
            wait.append(started[-LAG])
        bundle.send(wait)
        queue.append(bundle.coming)
        started.append(bundle.coming)


def ring_form(count):
    return count == 8


COLUMN_FIRST = (0, 1, 2)

TURNS = (0, 1, 2, 3, 0, 1, 2, 3, 1, 2, 1, 3, 2, 3, 2, 3, 3)
COLUMN_DEPTH, Z_DEPTH = 3,4
LAG = 4


def after(value, other):
    return lax.optimization_barrier((value, other))[0]


class Bundle:
    def __init__(self, pieces, order):
        self.ring = ring_form(lax.axis_size("tok"))
        self.step, self.order = 0, order
        self.parts = [tuple(pieces)]
        self.coming = ()

    def add(self, pieces):
        self.parts.append(tuple(pieces))
        if self.ring:
            self.coming += (swap(pieces[1], "tok", 1 << self.order[0]),)

    def send(self, other=None):
        if not self.ring or self.step == 6:
            return
        if self.step == 0:
            out = self.parts[0][1]
            self.kept = tuple(kept for kept, _ in self.parts)
        else:
            if self.step == 1:
                self.kept = tuple(kept for kept, _ in self.parts)
            kept, came = self.kept, self.coming
            if other is not None:
                kept, came = after((kept, came), other)
            if self.step < 3:
                kept, out = merge("split", kept, came)
            else:
                (kept,) = merge("add" if self.step == 3 else "join", kept, came)
                out = kept
            self.kept = (kept,)
        if other is not None:
            out = after(out, other)
        stage = self.step if self.step < 3 else 5 - self.step
        self.coming = (swap(out, "tok", 1 << self.order[stage]),)
        self.step += 1

    def take(self, other):
        if not self.ring:
            return other
        self.coming, other = lax.optimization_barrier((self.coming, other))
        return other

    def finish(self):
        while self.ring and self.step < 6:
            self.send()
        if self.ring:
            return self.kept + self.coming
        summed = lax.psum(self.parts, "tok")
        return tuple(
            jnp.concatenate([part[i] for part in summed], axis=1) for i in range(2)
        )


def gather_blocks(chunks):
    count = lax.axis_size("tok")
    if not ring_form(count):
        return [lax.all_gather(chunk, "tok") for chunk in chunks]
    parts = [None] * (2 * count)
    for k, current in enumerate(chunks):
        for hop in range(count // 2):
            other = swap(current, "tok", 1)
            after = None
            if hop < count // 2 - 1:
                after = rotate(current, "tok", 2)
                current, other, after = lax.optimization_barrier((current, other, after))
            parts[4 * hop + k] = current
            parts[4 * hop + 2 + k] = other
            current = after
    return parts


def return_blocks(parts, meanwhile):
    count = lax.axis_size("tok")
    if not ring_form(count):
        return [
            [lax.psum_scatter(part, "tok", scatter_dimension=0, tiled=False)] for part in parts
        ]
    running = [None, None]
    own = [None, None]
    got = [None, None]
    for d in range(count // 2 - 1, -1, -1):
        for k in range(2):
            mine, other = parts[4 * d + k], parts[4 * d + 2 + k]
            if got[k] is not None:
                other, got[k] = lax.optimization_barrier((other, got[k]))
                total = own[k].astype(f32) + got[k].astype(f32)
                if running[k] is not None:
                    total = total + running[k].astype(f32)
                running[k] = rotate(total.astype(bf16), "tok", -2)
            own[k], got[k] = mine, swap(other, "tok", 1)
        if d == 1:
            running = meanwhile(running)
    return [[own[k], got[k], running[k]] for k in range(2)]


def slot_of(block, tok, count):
    if not ring_form(count):
        return block
    away = (tok >> 1) - (block >> 1)
    return 2 * jnp.maximum(away, 0) + ((tok ^ block) & 1)


ON_LANES = (((1,), (1,)), ((), ()))
ON_ROWS = (((0,), (0,)), ((), ()))


def normalise(rows):
    average = jnp.mean(rows, axis=-1, keepdims=True)
    centred = rows - average
    spread = jnp.mean(centred * centred, axis=-1, keepdims=True)
    inverse = lax.rsqrt(spread + epsilon)
    return centred * inverse, inverse


def row(ref, index):
    return ref[index : index + 1, :].astype(f32)


def piece_rows(place, step, size):
    return pl.ds(pl.multiple_of((place[0] ^ step) * size, size), size)


def half_rows(place, k, size):
    return pl.ds(pl.multiple_of(((place[0] & 1) ^ k) * size, size), size)


def project_kernel(place, *refs, heads, first):
    if first:
        pieces, param_pieces = refs[:4], refs[4:8]
        w_ref, bias_ref, normed_ref, q_ref = refs[8:12]
        kv_refs = refs[12:14]
        low_ref, param_ref, staged, turned = refs[14:]
        width = staged.shape[0] // 4
        for k in range(4):
            staged[piece_rows(place, STEPS[k], width), :] = pieces[k][...]
            turned[piece_rows(place, STEPS[k], width), :] = param_pieces[k][...].astype(f32)
        param_ref[...] = jnp.transpose(turned[...])[:PARAM_ROWS]
    else:
        pieces = refs[:2]
        w_ref, bias_ref, normed_ref, q_ref = refs[2:6]
        kv_refs = refs[6:]
    size = normed_ref.shape[0] // 2
    for k in range(2):
        rows = half_rows(place, k, size)
        if first:
            part = jnp.transpose(staged[:, rows].astype(f32))
            if k == 0:
                low_ref[...] = part.astype(bf16)
            unit, _ = normalise(part)
            normed = (unit * row(param_ref, GAIN) + row(param_ref, SHIFT)).astype(bf16)
        else:
            normed = pieces[k][...]
        normed_ref[rows, :] = normed
        projected = lax.dot_general(normed, w_ref[...], ON_LANES, preferred_element_type=f32)
        projected = projected + bias_ref[...]
        for h in range(heads):
            q_ref[h, rows, :] = (projected[:, h * WIDE : (h + 1) * WIDE] * scale).astype(bf16)
            at = (heads + h) * WIDE
            kv_refs[k][h] = projected[:, at : at + WIDE].astype(bf16)


def whole(shape):
    return pl.BlockSpec(shape, lambda *_: (0,) * len(shape))


def project(place, pieces, param_pieces, w_all, bias_all, rows, heads):
    first = param_pieces is not None
    arrays = tuple(pieces) + (tuple(param_pieces) if first else ())
    columns = w_all.shape[0]
    out_shapes = [
        jax.ShapeDtypeStruct((rows, D), bf16),
        jax.ShapeDtypeStruct((heads, rows, WIDE), bf16),
        jax.ShapeDtypeStruct((heads, rows // 2, WIDE), bf16),
        jax.ShapeDtypeStruct((heads, rows // 2, WIDE), bf16),
    ]
    scratch = []
    if first:
        out_shapes += [
            jax.ShapeDtypeStruct((rows // 2, D), bf16),
            jax.ShapeDtypeStruct((PARAM_ROWS, D), f32),
        ]
        scratch = [pltpu.VMEM((D, rows), bf16), pltpu.VMEM((D, 128), f32)]
    return pl.pallas_call(
        functools.partial(project_kernel, heads=heads, first=first),
        grid_spec=pltpu.PrefetchScalarGridSpec(
            num_scalar_prefetch=1,
            grid=(1,),
            in_specs=[whole(array.shape) for array in arrays + (w_all, bias_all)],
            out_specs=[whole(shape.shape) for shape in out_shapes],
            scratch_shapes=scratch,
        ),
        out_shape=out_shapes,
        compiler_params=params(12),
        cost_estimate=cost(2 * rows * D * columns, 2 * D * columns + 8 * rows * D),
        name="project",
    )(place, *arrays, w_all, bias_all)


def turn_kernel(place, *refs):
    pieces = refs[:4]
    out_ref, sums_ref, staged = refs[4:]
    width = staged.shape[0] // 4
    size = out_ref.shape[0] // 2
    for k in range(4):
        staged[piece_rows(place, STEPS[k], width), :] = pieces[k][...]
    for k in range(2):
        part = jnp.transpose(staged[:, k * size : (k + 1) * size].astype(f32))
        out_ref[k * size : (k + 1) * size, :] = part.astype(bf16)

        @pl.when((place[0] & 1) == k)
        def _():
            sums_ref[...] = jnp.sum(part, axis=0, keepdims=True)


def turn(place, pieces):
    width, rows = pieces[0].shape
    return pl.pallas_call(
        turn_kernel,
        grid_spec=pltpu.PrefetchScalarGridSpec(
            num_scalar_prefetch=1,
            grid=(1,),
            in_specs=[whole((width, rows))] * 4,
            out_specs=[whole((rows, D)), whole((1, D))],
            scratch_shapes=[pltpu.VMEM((D, rows), bf16)],
        ),
        out_shape=[jax.ShapeDtypeStruct((rows, D), bf16), jax.ShapeDtypeStruct((1, D), f32)],
        compiler_params=params(6),
        cost_estimate=cost(rows * D, 4 * rows * D),
        name="turn",
    )(place, *pieces)


def merge_kernel(*refs, act, parts):
    count = refs[0].shape[0]
    outs = refs[2 * parts :]
    each = count // len(outs)
    for part in range(parts):
        kept, came = refs[part], refs[parts + part]
        size = kept.shape[1]
        rows = slice(part * size, (part + 1) * size)
        if act == "join":
            outs[0][:count, rows] = kept[...]
            outs[0][count:, rows] = came[...]
            continue
        for i, out in enumerate(outs):
            at = slice(i * each, (i + 1) * each)
            out[:, rows] = (kept[at].astype(f32) + came[at].astype(f32)).astype(bf16)


def merge(act, kept, came):
    count, _, width = kept[0].shape
    size = sum(array.shape[1] for array in kept)
    counts = {"add": [count], "split": [count // 2] * 2, "join": [2 * count]}[act]
    shapes = [(n, size, width) for n in counts]
    total = count * size * width
    return pl.pallas_call(
        functools.partial(merge_kernel, act=act, parts=len(kept)),
        grid=(1,),
        in_specs=[whole(array.shape) for array in (*kept, *came)],
        out_specs=[whole(shape) for shape in shapes],
        out_shape=[jax.ShapeDtypeStruct(shape, bf16) for shape in shapes],
        compiler_params=params(12),
        cost_estimate=cost(total, 8 * total),
        name="merge",
    )(*kept, *came)


def chunk_rows(place, slot, k, rows):
    return pl.ds(pl.multiple_of(slot * rows + ((place[0] & 1) ^ k) * (rows // 2), rows // 2), rows // 2)


def copies(place, parts, scratch, sems, head, buffer, rows):
    if len(parts) == 2:
        sources = [parts[k].at[slot, head] for slot in range(parts[0].shape[0]) for k in range(2)]
    else:
        sources = [part.at[head] for part in parts]
    return [
        pltpu.make_async_copy(
            source,
            scratch.at[buffer, chunk_rows(place, i // 2, i % 2, rows), :],
            sems.at[buffer, i],
        )
        for i, source in enumerate(sources)
    ]


def bring_blocks(place, parts, scratch, sems, heads, rows):
    head = pl.program_id(0)
    buffer = lax.rem(head, 2)

    @pl.when(head == 0)
    def _():
        for copy in copies(place, parts, scratch, sems, 0, 0, rows):
            copy.start()

    @pl.when(head + 1 < heads)
    def _():
        for copy in copies(place, parts, scratch, sems, head + 1, 1 - buffer, rows):
            copy.start()

    for copy in copies(place, parts, scratch, sems, head, buffer, rows):
        copy.wait()
    return head, buffer


def listed_rows(place, starts, head, b, rows):
    own, before = place[3], place[4]
    if b == 0:
        near = [
            (pl.multiple_of(before + rows - WINDOW, WINDOW), WINDOW),
            (pl.multiple_of(own, WINDOW), WINDOW),
        ]
    else:
        near = [(pl.multiple_of(own + (b - 1) * QB, WINDOW), 2 * WINDOW)]
    far = [(pl.multiple_of(starts[head, b * SEL + s], KB), KB) for s in range(SEL)]
    return near + far


def load_rows(keys, buffer, where):
    return jnp.concatenate([keys[buffer, pl.ds(start, size), :] for start, size in where], axis=0)


def mask_kernel(place, chosen, near_ref, far_ref, out_ref, *, heads, blocks):
    rows = blocks * QB
    tok, boundary = place[1], place[2]
    wide = 2 * WINDOW
    line = lax.broadcasted_iota(jnp.int32, (QB, wide), 1)
    column = lax.broadcasted_iota(jnp.int32, (QB, wide), 0)
    band = (line > column) & (line <= column + WINDOW)
    diagonal = line == column + WINDOW
    in_second = lambda position: jnp.where(position >= boundary, 1, 0)
    lane = lax.broadcasted_iota(jnp.int32, (1, SEL * KB), 1)
    for b in range(blocks):
        first = tok * rows + b * QB
        query_seq = in_second(first + lax.broadcasted_iota(jnp.int32, (QB, 1), 0))
        key = first - WINDOW + lax.broadcasted_iota(jnp.int32, (1, wide), 1)
        near = band & (diagonal | (near_ref[b : b + 1, :] > 0.0))
        near = jnp.where(near & (in_second(key) == query_seq), 0.0, negative)
        for head in range(heads):
            usable = jnp.zeros((1, SEL * KB), f32)
            token = lane & (KB - 1)
            for s in range(SEL):
                block = chosen[head, b * SEL + s]
                here = (lane >= s * KB) & (lane < (s + 1) * KB)
                early = block * KB + KB <= first - WINDOW
                usable = jnp.where(here & early, far_ref[pl.ds(block, 1), :], usable)
                token = token + jnp.where(here, block * KB, 0)
            far = (usable > 0.0) & (in_second(token) == query_seq)
            at = pl.ds(b * QB, QB)
            out_ref[head, at, :wide] = near
            out_ref[head, at, wide:] = jnp.where(far, 0.0, negative)


def masks(place, chosen, near_valid, far_valid, heads, rows):
    listed = 2 * WINDOW + SEL * KB
    return pl.pallas_call(
        functools.partial(mask_kernel, heads=heads, blocks=rows // QB),
        grid_spec=pltpu.PrefetchScalarGridSpec(
            num_scalar_prefetch=2,
            grid=(1,),
            in_specs=[whole(near_valid.shape), whole(far_valid.shape)],
            out_specs=whole((heads, rows, listed)),
        ),
        out_shape=jax.ShapeDtypeStruct((heads, rows, listed), f32),
        compiler_params=params(6),
        cost_estimate=cost(20 * heads * rows * listed, 4 * heads * rows * listed),
        name="masks",
    )(place, chosen, near_valid, far_valid)


def attend_kernel(place, starts, *refs, heads, blocks, parts):
    q_ref, w_ref, mask_ref = refs[:3]
    kv_parts = refs[3 : 3 + parts]
    mixed_ref, probs_ref = refs[3 + parts : 5 + parts]
    outs = refs[5 + parts : 7 + parts]
    keys, gathered, work, sems = refs[7 + parts :]
    rows = blocks * QB
    head, buffer = bring_blocks(place, kv_parts, keys, sems, heads, rows)
    blocks_at = [pl.ds(b * QB, QB) for b in range(blocks)]
    where = [listed_rows(place, starts, head, b, rows) for b in range(blocks)]
    for b, at in enumerate(blocks_at):
        kv = load_rows(keys, buffer, where[b])
        scores = lax.dot_general(q_ref[0, at, :], kv, ON_LANES, preferred_element_type=f32)
        work[at, :] = scores + mask_ref[0, at, :]
    scores = work[...]
    weights = jnp.exp(scores - jnp.max(scores, axis=-1, keepdims=True))
    weights = weights * (1.0 / jnp.sum(weights, axis=-1, keepdims=True))
    probs_ref[0] = weights.astype(bf16)
    for b, at in enumerate(blocks_at):
        kv = load_rows(keys, buffer, where[b])
        out = jnp.dot(probs_ref[0, at, :], kv, preferred_element_type=f32).astype(bf16)
        mixed_ref[0, at, :] = out
        gathered[head, at, :] = out

    @pl.when(head == heads - 1)
    def _():
        size = rows // 2
        for k in range(2):
            at = half_rows(place, k, size)
            mixed = jnp.concatenate([gathered[h, at, :] for h in range(heads)], axis=1)
            outs[k][...] = jnp.dot(mixed, w_ref[...], preferred_element_type=f32).astype(bf16)


def attend(place, starts, queries, w_out, mask, parts, count):
    heads, rows, _ = queries.shape
    listed = mask.shape[2]
    per_head = lambda columns: pl.BlockSpec((1, rows, columns), lambda h, *_: (h, 0, 0))
    slots = count if len(parts) == 2 else len(parts) // 2
    return pl.pallas_call(
        functools.partial(attend_kernel, heads=heads, blocks=rows // QB, parts=len(parts)),
        grid_spec=pltpu.PrefetchScalarGridSpec(
            num_scalar_prefetch=2,
            grid=(heads,),
            in_specs=[per_head(WIDE), whole(w_out.shape), per_head(listed)]
            + [pl.BlockSpec(memory_space=pl.ANY)] * len(parts),
            out_specs=[per_head(WIDE), per_head(listed)] + [whole((rows // 2, D))] * 2,
            scratch_shapes=[
                pltpu.VMEM((2, slots * rows, WIDE), bf16),
                pltpu.VMEM((heads, rows, WIDE), bf16),
                pltpu.VMEM((rows, listed), f32),
                pltpu.SemaphoreType.DMA((2, 2 * slots)),
            ],
        ),
        out_shape=[
            jax.ShapeDtypeStruct((heads, rows, WIDE), bf16),
            jax.ShapeDtypeStruct((heads, rows, listed), bf16),
        ]
        + [jax.ShapeDtypeStruct((rows // 2, D), bf16)] * 2,
        compiler_params=params(30 if len(parts) == 2 else 12),
        cost_estimate=cost(
            2 * rows * heads * WIDE * (D + 512), 2 * heads * WIDE * rows * (slots + 4)
        ),
        name="attend",
    )(place, starts, queries, w_out, mask, *parts)


def attend_back_kernel(place, starts, *refs, heads, count, blocks, parts):
    q_ref, probs_ref, w_ref = refs[:3]
    pieces = refs[3:5]
    kv_parts = refs[5 : 5 + parts]
    dq_ref, grad_ref = refs[5 + parts : 7 + parts]
    outs = refs[7 + parts : 7 + 2 * parts]
    keys, sums, mixed_ref, work, scores_ref, grads_ref, sems = refs[7 + 2 * parts :]
    rows = blocks * QB
    size = rows // 2
    head, buffer = bring_blocks(place, kv_parts, keys, sems, heads, rows)

    @pl.when(head == 0)
    def _():
        for k in range(2):
            grad_ref[half_rows(place, k, size), :] = pieces[k][...]

    sums[...] = jnp.zeros_like(sums)
    mixed_ref[...] = lax.dot_general(
        grad_ref[...], w_ref[...], ON_LANES, preferred_element_type=f32
    ).astype(bf16)
    blocks_at = [pl.ds(b * QB, QB) for b in range(blocks)]
    where = [listed_rows(place, starts, head, b, rows) for b in range(blocks)]
    for b, at in enumerate(blocks_at):
        kv = load_rows(keys, buffer, where[b])
        work[at, :] = lax.dot_general(
            mixed_ref[at, :], kv, ON_LANES, preferred_element_type=f32
        )
    weights = probs_ref[0].astype(f32)
    grad_probs = work[...]
    inner = jnp.sum(weights * grad_probs, axis=-1, keepdims=True)
    scores_ref[...] = (weights * (grad_probs - inner)).astype(bf16)
    for b, at in enumerate(blocks_at):
        kv = load_rows(keys, buffer, where[b])
        grad_q = jnp.dot(scores_ref[at, :], kv, preferred_element_type=f32)
        dq_ref[0, at, :] = (grad_q.astype(bf16).astype(f32) * scale).astype(bf16)
    for b, at in enumerate(blocks_at):
        grads_ref[b] = lax.dot_general(
            jnp.concatenate([scores_ref[at, :], probs_ref[0, at, :]], axis=0),
            jnp.concatenate([q_ref[0, at, :], mixed_ref[at, :]], axis=0),
            ON_ROWS,
            preferred_element_type=f32,
        )
    for b in range(blocks):
        done = 0
        for start, length in where[b]:
            sums[pl.ds(start, length), :] += grads_ref[b, done : done + length, :]
            done += length
    for i in range(2 * count if parts == 2 else parts):
        chunk = sums[chunk_rows(place, i // 2, i % 2, rows), :].astype(bf16)
        if parts == 2:
            outs[i % 2][i // 2, 0] = chunk
        else:
            outs[i][0] = chunk


def attend_back(place, starts, queries, probs, w_out, pieces, parts, count):
    heads, rows, _ = queries.shape
    listed = probs.shape[2]
    per_head = lambda columns: pl.BlockSpec((1, rows, columns), lambda h, *_: (h, 0, 0))
    slots = count if len(parts) == 2 else len(parts) // 2
    if len(parts) == 2:
        out_specs = [pl.BlockSpec((count, 1, rows // 2, WIDE), lambda h, *_: (0, h, 0, 0))] * 2
    else:
        out_specs = [pl.BlockSpec((1, rows // 2, WIDE), lambda h, *_: (h, 0, 0))] * len(parts)
    return pl.pallas_call(
        functools.partial(
            attend_back_kernel, heads=heads, count=count, blocks=rows // QB, parts=len(parts)
        ),
        grid_spec=pltpu.PrefetchScalarGridSpec(
            num_scalar_prefetch=2,
            grid=(heads,),
            in_specs=[
                per_head(WIDE),
                per_head(listed),
                pl.BlockSpec((WIDE, D), lambda h, *_: (h, 0)),
            ]
            + [whole((rows // 2, D))] * 2
            + [pl.BlockSpec(memory_space=pl.ANY)] * len(parts),
            out_specs=[per_head(WIDE), whole((rows, D))] + out_specs,
            scratch_shapes=[
                pltpu.VMEM((2, slots * rows, WIDE), bf16),
                pltpu.VMEM((slots * rows, WIDE), f32),
                pltpu.VMEM((rows, WIDE), bf16),
                pltpu.VMEM((rows, listed), f32),
                pltpu.VMEM((rows, listed), bf16),
                pltpu.VMEM((rows // QB, listed, WIDE), f32),
                pltpu.SemaphoreType.DMA((2, 2 * slots)),
            ],
        ),
        out_shape=[
            jax.ShapeDtypeStruct((heads, rows, WIDE), bf16),
            jax.ShapeDtypeStruct((rows, D), bf16),
        ]
        + [jax.ShapeDtypeStruct(part.shape, bf16) for part in parts],
        compiler_params=params(62 if len(parts) == 2 else 16),
        cost_estimate=cost(
            2 * rows * heads * WIDE * (D + 1536), 4 * heads * WIDE * rows * (slots + 4)
        ),
        name="attend_back",
    )(place, starts, queries, probs, w_out, *pieces, *parts)


def project_back_kernel(place, *refs, heads, terms, norm_row):
    dq_ref, w_ref, normed_ref, param = refs[:4]
    kv_refs = refs[4 : 4 + 2 * terms]
    dkv_ref, bias_ref, sums_ref = refs[4 + 2 * terms : 7 + 2 * terms]
    outs = refs[7 + 2 * terms :]
    gain, shift = row(param, GAIN + norm_row), row(param, SHIFT + norm_row)
    sums_ref[...] = jnp.zeros_like(sums_ref)
    rows = dq_ref.shape[1]
    size = rows // 2
    for h in range(heads):
        bias_ref[h : h + 1, :] = jnp.sum(dq_ref[h].astype(f32), axis=0, keepdims=True)
        over_rows = jnp.zeros((1, WIDE), f32)
        for k in range(2):
            total = kv_refs[k * terms][h].astype(f32)
            for term in kv_refs[k * terms + 1 : (k + 1) * terms]:
                total = total + term[h].astype(f32)
            low = total.astype(bf16)
            dkv_ref[h, half_rows(place, k, size), :] = low
            over_rows = over_rows + jnp.sum(low.astype(f32), axis=0, keepdims=True)
        bias_ref[heads + h : heads + h + 1, :] = over_rows
    for k in range(2):
        at = half_rows(place, k, size)
        grads = jnp.concatenate(
            [dq_ref[h, at, :] for h in range(heads)] + [dkv_ref[h, at, :] for h in range(heads)],
            axis=1,
        )
        grad_normed = jnp.dot(grads, w_ref[...], preferred_element_type=f32)
        outs[k][...] = grad_normed.astype(bf16)
        unit = (normed_ref[at, :].astype(f32) - shift) / gain
        sums_ref[0:1, :] += jnp.sum(grad_normed * unit, axis=0, keepdims=True)
        sums_ref[1:2, :] += jnp.sum(grad_normed, axis=0, keepdims=True)


def project_back(place, dq, w_all, normed, param, kv_terms, norm_row):
    heads, rows, _ = dq.shape
    half = rows // 2
    return pl.pallas_call(
        functools.partial(
            project_back_kernel, heads=heads, terms=len(kv_terms[0]), norm_row=norm_row
        ),
        grid_spec=pltpu.PrefetchScalarGridSpec(
            num_scalar_prefetch=1,
            grid=(1,),
            in_specs=[whole(array.shape) for array in (dq, w_all, normed, param)]
            + [whole((heads, half, WIDE))] * (2 * len(kv_terms[0])),
            out_specs=[whole(dq.shape), whole((2 * heads, WIDE)), whole((2, D))]
            + [whole((half, D))] * 2,
        ),
        out_shape=[
            jax.ShapeDtypeStruct(dq.shape, bf16),
            jax.ShapeDtypeStruct((2 * heads, WIDE), f32),
            jax.ShapeDtypeStruct((2, D), f32),
        ]
        + [jax.ShapeDtypeStruct((half, D), bf16)] * 2,
        compiler_params=params(12),
        cost_estimate=cost(4 * rows * D * heads * WIDE, 4 * D * heads * WIDE + 12 * rows * D),
        name="project_back",
    )(place, dq, w_all, normed, param, *kv_terms[0], *kv_terms[1])


def feed_kernel(place, *refs):
    pieces = refs[:2]
    up_ref, bias_ref, down_ref, kept_ref, slope_ref = refs[2:7]
    outs = refs[7:]
    size = pieces[0].shape[0]
    root = 0.7978845608028654
    cubic = 0.044715
    for k in range(2):
        at = pl.ds(k * size, size)
        normed = pieces[k][...]
        kept_ref[0, at, :] = normed
        inner = jnp.dot(normed, up_ref[...], preferred_element_type=f32) + bias_ref[...]
        square = inner * inner
        bend = jnp.tanh(root * inner * (1.0 + cubic * square))
        half = 0.5 * (1.0 + bend)
        hidden = (inner * half).astype(bf16)
        kept_ref[1, at, :] = hidden
        slope = half + 0.5 * inner * (1.0 - bend * bend) * (root * (1.0 + 3.0 * cubic * square))
        slope_ref[at, :] = slope.astype(bf16)
        outs[k][...] = jnp.dot(hidden, down_ref[...], preferred_element_type=f32).astype(bf16)


def feed(place, pieces, w_up, b_up, w_down):
    half = pieces[0].shape[0]
    rows = 2 * half
    units = w_up.shape[1]
    return pl.pallas_call(
        feed_kernel,
        grid_spec=pltpu.PrefetchScalarGridSpec(
            num_scalar_prefetch=1,
            grid=(1,),
            in_specs=[whole((half, D))] * 2
            + [whole(w_up.shape), whole(b_up.shape), whole(w_down.shape)],
            out_specs=[whole((2, rows, D)), whole((rows, units))] + [whole((half, D))] * 2,
        ),
        out_shape=[
            jax.ShapeDtypeStruct((2, rows, D), bf16),
            jax.ShapeDtypeStruct((rows, units), bf16),
        ]
        + [jax.ShapeDtypeStruct((half, D), bf16)] * 2,
        compiler_params=params(14),
        cost_estimate=cost(4 * rows * D * units, 4 * D * units + 10 * rows * D, rows * units),
        name="feed",
    )(place, *pieces, w_up, b_up, w_down)


def feed_back_kernel(place, *refs):
    pieces = refs[:2]
    down_ref, up_ref, slope_ref, inner_ref, bias_ref = refs[2:7]
    outs = refs[7:]
    size = pieces[0].shape[0]
    transposed = (((1,), (1,)), ((), ()))
    total = None
    for k in range(2):
        at = pl.ds(k * size, size)
        grad = pieces[k][...]
        hidden = lax.dot_general(grad, down_ref[...], transposed, preferred_element_type=f32)
        inner = (hidden * slope_ref[at, :].astype(f32)).astype(bf16)
        inner_ref[at, :] = inner
        part = jnp.sum(inner.astype(f32), axis=0, keepdims=True)
        total = part if total is None else total + part
        outs[k][...] = lax.dot_general(
            inner, up_ref[...], transposed, preferred_element_type=f32
        ).astype(bf16)
    bias_ref[...] = total


def halves_of(pieces, half):
    if len(pieces) == 2:
        return tuple(pieces), [whole((half, D))] * 2
    specs = [
        pl.BlockSpec((half, D), lambda i, place, k=k: ((place[0] & 1) ^ k, 0)) for k in range(2)
    ]
    return tuple(pieces) * 2, specs


def feed_back(place, pieces, w_up, w_down, slope):
    rows, units = slope.shape
    half = rows // 2
    arrays, specs = halves_of(pieces, half)
    return pl.pallas_call(
        feed_back_kernel,
        grid_spec=pltpu.PrefetchScalarGridSpec(
            num_scalar_prefetch=1,
            grid=(1,),
            in_specs=specs + [whole(w_down.shape), whole(w_up.shape), whole(slope.shape)],
            out_specs=[whole((rows, units)), whole((1, units))] + [whole((half, D))] * 2,
        ),
        out_shape=[
            jax.ShapeDtypeStruct((rows, units), bf16),
            jax.ShapeDtypeStruct((1, units), f32),
        ]
        + [jax.ShapeDtypeStruct((half, D), bf16)] * 2,
        compiler_params=params(14),
        cost_estimate=cost(4 * rows * D * units, 4 * D * units + 10 * rows * D),
        name="feed_back",
    )(place, *arrays, w_down, w_up, slope)


def add_norm_kernel(place, *refs, bias_row, norm_row):
    a, b, residual, param, valid = refs[:5]
    out_ref, low_ref, normed_ref, squares_ref = refs[5:]
    branch = a[...].astype(f32) + b[...].astype(f32) + row(param, bias_row)
    total = residual[...].astype(f32) + branch
    out_ref[...] = total
    low = total.astype(bf16)
    low_ref[...] = low
    if norm_row is not None:
        unit, _ = normalise(low.astype(f32))
        gain, shift = row(param, GAIN + norm_row), row(param, SHIFT + norm_row)
        normed_ref[...] = (unit * gain + shift).astype(bf16)
    else:
        normed_ref[...] = low
    weight = valid[...]
    squares_ref[0:1, :] = jnp.sum(weight * branch * branch, axis=0, keepdims=True)
    squares_ref[1:2, :] = jnp.sum(weight * total * total, axis=0, keepdims=True)


def own_half(half):
    return pl.BlockSpec((half, D), lambda i, place: (place[0] & 1, 0))


def add_norm(place, terms, residual, param, valid, rows, bias_row, norm_row):
    half = rows // 2
    spec = whole((half, D))
    return pl.pallas_call(
        functools.partial(add_norm_kernel, bias_row=bias_row, norm_row=norm_row),
        grid_spec=pltpu.PrefetchScalarGridSpec(
            num_scalar_prefetch=1,
            grid=(1,),
            in_specs=[spec] * 2
            + [
                spec,
                whole((PARAM_ROWS, D)),
                whole(valid.shape),
            ],
            out_specs=[spec, spec, spec, whole((2, D))],
        ),
        out_shape=[
            jax.ShapeDtypeStruct((half, D), f32),
            jax.ShapeDtypeStruct((half, D), bf16),
            jax.ShapeDtypeStruct((half, D), bf16),
            jax.ShapeDtypeStruct((2, D), f32),
        ],
        compiler_params=params(8),
        cost_estimate=cost(20 * half * D, 18 * half * D),
        name="add_norm",
    )(place, *terms, residual, param, valid)


def norm_back_kernel(place, *refs, norm_row):
    a, b, source, gradient, param = refs[:5]
    out_ref, low_ref, sums_ref = refs[5:]
    grad_normed = a[...].astype(f32) + b[...].astype(f32)
    unit, inverse = normalise(source[...].astype(f32))
    grad_unit = grad_normed * row(param, GAIN + norm_row)
    first = jnp.mean(grad_unit, axis=-1, keepdims=True)
    second = jnp.mean(grad_unit * unit, axis=-1, keepdims=True)
    total = gradient[...].astype(f32) + inverse * (grad_unit - first - unit * second)
    out_ref[...] = total
    low = total.astype(bf16)
    low_ref[...] = low
    sums_ref[0:1, :] = jnp.sum(grad_normed * unit, axis=0, keepdims=True)
    sums_ref[1:2, :] = jnp.sum(grad_normed, axis=0, keepdims=True)
    sums_ref[2:3, :] = jnp.sum(low.astype(f32), axis=0, keepdims=True)


def norm_back(place, terms, source, gradient, param, rows, norm_row):
    half = rows // 2
    spec = whole((half, D))
    pick = lambda array: spec if array.shape[0] == half else own_half(half)
    return pl.pallas_call(
        functools.partial(norm_back_kernel, norm_row=norm_row),
        grid_spec=pltpu.PrefetchScalarGridSpec(
            num_scalar_prefetch=1,
            grid=(1,),
            in_specs=[spec] * 2 + [pick(source), pick(gradient), whole((PARAM_ROWS, D))],
            out_specs=[spec, spec, whole((3, D))],
        ),
        out_shape=[
            jax.ShapeDtypeStruct((half, D), f32),
            jax.ShapeDtypeStruct((half, D), bf16),
            jax.ShapeDtypeStruct((3, D), f32),
        ],
        compiler_params=params(8),
        cost_estimate=cost(20 * half * D, 18 * half * D),
        name="norm_back",
    )(place, *terms, source, gradient, param)


def piece_slot(place, piece, order):
    away = piece ^ place[5]
    bit = lambda i: (away >> order[i]) & 1
    return bit(0), 2 * bit(1) + bit(2)


def put_piece(place, outs, order, part, piece, value):
    low = value.shape[0]
    at = slice(part * low, (part + 1) * low)
    sent, k = piece_slot(place, piece, order)

    @pl.when(sent == 0)
    def _():
        outs[0][k, at] = value

    @pl.when(sent == 1)
    def _():
        outs[1][k, at] = value


def take_pieces(place, refs, order, staged):
    for piece in range(8):
        sent, k = piece_slot(place, piece, order)

        @pl.when(sent == 0)
        def _():
            staged[piece] = refs[0][k]

        @pl.when(sent == 1)
        def _():
            staged[piece] = refs[1][k]


def square_grads_kernel(place, left_ref, *refs, order, terms):
    rights, outs = refs[:terms], refs[terms:]
    half = D // 2
    low = half // 2
    size = left_ref.shape[1] // terms
    for i in range(2):
        for j in range(2):
            value = sum(
                lax.dot_general(
                    left_ref[0, k * size : (k + 1) * size, i * half : (i + 1) * half],
                    right[:, j * half : (j + 1) * half],
                    ON_ROWS,
                    preferred_element_type=f32,
                )
                for k, right in enumerate(rights)
            ).astype(bf16)
            for part in range(2):
                piece = 4 * i + 2 * j + part
                put_piece(place, outs, order, 0, piece, value[part * low : (part + 1) * low])


def square_grads(place, fed, which, rights, order):
    rows = fed.shape[1]
    if which:
        arrays, specs = halves_of(rights, rows // 2)
    else:
        arrays, specs = tuple(rights), [whole(rights[0].shape)]
    left = pl.BlockSpec((1, rows, D), lambda *_: (which, 0, 0))
    return pieces_call(
        functools.partial(square_grads_kernel, order=order, terms=len(arrays)),
        "down_grads" if which else "up_grads",
        place,
        (fed, *arrays),
        (D // 4, D // 2),
        2 * rows * D * D,
        [left, *specs],
    )


def pieces_call(kernel, name, place, arrays, shape, flops, specs=None):
    return pl.pallas_call(
        kernel,
        grid_spec=pltpu.PrefetchScalarGridSpec(
            num_scalar_prefetch=1,
            grid=(1,),
            in_specs=specs or [whole(array.shape) for array in arrays],
            out_specs=[whole((4,) + shape)] * 2,
        ),
        out_shape=[jax.ShapeDtypeStruct((4,) + shape, bf16)] * 2,
        compiler_params=params(14),
        cost_estimate=cost(flops, 2 * sum(array.size for array in arrays)),
        name=name,
    )(place, *arrays)


def mix_grads_kernel(place, *refs, arrays, groups, order):
    sources, outs = refs[:arrays], refs[arrays:]
    half = D // 2
    parts = 8 // len(groups)
    for j in range(2):
        at = slice(j * half, (j + 1) * half)
        products = {}
        for g, (left, right, first) in enumerate(groups):
            if left not in products:
                heads = sources[left].shape[0]
                products[left] = [
                    lax.dot_general(
                        sources[left][h],
                        sources[right][:, at],
                        ON_ROWS,
                        preferred_element_type=f32,
                    ).astype(bf16)
                    for h in range(heads)
                ]
            value = jnp.concatenate(
                [product[first : first + HD] for product in products[left]], axis=0
            )
            low = value.shape[0] // parts
            for part in range(parts):
                piece = parts * g + part
                put_piece(place, outs, order, j, piece, value[part * low : (part + 1) * low])


def mix_grads(place, arrays, groups, order):
    heads, rows, _ = arrays[0].shape
    return pieces_call(
        functools.partial(mix_grads_kernel, arrays=len(arrays), groups=groups, order=order),
        "mix_grads",
        place,
        arrays,
        (heads * HD * len(groups) // 4, D // 2),
        2 * len(groups) * rows * D * heads * WIDE,
    )


def feed_place_kernel(place, *refs, order):
    outs, staged = refs[-3:-1], refs[-1]
    half = D // 2
    low = half // 2
    take_pieces(place, refs[:2], order, staged)
    for w, out in enumerate(outs):
        for piece in range(8):
            i, j, part = piece // 4, (piece // 2) % 2, piece % 2
            top = i * half + part * low
            value = staged[piece, w * low : (w + 1) * low]
            out[0, top : top + low, j * half : (j + 1) * half] = value.astype(f32)


def mix_place_kernel(place, *refs, bundles):
    first_staged = len(refs) - len(bundles)
    qkv_ref, out_ref = refs[first_staged - 2 : first_staged]
    half = D // 2
    for i, (order, groups) in enumerate(bundles):
        staged = refs[first_staged + i]
        take_pieces(place, refs[2 * i : 2 * i + 2], order, staged)
        parts = 8 // len(groups)
        low = staged.shape[1] // 2
        for j in range(2):
            columns_at = slice(j * half, (j + 1) * half)
            for piece in range(8):
                g, part = groups[piece // parts], piece % parts
                rows = slice(part * low, (part + 1) * low)
                value = staged[piece, j * low : (j + 1) * low].astype(f32)
                if g < 3:
                    qkv_ref[0, g, rows, columns_at] = value
                else:
                    out_ref[0, rows, columns_at] = value


def place_call(kernel, name, place, bundles, earlier, shapes, layer):
    arrays = [array for bundle in bundles for array in bundle]
    specs = [
        pl.BlockSpec((1,) + shape, lambda *_, rank=len(shape): (layer,) + (0,) * rank)
        for shape in shapes
    ]
    kept = [pl.BlockSpec(memory_space=pl.ANY)] * len(earlier)
    size = sum(array.size for array in arrays)
    return pl.pallas_call(
        kernel,
        grid_spec=pltpu.PrefetchScalarGridSpec(
            num_scalar_prefetch=1,
            grid=(1,),
            in_specs=[whole(array.shape) for array in arrays] + kept,
            out_specs=specs,
            scratch_shapes=[pltpu.VMEM((8,) + bundle[0].shape[1:], bf16) for bundle in bundles],
        ),
        out_shape=[jax.ShapeDtypeStruct((LAYERS,) + shape, f32) for shape in shapes],
        input_output_aliases={1 + len(arrays) + i: i for i in range(len(earlier))},
        compiler_params=params(18),
        cost_estimate=cost(size, 6 * size),
        name=name,
    )(place, *arrays, *earlier)


def columns_kernel(place, *refs):
    pieces, out = refs[:2], refs[2]
    size = pieces[0].shape[0]
    width = out.shape[0]
    for p in range(4):

        @pl.when(place[0] == p)
        def _():
            for k in range(2):
                part = pieces[k][:, p * width : (p + 1) * width].astype(f32)
                q = (p & 1) ^ k
                out[:, q * size : (q + 1) * size] = jnp.transpose(part).astype(bf16)


def columns(place, pieces):
    half = pieces[0].shape[0]
    return pl.pallas_call(
        columns_kernel,
        grid_spec=pltpu.PrefetchScalarGridSpec(
            num_scalar_prefetch=1,
            grid=(1,),
            in_specs=[whole((half, D))] * 2,
            out_specs=whole((D // 4, 2 * half)),
        ),
        out_shape=jax.ShapeDtypeStruct((D // 4, 2 * half), bf16),
        compiler_params=params(8),
        cost_estimate=cost(half * D, 8 * half * D),
        name="columns",
    )(place, *pieces)


def on_device(
    residual_in,
    cotangent,
    w_qkv,
    b_qv,
    w_out,
    b_out,
    w_up,
    b_up,
    w_down,
    b_down,
    ln_gain,
    ln_bias,
    selection,
    lengths,
    valid,
):
    rows = residual_in.shape[0]
    heads = selection.shape[0]
    blocks = rows // QB
    half = rows // 2
    count = lax.axis_size("tok")
    position = lax.axis_index("tok")
    member = lax.axis_index("head")
    width = D // 4
    first_row = position * rows
    chosen = lax.dynamic_slice_in_dim(selection, position * blocks, blocks, 1).reshape(heads, -1)
    per_device = rows // KB
    starts = slot_of(chosen // per_device, position, count) * rows + (chosen % per_device) * KB
    place = jnp.stack(
        [
            member,
            position,
            lengths[0],
            slot_of(position, position, count) * rows,
            slot_of(jnp.maximum(position - 1, 0), position, count) * rows,
            position if ring_form(count) else 0,
        ]
    ).astype(jnp.int32)

    first_pieces = share_features(residual_in.T)
    small = jnp.concatenate(
        [ln_gain.reshape(-1, width), ln_bias.reshape(-1, width), b_out, b_down], axis=0
    )
    small = jnp.pad(small, ((0, 128 - small.shape[0]), (0, 0)))
    param_pieces = share_features(small.T)

    split = jnp.transpose(w_qkv, (0, 2, 3, 1)).reshape(LAYERS, 3, heads, HD, D)
    w_all = jnp.concatenate(
        [
            jnp.pad(split[:, 0], ((0, 0), (0, 0), (0, WIDE - HD), (0, 0))),
            jnp.concatenate([split[:, 1], split[:, 2]], axis=2),
        ],
        axis=1,
    ).reshape(LAYERS, 2 * heads * WIDE, D)
    b_split = b_qv.reshape(LAYERS, 2, heads, HD)
    b_all = (
        jnp.concatenate(
            [
                jnp.pad(b_split[:, 0], ((0, 0), (0, 0), (0, HD))),
                jnp.pad(b_split[:, 1], ((0, 0), (0, 0), (HD, 0))),
            ],
            axis=1,
        )
        .reshape(LAYERS, 1, 2 * heads * WIDE)
        .astype(f32)
    )
    w_mix = jnp.pad(
        w_out.reshape(LAYERS, heads, HD, D), ((0, 0), (0, 0), (HD, 0), (0, 0))
    ).reshape(LAYERS, heads * WIDE, D)
    b_inner = b_up.astype(f32)

    far_valid = jnp.tile(valid.reshape(-1, KB), (1, SEL)).astype(f32)
    padded = jnp.concatenate([jnp.zeros((WINDOW,), jnp.int32), valid])
    near = lax.dynamic_slice_in_dim(padded, first_row, rows + WINDOW).reshape(-1, WINDOW)
    near_valid = jnp.concatenate([near[:-1], near[1:]], axis=1).astype(f32)
    own_valid = lax.dynamic_slice_in_dim(valid, first_row + (member & 1) * half, half)
    own_valid = own_valid.astype(f32)[:, None]
    mask = masks(place, chosen, near_valid, far_valid, heads, rows)

    pieces = first_pieces
    lows = []
    kept = []
    squares = []
    for l in range(LAYERS):
        normed, queries, *own_kv = project(
            place, pieces, None if l else param_pieces, w_all[l], b_all[l], rows, heads
        )
        if l == 0:
            own_kv, (low_first, param) = own_kv[:2], own_kv[2:]
            residual = low_first
        parts = gather_blocks(own_kv)
        mixed, probs, *pieces = attend(place, starts, queries, w_mix[l], mask, parts, count)
        residual, low_second, normed_own, branch_squares = add_norm(
            place, sum_rows(pieces), residual, param, own_valid, rows, B_OUT + l, 2 * l + 1
        )
        fed, slope, *pieces = feed(
            place, share_rows(normed_own), w_up[l], b_inner[l : l + 1], w_down[l]
        )
        residual, low_next, normed_own, second_squares = add_norm(
            place,
            sum_rows(pieces),
            residual,
            param,
            own_valid,
            rows,
            B_DOWN + l,
            2 * l + 2 if l + 1 < LAYERS else None,
        )
        squares.append((second_squares[1], branch_squares[0], second_squares[0]))
        kept.append((normed, queries, parts, mixed, probs, low_second, fed, slope))
        lows.append(low_next)
        if l + 1 < LAYERS:
            pieces = share_rows(normed_own)
    residual_out = columns(place, share_rows(lows[-1])).T

    gradient, sums_down = turn(place, share_features(cotangent.T))
    sums_down = sums_down[0]
    grad_pieces = (gradient,)
    grads = [None] * LAYERS
    placed_feed = placed_mix = ()
    shapes_mix = ((3, heads * HD, D), (heads * HD, D))
    for l in reversed(range(LAYERS)):
        last = l == 0
        normed, queries, parts, mixed, probs, low_second, fed, slope = kept[l]
        down_pieces = square_grads(place, fed, 1, grad_pieces, COLUMN_FIRST)
        feeding = Bundle(down_pieces, COLUMN_FIRST)
        feeding.send()
        inner, grad_b_up, *pieces = feed_back(place, grad_pieces, w_up[l], w_down[l], slope)
        up_pieces = square_grads(place, fed, 0, (inner,), COLUMN_FIRST)
        terms, _ = lax.optimization_barrier((sum_rows(pieces), up_pieces))
        terms = feeding.take(terms)
        feeding.add(up_pieces)
        if last:
            terms = feed_before.take(terms)
            feed_before.send()
        gradient, low, second_sums = norm_back(
            place, terms, low_second, gradient, param, rows, 2 * l + 1
        )
        pieces = share_rows(low)
        dq, branch_full, *kv_grads = attend_back(
            place, starts, queries, probs, w_mix[l], pieces, parts, count
        )
        kv_grads = feeding.take(kv_grads)
        if last:
            kv_grads = mix_before.take(feed_before.take(kv_grads))
        kv_terms = return_blocks(kv_grads, lambda other: other)
        if last:
            kv_terms, residual_out = lax.optimization_barrier((kv_terms, residual_out))
        dkv, bias_sums, first_sums, *pieces = project_back(
            place, dq, w_all[l], normed, param, kv_terms, 2 * l
        )
        if not last:
            feeding.send(dkv)
        groups = ((0, 3, 0), (1, 3, 0), (1, 3, HD), (2, 4, HD))
        mix_pieces = mix_grads(
            place, (dq, dkv, mixed, normed, branch_full), groups, COLUMN_FIRST
        )
        mix = Bundle(mix_pieces, COLUMN_FIRST)
        if last:
            finish_in_turn(dkv, feed_before, mix_before, feeding, mix)
        else:
            mix.send()
        terms, _ = lax.optimization_barrier((sum_rows(pieces), mix_pieces))
        if not last:
            terms = feeding.take(terms)
            feeding.send()
            feed_before, mix_before = feeding, mix
        gradient, low, low_sums = norm_back(
            place, terms, lows[l - 1] if l else low_first, gradient, param, rows, 2 * l
        )
        pieces = share_rows(low)
        if not last:
            pieces = mix.take(pieces)
            mix.send()
        grad_pieces = pieces
        grads[l] = (
            None,
            grad_b_up[0],
            jnp.concatenate(
                [
                    bias_sums[:heads, :HD].reshape(-1),
                    bias_sums[heads:, HD:].reshape(-1),
                    jnp.zeros((D - 2 * heads * HD,), f32),
                ]
            ),
            None,
            None,
            second_sums[2],
            sums_down,
            first_sums,
            second_sums,
        )
        sums_down = low_sums[2]
    grad_residual = columns(place, pieces).T
    for l, bundles in ((1, (feed_before, mix_before)), (0, (feeding, mix))):
        placed_feed = place_call(
            functools.partial(feed_place_kernel, order=COLUMN_FIRST),
            "feed_place",
            place,
            [bundles[0].finish()],
            placed_feed,
            ((D, D), (D, D)),
            l,
        )
        done = bundles[1].finish()
        if l == 0:
            done, placed_feed, placed_mix = lax.optimization_barrier(
                (done, placed_feed, placed_mix)
            )
        placed_mix = place_call(
            functools.partial(mix_place_kernel, bundles=((COLUMN_FIRST, (0, 1, 2, 3)),)),
            "mix_place",
            place,
            [done],
            placed_mix,
            shapes_mix,
            l,
        )

    first = jnp.concatenate([grads[l][7] for l in range(LAYERS)], axis=0)
    first = first + swap(first, "head", 2)
    over_all = jnp.concatenate(
        [first]
        + [grads[l][8][:2] for l in range(LAYERS)]
        + [jnp.stack([grads[l][5] for l in range(LAYERS)])]
        + [jnp.stack([grads[l][6] for l in range(LAYERS)])]
        + [jnp.stack([vector for layer in squares for vector in layer])],
        axis=0,
    )
    over_tok = jnp.stack(
        [grads[l][1] for l in range(LAYERS)] + [grads[l][2] for l in range(LAYERS)]
    )
    packed = small_sum(
        jnp.concatenate([over_all + swap(over_all, "head", 1), over_tok], axis=0), "tok"
    )
    stat_row = 4 * LAYERS + 2 * LAYERS
    tok_row = stat_row + 3 * LAYERS
    mine = lax.dynamic_slice_in_dim(packed[:stat_row], member * width, width, 1)
    norms = mine[: 4 * LAYERS].reshape(2, LAYERS, 2, width)
    grad_ln_gain = jnp.stack([norms[0, :, 0], norms[1, :, 0]], axis=1)
    grad_ln_bias = jnp.stack([norms[0, :, 1], norms[1, :, 1]], axis=1)
    grad_b_out = mine[4 * LAYERS : 5 * LAYERS]
    grad_b_down = mine[5 * LAYERS : 6 * LAYERS]
    square_sums = jnp.sum(packed[stat_row:tok_row], axis=-1).reshape(LAYERS, 3)
    valid_count = jnp.maximum(jnp.sum(valid.astype(f32)), 1.0)
    statistics = jnp.sqrt(square_sums / (valid_count * D))
    grad_b_up = packed[tok_row : tok_row + LAYERS]
    grad_b_qv = packed[tok_row + LAYERS :, : 2 * heads * HD].reshape(LAYERS, 2, heads * HD)
    return (
        residual_out,
        grad_residual,
        jnp.transpose(placed_mix[0], (0, 3, 1, 2)),
        grad_b_qv,
        placed_mix[1],
        grad_b_out,
        placed_feed[1],
        grad_b_up,
        placed_feed[0],
        grad_b_down,
        grad_ln_gain,
        grad_ln_bias,
        statistics,
    )


def solution(mesh):
    in_specs = (
        P("tok", "head"),
        P("tok", "head"),
        P(None, None, None, "head"),
        P(None, None, "head"),
        P(None, "head", None),
        P(None, "head"),
        P(None, None, "head"),
        P(None, "head"),
        P(None, "head", None),
        P(None, "head"),
        P(None, None, "head"),
        P(None, None, "head"),
        P("head", None, None),
        P(),
        P(),
    )
    out_specs = (
        P("tok", "head"),
        P("tok", "head"),
        P(None, None, None, "head"),
        P(None, None, "head"),
        P(None, "head", None),
        P(None, "head"),
        P(None, None, "head"),
        P(None, "head"),
        P(None, "head", None),
        P(None, "head"),
        P(None, None, "head"),
        P(None, None, "head"),
        P(),
    )
    return jax.shard_map(
        on_device, mesh=mesh, in_specs=in_specs, out_specs=out_specs, check_vma=False
    )
```

```python
import functools

import jax
import jax.numpy as jnp
from jax import lax
from jax.experimental import pallas as pl
from jax.experimental.pallas import tpu as pltpu
from jax.sharding import PartitionSpec as P

D = 768
HD = 64
LAYERS = 2
WINDOW = 64
KB = 16
SEL = 4
QB = 64
WIDE = 2 * HD

epsilon = 1e-05
negative = -1e30
scale = HD ** (-0.5)
bf16 = jnp.bfloat16
f32 = jnp.float32

STEPS = (0, 2, 1, 3)
GAIN, SHIFT, B_OUT, B_DOWN, PARAM_ROWS = 0, 4, 8, 10, 16


def params(megabytes):
    return pltpu.CompilerParams(vmem_limit_bytes=megabytes * 2**20)


def cost(flops, moved, special=0):
    return pl.CostEstimate(flops=int(flops), bytes_accessed=int(moved), transcendentals=int(special))


def swap(value, axis, step):
    return lax.ppermute(value, axis, [(i, i ^ step) for i in range(lax.axis_size(axis))])


def rotate(value, axis, step):
    count = lax.axis_size(axis)
    return lax.ppermute(value, axis, [(i, (i + step) % count) for i in range(count)])


def share_features(own):
    across = swap(own, "head", 2)
    beside = swap(own, "head", 1)
    both = swap(across, "head", 1)
    return own, across, beside, both


def share_rows(own):
    return own, swap(own, "head", 1)


def sum_rows(pieces):
    own, other = pieces
    chip = (own.astype(f32) + swap(other, "head", 1).astype(f32)).astype(bf16)
    return chip, swap(chip, "head", 2)


def small_sum(value, axis):
    step = 1
    while step < lax.axis_size(axis):
        value = value + swap(value, axis, step)
        step *= 2
    return value


def finish_in_turn(other, *bundles):
    if not bundles[0].ring:
        return
    turns = {True: [], False: []}
    started = []
    for index in TURNS:
        bundle = bundles[index]
        if bundle.step == 6:
            continue
        stage = bundle.step if bundle.step < 3 else 5 - bundle.step
        queue = turns[bundle.order[stage] == 0]
        depth = COLUMN_DEPTH if bundle.order[stage] == 0 else Z_DEPTH
        wait = [other]
        if len(queue) >= depth:
            wait.append(queue[-depth])
        if len(started) >= LAG:
            wait.append(started[-LAG])
        bundle.send(wait)
        queue.append(bundle.coming)
        started.append(bundle.coming)


def ring_form(count):
    return count == 8


COLUMN_FIRST = (0, 1, 2)

TURNS = (0, 1, 2, 3, 0, 1, 2, 3, 1, 2, 1, 3, 2, 3, 2, 3, 3)
COLUMN_DEPTH, Z_DEPTH = 3,4
LAG = 4


def after(value, other):
    return lax.optimization_barrier((value, other))[0]


class Bundle:
    def __init__(self, pieces, order):
        self.ring = ring_form(lax.axis_size("tok"))
        self.step, self.order = 0, order
        self.parts = [tuple(pieces)]
        self.coming = self.kept = ()

    def add(self, pieces):
        self.parts.append(tuple(pieces))
        if self.ring:
            self.coming += (swap(pieces[1], "tok", 1 << self.order[0]),)

    def send(self, other=None):
        if not self.ring or self.step == 6:
            return
        if self.step == 0:
            out = self.parts[0][1]
            self.kept = tuple(kept for kept, _ in self.parts)
        else:
            if self.step == 1:
                self.kept = tuple(kept for kept, _ in self.parts)
            kept, came = self.kept, self.coming
            if other is not None:
                kept, came = after((kept, came), other)
            if self.step < 3:
                kept, out = merge("split", kept, came)
            else:
                (kept,) = merge("add" if self.step == 3 else "join", kept, came)
                out = kept
            self.kept = (kept,)
        if other is not None:
            out = after(out, other)
        stage = self.step if self.step < 3 else 5 - self.step
        self.coming = (swap(out, "tok", 1 << self.order[stage]),)
        self.step += 1

    def take(self, other):
        if not self.ring:
            return other
        self.coming, other = lax.optimization_barrier((self.coming, other))
        return other

    def finish(self):
        while self.ring and self.step < 6:
            self.send()
        if self.ring:
            return self.kept + self.coming
        summed = lax.psum(self.parts, "tok")
        return tuple(
            jnp.concatenate([part[i] for part in summed], axis=1) for i in range(2)
        )


def gather_blocks(chunks):
    count = lax.axis_size("tok")
    if not ring_form(count):
        return [lax.all_gather(chunk, "tok") for chunk in chunks]
    parts = [None] * (2 * count)
    for k, current in enumerate(chunks):
        for hop in range(count // 2):
            other = swap(current, "tok", 1)
            after = None
            if hop < count // 2 - 1:
                after = rotate(current, "tok", 2)
                current, other, after = lax.optimization_barrier((current, other, after))
            parts[4 * hop + k] = current
            parts[4 * hop + 2 + k] = other
            current = after
    return parts


def return_blocks(parts, meanwhile):
    count = lax.axis_size("tok")
    if not ring_form(count):
        return [
            [lax.psum_scatter(part, "tok", scatter_dimension=0, tiled=False)] for part in parts
        ]
    running = [None, None]
    own = [None, None]
    got = [None, None]
    for d in range(count // 2 - 1, -1, -1):
        for k in range(2):
            mine, other = parts[4 * d + k], parts[4 * d + 2 + k]
            if got[k] is not None:
                other, got[k] = lax.optimization_barrier((other, got[k]))
                total = own[k].astype(f32) + got[k].astype(f32)
                if running[k] is not None:
                    total = total + running[k].astype(f32)
                running[k] = rotate(total.astype(bf16), "tok", -2)
            own[k], got[k] = mine, swap(other, "tok", 1)
        if d == 1:
            running = meanwhile(running)
    return [[own[k], got[k], running[k]] for k in range(2)]


def slot_of(block, tok, count):
    if not ring_form(count):
        return block
    away = (tok >> 1) - (block >> 1)
    return 2 * jnp.maximum(away, 0) + ((tok ^ block) & 1)


ON_LANES = (((1,), (1,)), ((), ()))
ON_ROWS = (((0,), (0,)), ((), ()))


def normalise(rows):
    average = jnp.mean(rows, axis=-1, keepdims=True)
    centred = rows - average
    spread = jnp.mean(centred * centred, axis=-1, keepdims=True)
    inverse = lax.rsqrt(spread + epsilon)
    return centred * inverse, inverse


def row(ref, index):
    return ref[index : index + 1, :].astype(f32)


def piece_rows(place, step, size):
    return pl.ds(pl.multiple_of((place[0] ^ step) * size, size), size)


def half_rows(place, k, size):
    return pl.ds(pl.multiple_of(((place[0] & 1) ^ k) * size, size), size)


def project_kernel(place, *refs, heads, first):
    if first:
        pieces, param_pieces = refs[:4], refs[4:8]
        w_ref, bias_ref, normed_ref, q_ref = refs[8:12]
        kv_refs = refs[12:14]
        low_ref, param_ref, staged, turned = refs[14:]
        width = staged.shape[0] // 4
        for k in range(4):
            staged[piece_rows(place, STEPS[k], width), :] = pieces[k][...]
            turned[piece_rows(place, STEPS[k], width), :] = param_pieces[k][...].astype(f32)
        param_ref[...] = jnp.transpose(turned[...])[:PARAM_ROWS]
    else:
        pieces = refs[:2]
        w_ref, bias_ref, normed_ref, q_ref = refs[2:6]
        kv_refs = refs[6:]
    size = normed_ref.shape[0] // 2
    for k in range(2):
        rows = half_rows(place, k, size)
        if first:
            part = jnp.transpose(staged[:, rows].astype(f32))
            if k == 0:
                low_ref[...] = part.astype(bf16)
            unit, _ = normalise(part)
            normed = (unit * row(param_ref, GAIN) + row(param_ref, SHIFT)).astype(bf16)
        else:
            normed = pieces[k][...]
        normed_ref[rows, :] = normed
        projected = lax.dot_general(normed, w_ref[...], ON_LANES, preferred_element_type=f32)
        projected = projected + bias_ref[...]
        for h in range(heads):
            q_ref[h, rows, :] = (projected[:, h * WIDE : (h + 1) * WIDE] * scale).astype(bf16)
            at = (heads + h) * WIDE
            kv_refs[k][h] = projected[:, at : at + WIDE].astype(bf16)


def whole(shape):
    return pl.BlockSpec(shape, lambda *_: (0,) * len(shape))


def project(place, pieces, param_pieces, w_all, bias_all, rows, heads):
    first = param_pieces is not None
    arrays = tuple(pieces) + (tuple(param_pieces) if first else ())
    columns = w_all.shape[0]
    out_shapes = [
        jax.ShapeDtypeStruct((rows, D), bf16),
        jax.ShapeDtypeStruct((heads, rows, WIDE), bf16),
        jax.ShapeDtypeStruct((heads, rows // 2, WIDE), bf16),
        jax.ShapeDtypeStruct((heads, rows // 2, WIDE), bf16),
    ]
    scratch = []
    if first:
        out_shapes += [
            jax.ShapeDtypeStruct((rows // 2, D), bf16),
            jax.ShapeDtypeStruct((PARAM_ROWS, D), f32),
        ]
        scratch = [pltpu.VMEM((D, rows), bf16), pltpu.VMEM((D, 128), f32)]
    return pl.pallas_call(
        functools.partial(project_kernel, heads=heads, first=first),
        grid_spec=pltpu.PrefetchScalarGridSpec(
            num_scalar_prefetch=1,
            grid=(1,),
            in_specs=[whole(array.shape) for array in arrays + (w_all, bias_all)],
            out_specs=[whole(shape.shape) for shape in out_shapes],
            scratch_shapes=scratch,
        ),
        out_shape=out_shapes,
        compiler_params=params(12),
        cost_estimate=cost(2 * rows * D * columns, 2 * D * columns + 8 * rows * D),
        name="project",
    )(place, *arrays, w_all, bias_all)


def turn_kernel(place, *refs):
    pieces = refs[:4]
    out_ref, sums_ref, staged = refs[4:]
    width = staged.shape[0] // 4
    size = out_ref.shape[0] // 2
    for k in range(4):
        staged[piece_rows(place, STEPS[k], width), :] = pieces[k][...]
    for k in range(2):
        part = jnp.transpose(staged[:, k * size : (k + 1) * size].astype(f32))
        out_ref[k * size : (k + 1) * size, :] = part.astype(bf16)

        @pl.when((place[0] & 1) == k)
        def _():
            sums_ref[...] = jnp.sum(part, axis=0, keepdims=True)


def turn(place, pieces):
    width, rows = pieces[0].shape
    return pl.pallas_call(
        turn_kernel,
        grid_spec=pltpu.PrefetchScalarGridSpec(
            num_scalar_prefetch=1,
            grid=(1,),
            in_specs=[whole((width, rows))] * 4,
            out_specs=[whole((rows, D)), whole((1, D))],
            scratch_shapes=[pltpu.VMEM((D, rows), bf16)],
        ),
        out_shape=[jax.ShapeDtypeStruct((rows, D), bf16), jax.ShapeDtypeStruct((1, D), f32)],
        compiler_params=params(6),
        cost_estimate=cost(rows * D, 4 * rows * D),
        name="turn",
    )(place, *pieces)


def merge_kernel(*refs, act, parts):
    count = refs[0].shape[0]
    outs = refs[2 * parts :]
    each = count // len(outs)
    for part in range(parts):
        kept, came = refs[part], refs[parts + part]
        size = kept.shape[1]
        rows = slice(part * size, (part + 1) * size)
        if act == "join":
            outs[0][:count, rows] = kept[...]
            outs[0][count:, rows] = came[...]
            continue
        for i, out in enumerate(outs):
            at = slice(i * each, (i + 1) * each)
            out[:, rows] = (kept[at].astype(f32) + came[at].astype(f32)).astype(bf16)


def merge(act, kept, came):
    count, _, width = kept[0].shape
    size = sum(array.shape[1] for array in kept)
    counts = {"add": [count], "split": [count // 2] * 2, "join": [2 * count]}[act]
    shapes = [(n, size, width) for n in counts]
    total = count * size * width
    return pl.pallas_call(
        functools.partial(merge_kernel, act=act, parts=len(kept)),
        grid=(1,),
        in_specs=[whole(array.shape) for array in (*kept, *came)],
        out_specs=[whole(shape) for shape in shapes],
        out_shape=[jax.ShapeDtypeStruct(shape, bf16) for shape in shapes],
        compiler_params=params(12),
        cost_estimate=cost(total, 8 * total),
        name="merge",
    )(*kept, *came)


def chunk_rows(place, slot, k, rows):
    return pl.ds(pl.multiple_of(slot * rows + ((place[0] & 1) ^ k) * (rows // 2), rows // 2), rows // 2)


def copies(place, parts, scratch, sems, head, buffer, rows):
    if len(parts) == 2:
        sources = [parts[k].at[slot, head] for slot in range(parts[0].shape[0]) for k in range(2)]
    else:
        sources = [part.at[head] for part in parts]
    return [
        pltpu.make_async_copy(
            source,
            scratch.at[buffer, chunk_rows(place, i // 2, i % 2, rows), :],
            sems.at[buffer, i],
        )
        for i, source in enumerate(sources)
    ]


def bring_blocks(place, parts, scratch, sems, heads, rows):
    head = pl.program_id(0)
    buffer = lax.rem(head, 2)

    @pl.when(head == 0)
    def _():
        for copy in copies(place, parts, scratch, sems, 0, 0, rows):
            copy.start()

    @pl.when(head + 1 < heads)
    def _():
        for copy in copies(place, parts, scratch, sems, head + 1, 1 - buffer, rows):
            copy.start()

    for copy in copies(place, parts, scratch, sems, head, buffer, rows):
        copy.wait()
    return head, buffer


def listed_rows(place, starts, head, b, rows):
    own, before = place[3], place[4]
    if b == 0:
        near = [
            (pl.multiple_of(before + rows - WINDOW, WINDOW), WINDOW),
            (pl.multiple_of(own, WINDOW), WINDOW),
        ]
    else:
        near = [(pl.multiple_of(own + (b - 1) * QB, WINDOW), 2 * WINDOW)]
    far = [(pl.multiple_of(starts[head, b * SEL + s], KB), KB) for s in range(SEL)]
    return near + far


def load_rows(keys, buffer, where):
    return jnp.concatenate([keys[buffer, pl.ds(start, size), :] for start, size in where], axis=0)


def mask_kernel(place, chosen, near_ref, far_ref, out_ref, *, heads, blocks):
    rows = blocks * QB
    tok, boundary = place[1], place[2]
    wide = 2 * WINDOW
    line = lax.broadcasted_iota(jnp.int32, (QB, wide), 1)
    column = lax.broadcasted_iota(jnp.int32, (QB, wide), 0)
    band = (line > column) & (line <= column + WINDOW)
    diagonal = line == column + WINDOW
    in_second = lambda position: jnp.where(position >= boundary, 1, 0)
    lane = lax.broadcasted_iota(jnp.int32, (1, SEL * KB), 1)
    for b in range(blocks):
        first = tok * rows + b * QB
        query_seq = in_second(first + lax.broadcasted_iota(jnp.int32, (QB, 1), 0))
        key = first - WINDOW + lax.broadcasted_iota(jnp.int32, (1, wide), 1)
        near = band & (diagonal | (near_ref[b : b + 1, :] > 0.0))
        near = jnp.where(near & (in_second(key) == query_seq), 0.0, negative)
        for head in range(heads):
            usable = jnp.zeros((1, SEL * KB), f32)
            token = lane & (KB - 1)
            for s in range(SEL):
                block = chosen[head, b * SEL + s]
                here = (lane >= s * KB) & (lane < (s + 1) * KB)
                early = block * KB + KB <= first - WINDOW
                usable = jnp.where(here & early, far_ref[pl.ds(block, 1), :], usable)
                token = token + jnp.where(here, block * KB, 0)
            far = (usable > 0.0) & (in_second(token) == query_seq)
            at = pl.ds(b * QB, QB)
            out_ref[head, at, :wide] = near
            out_ref[head, at, wide:] = jnp.where(far, 0.0, negative)


def masks(place, chosen, near_valid, far_valid, heads, rows):
    listed = 2 * WINDOW + SEL * KB
    return pl.pallas_call(
        functools.partial(mask_kernel, heads=heads, blocks=rows // QB),
        grid_spec=pltpu.PrefetchScalarGridSpec(
            num_scalar_prefetch=2,
            grid=(1,),
            in_specs=[whole(near_valid.shape), whole(far_valid.shape)],
            out_specs=whole((heads, rows, listed)),
        ),
        out_shape=jax.ShapeDtypeStruct((heads, rows, listed), f32),
        compiler_params=params(6),
        cost_estimate=cost(20 * heads * rows * listed, 4 * heads * rows * listed),
        name="masks",
    )(place, chosen, near_valid, far_valid)


def attend_kernel(place, starts, *refs, heads, blocks, parts):
    q_ref, w_ref, mask_ref = refs[:3]
    kv_parts = refs[3 : 3 + parts]
    mixed_ref, probs_ref = refs[3 + parts : 5 + parts]
    outs = refs[5 + parts : 7 + parts]
    keys, gathered, work, sems = refs[7 + parts :]
    rows = blocks * QB
    head, buffer = bring_blocks(place, kv_parts, keys, sems, heads, rows)
    blocks_at = [pl.ds(b * QB, QB) for b in range(blocks)]
    where = [listed_rows(place, starts, head, b, rows) for b in range(blocks)]
    for b, at in enumerate(blocks_at):
        kv = load_rows(keys, buffer, where[b])
        scores = lax.dot_general(q_ref[0, at, :], kv, ON_LANES, preferred_element_type=f32)
        work[at, :] = scores + mask_ref[0, at, :]
    scores = work[...]
    weights = jnp.exp(scores - jnp.max(scores, axis=-1, keepdims=True))
    weights = weights * (1.0 / jnp.sum(weights, axis=-1, keepdims=True))
    probs_ref[0] = weights.astype(bf16)
    for b, at in enumerate(blocks_at):
        kv = load_rows(keys, buffer, where[b])
        out = jnp.dot(probs_ref[0, at, :], kv, preferred_element_type=f32).astype(bf16)
        mixed_ref[0, at, :] = out
        gathered[head, at, :] = out

    @pl.when(head == heads - 1)
    def _():
        size = rows // 2
        for k in range(2):
            at = half_rows(place, k, size)
            mixed = jnp.concatenate([gathered[h, at, :] for h in range(heads)], axis=1)
            outs[k][...] = jnp.dot(mixed, w_ref[...], preferred_element_type=f32).astype(bf16)


def attend(place, starts, queries, w_out, mask, parts, count):
    heads, rows, _ = queries.shape
    listed = mask.shape[2]
    per_head = lambda columns: pl.BlockSpec((1, rows, columns), lambda h, *_: (h, 0, 0))
    slots = count if len(parts) == 2 else len(parts) // 2
    return pl.pallas_call(
        functools.partial(attend_kernel, heads=heads, blocks=rows // QB, parts=len(parts)),
        grid_spec=pltpu.PrefetchScalarGridSpec(
            num_scalar_prefetch=2,
            grid=(heads,),
            in_specs=[per_head(WIDE), whole(w_out.shape), per_head(listed)]
            + [pl.BlockSpec(memory_space=pl.ANY)] * len(parts),
            out_specs=[per_head(WIDE), per_head(listed)] + [whole((rows // 2, D))] * 2,
            scratch_shapes=[
                pltpu.VMEM((2, slots * rows, WIDE), bf16),
                pltpu.VMEM((heads, rows, WIDE), bf16),
                pltpu.VMEM((rows, listed), f32),
                pltpu.SemaphoreType.DMA((2, 2 * slots)),
            ],
        ),
        out_shape=[
            jax.ShapeDtypeStruct((heads, rows, WIDE), bf16),
            jax.ShapeDtypeStruct((heads, rows, listed), bf16),
        ]
        + [jax.ShapeDtypeStruct((rows // 2, D), bf16)] * 2,
        compiler_params=params(30 if len(parts) == 2 else 12),
        cost_estimate=cost(
            2 * rows * heads * WIDE * (D + 512), 2 * heads * WIDE * rows * (slots + 4)
        ),
        name="attend",
    )(place, starts, queries, w_out, mask, *parts)


def attend_back_kernel(place, starts, *refs, heads, count, blocks, parts):
    q_ref, probs_ref, w_ref = refs[:3]
    pieces = refs[3:5]
    kv_parts = refs[5 : 5 + parts]
    dq_ref, grad_ref = refs[5 + parts : 7 + parts]
    outs = refs[7 + parts : 7 + 2 * parts]
    keys, sums, mixed_ref, work, scores_ref, grads_ref, sems = refs[7 + 2 * parts :]
    rows = blocks * QB
    size = rows // 2
    head, buffer = bring_blocks(place, kv_parts, keys, sems, heads, rows)

    @pl.when(head == 0)
    def _():
        for k in range(2):
            grad_ref[half_rows(place, k, size), :] = pieces[k][...]

    sums[...] = jnp.zeros_like(sums)
    mixed_ref[...] = lax.dot_general(
        grad_ref[...], w_ref[...], ON_LANES, preferred_element_type=f32
    ).astype(bf16)
    blocks_at = [pl.ds(b * QB, QB) for b in range(blocks)]
    where = [listed_rows(place, starts, head, b, rows) for b in range(blocks)]
    for b, at in enumerate(blocks_at):
        kv = load_rows(keys, buffer, where[b])
        work[at, :] = lax.dot_general(
            mixed_ref[at, :], kv, ON_LANES, preferred_element_type=f32
        )
    weights = probs_ref[0].astype(f32)
    grad_probs = work[...]
    inner = jnp.sum(weights * grad_probs, axis=-1, keepdims=True)
    scores_ref[...] = (weights * (grad_probs - inner)).astype(bf16)
    for b, at in enumerate(blocks_at):
        kv = load_rows(keys, buffer, where[b])
        grad_q = jnp.dot(scores_ref[at, :], kv, preferred_element_type=f32)
        dq_ref[0, at, :] = (grad_q.astype(bf16).astype(f32) * scale).astype(bf16)
    for b, at in enumerate(blocks_at):
        grads_ref[b] = lax.dot_general(
            jnp.concatenate([scores_ref[at, :], probs_ref[0, at, :]], axis=0),
            jnp.concatenate([q_ref[0, at, :], mixed_ref[at, :]], axis=0),
            ON_ROWS,
            preferred_element_type=f32,
        )
    for b in range(blocks):
        done = 0
        for start, length in where[b]:
            sums[pl.ds(start, length), :] += grads_ref[b, done : done + length, :]
            done += length
    for i in range(2 * count if parts == 2 else parts):
        chunk = sums[chunk_rows(place, i // 2, i % 2, rows), :].astype(bf16)
        if parts == 2:
            outs[i % 2][i // 2, 0] = chunk
        else:
            outs[i][0] = chunk


def attend_back(place, starts, queries, probs, w_out, pieces, parts, count):
    heads, rows, _ = queries.shape
    listed = probs.shape[2]
    per_head = lambda columns: pl.BlockSpec((1, rows, columns), lambda h, *_: (h, 0, 0))
    slots = count if len(parts) == 2 else len(parts) // 2
    if len(parts) == 2:
        out_specs = [pl.BlockSpec((count, 1, rows // 2, WIDE), lambda h, *_: (0, h, 0, 0))] * 2
    else:
        out_specs = [pl.BlockSpec((1, rows // 2, WIDE), lambda h, *_: (h, 0, 0))] * len(parts)
    return pl.pallas_call(
        functools.partial(
            attend_back_kernel, heads=heads, count=count, blocks=rows // QB, parts=len(parts)
        ),
        grid_spec=pltpu.PrefetchScalarGridSpec(
            num_scalar_prefetch=2,
            grid=(heads,),
            in_specs=[
                per_head(WIDE),
                per_head(listed),
                pl.BlockSpec((WIDE, D), lambda h, *_: (h, 0)),
            ]
            + [whole((rows // 2, D))] * 2
            + [pl.BlockSpec(memory_space=pl.ANY)] * len(parts),
            out_specs=[per_head(WIDE), whole((rows, D))] + out_specs,
            scratch_shapes=[
                pltpu.VMEM((2, slots * rows, WIDE), bf16),
                pltpu.VMEM((slots * rows, WIDE), f32),
                pltpu.VMEM((rows, WIDE), bf16),
                pltpu.VMEM((rows, listed), f32),
                pltpu.VMEM((rows, listed), bf16),
                pltpu.VMEM((rows // QB, listed, WIDE), f32),
                pltpu.SemaphoreType.DMA((2, 2 * slots)),
            ],
        ),
        out_shape=[
            jax.ShapeDtypeStruct((heads, rows, WIDE), bf16),
            jax.ShapeDtypeStruct((rows, D), bf16),
        ]
        + [jax.ShapeDtypeStruct(part.shape, bf16) for part in parts],
        compiler_params=params(62 if len(parts) == 2 else 16),
        cost_estimate=cost(
            2 * rows * heads * WIDE * (D + 1536), 4 * heads * WIDE * rows * (slots + 4)
        ),
        name="attend_back",
    )(place, starts, queries, probs, w_out, *pieces, *parts)


def project_back_kernel(place, *refs, heads, terms, norm_row):
    dq_ref, w_ref, normed_ref, param = refs[:4]
    kv_refs = refs[4 : 4 + 2 * terms]
    dkv_ref, bias_ref, sums_ref = refs[4 + 2 * terms : 7 + 2 * terms]
    outs = refs[7 + 2 * terms :]
    gain, shift = row(param, GAIN + norm_row), row(param, SHIFT + norm_row)
    sums_ref[...] = jnp.zeros_like(sums_ref)
    rows = dq_ref.shape[1]
    size = rows // 2
    for h in range(heads):
        bias_ref[h : h + 1, :] = jnp.sum(dq_ref[h].astype(f32), axis=0, keepdims=True)
        over_rows = jnp.zeros((1, WIDE), f32)
        for k in range(2):
            total = kv_refs[k * terms][h].astype(f32)
            for term in kv_refs[k * terms + 1 : (k + 1) * terms]:
                total = total + term[h].astype(f32)
            low = total.astype(bf16)
            dkv_ref[h, half_rows(place, k, size), :] = low
            over_rows = over_rows + jnp.sum(low.astype(f32), axis=0, keepdims=True)
        bias_ref[heads + h : heads + h + 1, :] = over_rows
    for k in range(2):
        at = half_rows(place, k, size)
        grads = jnp.concatenate(
            [dq_ref[h, at, :] for h in range(heads)] + [dkv_ref[h, at, :] for h in range(heads)],
            axis=1,
        )
        grad_normed = jnp.dot(grads, w_ref[...], preferred_element_type=f32)
        outs[k][...] = grad_normed.astype(bf16)
        unit = (normed_ref[at, :].astype(f32) - shift) / gain
        sums_ref[0:1, :] += jnp.sum(grad_normed * unit, axis=0, keepdims=True)
        sums_ref[1:2, :] += jnp.sum(grad_normed, axis=0, keepdims=True)


def project_back(place, dq, w_all, normed, param, kv_terms, norm_row):
    heads, rows, _ = dq.shape
    half = rows // 2
    return pl.pallas_call(
        functools.partial(
            project_back_kernel, heads=heads, terms=len(kv_terms[0]), norm_row=norm_row
        ),
        grid_spec=pltpu.PrefetchScalarGridSpec(
            num_scalar_prefetch=1,
            grid=(1,),
            in_specs=[whole(array.shape) for array in (dq, w_all, normed, param)]
            + [whole((heads, half, WIDE))] * (2 * len(kv_terms[0])),
            out_specs=[whole(dq.shape), whole((2 * heads, WIDE)), whole((2, D))]
            + [whole((half, D))] * 2,
        ),
        out_shape=[
            jax.ShapeDtypeStruct(dq.shape, bf16),
            jax.ShapeDtypeStruct((2 * heads, WIDE), f32),
            jax.ShapeDtypeStruct((2, D), f32),
        ]
        + [jax.ShapeDtypeStruct((half, D), bf16)] * 2,
        compiler_params=params(12),
        cost_estimate=cost(4 * rows * D * heads * WIDE, 4 * D * heads * WIDE + 12 * rows * D),
        name="project_back",
    )(place, dq, w_all, normed, param, *kv_terms[0], *kv_terms[1])


def feed_kernel(place, *refs):
    pieces = refs[:2]
    up_ref, bias_ref, down_ref, kept_ref, slope_ref = refs[2:7]
    outs = refs[7:]
    size = pieces[0].shape[0]
    root = 0.7978845608028654
    cubic = 0.044715
    for k in range(2):
        at = pl.ds(k * size, size)
        normed = pieces[k][...]
        kept_ref[0, at, :] = normed
        inner = jnp.dot(normed, up_ref[...], preferred_element_type=f32) + bias_ref[...]
        square = inner * inner
        bend = jnp.tanh(root * inner * (1.0 + cubic * square))
        half = 0.5 * (1.0 + bend)
        hidden = (inner * half).astype(bf16)
        kept_ref[1, at, :] = hidden
        slope = half + 0.5 * inner * (1.0 - bend * bend) * (root * (1.0 + 3.0 * cubic * square))
        slope_ref[at, :] = slope.astype(bf16)
        outs[k][...] = jnp.dot(hidden, down_ref[...], preferred_element_type=f32).astype(bf16)


def feed(place, pieces, w_up, b_up, w_down):
    half = pieces[0].shape[0]
    rows = 2 * half
    units = w_up.shape[1]
    return pl.pallas_call(
        feed_kernel,
        grid_spec=pltpu.PrefetchScalarGridSpec(
            num_scalar_prefetch=1,
            grid=(1,),
            in_specs=[whole((half, D))] * 2
            + [whole(w_up.shape), whole(b_up.shape), whole(w_down.shape)],
            out_specs=[whole((2, rows, D)), whole((rows, units))] + [whole((half, D))] * 2,
        ),
        out_shape=[
            jax.ShapeDtypeStruct((2, rows, D), bf16),
            jax.ShapeDtypeStruct((rows, units), bf16),
        ]
        + [jax.ShapeDtypeStruct((half, D), bf16)] * 2,
        compiler_params=params(14),
        cost_estimate=cost(4 * rows * D * units, 4 * D * units + 10 * rows * D, rows * units),
        name="feed",
    )(place, *pieces, w_up, b_up, w_down)


def feed_back_kernel(place, *refs):
    pieces = refs[:2]
    down_ref, up_ref, slope_ref, inner_ref, bias_ref = refs[2:7]
    outs = refs[7:]
    size = pieces[0].shape[0]
    transposed = (((1,), (1,)), ((), ()))
    total = None
    for k in range(2):
        at = pl.ds(k * size, size)
        grad = pieces[k][...]
        hidden = lax.dot_general(grad, down_ref[...], transposed, preferred_element_type=f32)
        inner = (hidden * slope_ref[at, :].astype(f32)).astype(bf16)
        inner_ref[at, :] = inner
        part = jnp.sum(inner.astype(f32), axis=0, keepdims=True)
        total = part if total is None else total + part
        outs[k][...] = lax.dot_general(
            inner, up_ref[...], transposed, preferred_element_type=f32
        ).astype(bf16)
    bias_ref[...] = total


def halves_of(pieces, half):
    if len(pieces) == 2:
        return tuple(pieces), [whole((half, D))] * 2
    specs = [
        pl.BlockSpec((half, D), lambda i, place, k=k: ((place[0] & 1) ^ k, 0)) for k in range(2)
    ]
    return tuple(pieces) * 2, specs


def feed_back(place, pieces, w_up, w_down, slope):
    rows, units = slope.shape
    half = rows // 2
    arrays, specs = halves_of(pieces, half)
    return pl.pallas_call(
        feed_back_kernel,
        grid_spec=pltpu.PrefetchScalarGridSpec(
            num_scalar_prefetch=1,
            grid=(1,),
            in_specs=specs + [whole(w_down.shape), whole(w_up.shape), whole(slope.shape)],
            out_specs=[whole((rows, units)), whole((1, units))] + [whole((half, D))] * 2,
        ),
        out_shape=[
            jax.ShapeDtypeStruct((rows, units), bf16),
            jax.ShapeDtypeStruct((1, units), f32),
        ]
        + [jax.ShapeDtypeStruct((half, D), bf16)] * 2,
        compiler_params=params(14),
        cost_estimate=cost(4 * rows * D * units, 4 * D * units + 10 * rows * D),
        name="feed_back",
    )(place, *arrays, w_down, w_up, slope)


def add_norm_kernel(place, *refs, bias_row, norm_row):
    a, b, residual, param, valid = refs[:5]
    out_ref, low_ref, normed_ref, squares_ref = refs[5:]
    branch = a[...].astype(f32) + b[...].astype(f32) + row(param, bias_row)
    total = residual[...].astype(f32) + branch
    out_ref[...] = total
    low = total.astype(bf16)
    low_ref[...] = low
    if norm_row is not None:
        unit, _ = normalise(low.astype(f32))
        gain, shift = row(param, GAIN + norm_row), row(param, SHIFT + norm_row)
        normed_ref[...] = (unit * gain + shift).astype(bf16)
    else:
        normed_ref[...] = low
    weight = valid[...]
    squares_ref[0:1, :] = jnp.sum(weight * branch * branch, axis=0, keepdims=True)
    squares_ref[1:2, :] = jnp.sum(weight * total * total, axis=0, keepdims=True)


def own_half(half):
    return pl.BlockSpec((half, D), lambda i, place: (place[0] & 1, 0))


def add_norm(place, terms, residual, param, valid, rows, bias_row, norm_row):
    half = rows // 2
    spec = whole((half, D))
    return pl.pallas_call(
        functools.partial(add_norm_kernel, bias_row=bias_row, norm_row=norm_row),
        grid_spec=pltpu.PrefetchScalarGridSpec(
            num_scalar_prefetch=1,
            grid=(1,),
            in_specs=[spec] * 2
            + [
                spec,
                whole((PARAM_ROWS, D)),
                whole(valid.shape),
            ],
            out_specs=[spec, spec, spec, whole((2, D))],
        ),
        out_shape=[
            jax.ShapeDtypeStruct((half, D), f32),
            jax.ShapeDtypeStruct((half, D), bf16),
            jax.ShapeDtypeStruct((half, D), bf16),
            jax.ShapeDtypeStruct((2, D), f32),
        ],
        compiler_params=params(8),
        cost_estimate=cost(20 * half * D, 18 * half * D),
        name="add_norm",
    )(place, *terms, residual, param, valid)


def norm_back_kernel(place, *refs, norm_row):
    a, b, source, gradient, param = refs[:5]
    out_ref, low_ref, sums_ref = refs[5:]
    grad_normed = a[...].astype(f32) + b[...].astype(f32)
    unit, inverse = normalise(source[...].astype(f32))
    grad_unit = grad_normed * row(param, GAIN + norm_row)
    first = jnp.mean(grad_unit, axis=-1, keepdims=True)
    second = jnp.mean(grad_unit * unit, axis=-1, keepdims=True)
    total = gradient[...].astype(f32) + inverse * (grad_unit - first - unit * second)
    out_ref[...] = total
    low = total.astype(bf16)
    low_ref[...] = low
    sums_ref[0:1, :] = jnp.sum(grad_normed * unit, axis=0, keepdims=True)
    sums_ref[1:2, :] = jnp.sum(grad_normed, axis=0, keepdims=True)
    sums_ref[2:3, :] = jnp.sum(low.astype(f32), axis=0, keepdims=True)


def norm_back(place, terms, source, gradient, param, rows, norm_row):
    half = rows // 2
    spec = whole((half, D))
    pick = lambda array: spec if array.shape[0] == half else own_half(half)
    return pl.pallas_call(
        functools.partial(norm_back_kernel, norm_row=norm_row),
        grid_spec=pltpu.PrefetchScalarGridSpec(
            num_scalar_prefetch=1,
            grid=(1,),
            in_specs=[spec] * 2 + [pick(source), pick(gradient), whole((PARAM_ROWS, D))],
            out_specs=[spec, spec, whole((3, D))],
        ),
        out_shape=[
            jax.ShapeDtypeStruct((half, D), f32),
            jax.ShapeDtypeStruct((half, D), bf16),
            jax.ShapeDtypeStruct((3, D), f32),
        ],
        compiler_params=params(8),
        cost_estimate=cost(20 * half * D, 18 * half * D),
        name="norm_back",
    )(place, *terms, source, gradient, param)


def piece_slot(place, piece, order):
    away = piece ^ place[5]
    bit = lambda i: (away >> order[i]) & 1
    return bit(0), 2 * bit(1) + bit(2)


def put_piece(place, outs, order, part, piece, value):
    low = value.shape[0]
    at = slice(part * low, (part + 1) * low)
    sent, k = piece_slot(place, piece, order)

    @pl.when(sent == 0)
    def _():
        outs[0][k, at] = value

    @pl.when(sent == 1)
    def _():
        outs[1][k, at] = value


def take_pieces(place, refs, order, staged):
    for piece in range(8):
        sent, k = piece_slot(place, piece, order)

        @pl.when(sent == 0)
        def _():
            staged[piece] = refs[0][k]

        @pl.when(sent == 1)
        def _():
            staged[piece] = refs[1][k]


def square_grads_kernel(place, left_ref, *refs, order, terms):
    rights, outs = refs[:terms], refs[terms:]
    half = D // 2
    low = half // 2
    size = left_ref.shape[1] // terms
    for i in range(2):
        for j in range(2):
            value = sum(
                lax.dot_general(
                    left_ref[0, k * size : (k + 1) * size, i * half : (i + 1) * half],
                    right[:, j * half : (j + 1) * half],
                    ON_ROWS,
                    preferred_element_type=f32,
                )
                for k, right in enumerate(rights)
            ).astype(bf16)
            for part in range(2):
                piece = 4 * i + 2 * j + part
                put_piece(place, outs, order, 0, piece, value[part * low : (part + 1) * low])


def square_grads(place, fed, which, rights, order):
    rows = fed.shape[1]
    if which:
        arrays, specs = halves_of(rights, rows // 2)
    else:
        arrays, specs = tuple(rights), [whole(rights[0].shape)]
    left = pl.BlockSpec((1, rows, D), lambda *_: (which, 0, 0))
    return pieces_call(
        functools.partial(square_grads_kernel, order=order, terms=len(arrays)),
        "down_grads" if which else "up_grads",
        place,
        (fed, *arrays),
        (D // 4, D // 2),
        2 * rows * D * D,
        [left, *specs],
    )


def pieces_call(kernel, name, place, arrays, shape, flops, specs=None):
    return pl.pallas_call(
        kernel,
        grid_spec=pltpu.PrefetchScalarGridSpec(
            num_scalar_prefetch=1,
            grid=(1,),
            in_specs=specs or [whole(array.shape) for array in arrays],
            out_specs=[whole((4,) + shape)] * 2,
        ),
        out_shape=[jax.ShapeDtypeStruct((4,) + shape, bf16)] * 2,
        compiler_params=params(14),
        cost_estimate=cost(flops, 2 * sum(array.size for array in arrays)),
        name=name,
    )(place, *arrays)


def mix_grads_kernel(place, *refs, arrays, groups, order):
    sources, outs = refs[:arrays], refs[arrays:]
    half = D // 2
    parts = 8 // len(groups)
    for j in range(2):
        at = slice(j * half, (j + 1) * half)
        products = {}
        for g, (left, right, first) in enumerate(groups):
            if left not in products:
                heads = sources[left].shape[0]
                products[left] = [
                    lax.dot_general(
                        sources[left][h],
                        sources[right][:, at],
                        ON_ROWS,
                        preferred_element_type=f32,
                    ).astype(bf16)
                    for h in range(heads)
                ]
            value = jnp.concatenate(
                [product[first : first + HD] for product in products[left]], axis=0
            )
            low = value.shape[0] // parts
            for part in range(parts):
                piece = parts * g + part
                put_piece(place, outs, order, j, piece, value[part * low : (part + 1) * low])


def mix_grads(place, arrays, groups, order):
    heads, rows, _ = arrays[0].shape
    return pieces_call(
        functools.partial(mix_grads_kernel, arrays=len(arrays), groups=groups, order=order),
        "mix_grads",
        place,
        arrays,
        (heads * HD * len(groups) // 4, D // 2),
        2 * len(groups) * rows * D * heads * WIDE,
    )


def feed_place_kernel(place, *refs, order):
    outs, staged = refs[-3:-1], refs[-1]
    half = D // 2
    low = half // 2
    take_pieces(place, refs[:2], order, staged)
    for w, out in enumerate(outs):
        for piece in range(8):
            i, j, part = piece // 4, (piece // 2) % 2, piece % 2
            top = i * half + part * low
            value = staged[piece, w * low : (w + 1) * low]
            out[0, top : top + low, j * half : (j + 1) * half] = value.astype(f32)


def mix_place_kernel(place, *refs, bundles):
    first_staged = len(refs) - len(bundles)
    qkv_ref, out_ref = refs[first_staged - 2 : first_staged]
    half = D // 2
    for i, (order, groups) in enumerate(bundles):
        staged = refs[first_staged + i]
        take_pieces(place, refs[2 * i : 2 * i + 2], order, staged)
        parts = 8 // len(groups)
        low = staged.shape[1] // 2
        for j in range(2):
            columns_at = slice(j * half, (j + 1) * half)
            for piece in range(8):
                g, part = groups[piece // parts], piece % parts
                rows = slice(part * low, (part + 1) * low)
                value = staged[piece, j * low : (j + 1) * low].astype(f32)
                if g < 3:
                    qkv_ref[0, g, rows, columns_at] = value
                else:
                    out_ref[0, rows, columns_at] = value


def place_call(kernel, name, place, bundles, earlier, shapes, layer):
    arrays = [array for bundle in bundles for array in bundle]
    specs = [
        pl.BlockSpec((1,) + shape, lambda *_, rank=len(shape): (layer,) + (0,) * rank)
        for shape in shapes
    ]
    kept = [pl.BlockSpec(memory_space=pl.ANY)] * len(earlier)
    size = sum(array.size for array in arrays)
    return pl.pallas_call(
        kernel,
        grid_spec=pltpu.PrefetchScalarGridSpec(
            num_scalar_prefetch=1,
            grid=(1,),
            in_specs=[whole(array.shape) for array in arrays] + kept,
            out_specs=specs,
            scratch_shapes=[pltpu.VMEM((8,) + bundle[0].shape[1:], bf16) for bundle in bundles],
        ),
        out_shape=[jax.ShapeDtypeStruct((LAYERS,) + shape, f32) for shape in shapes],
        input_output_aliases={1 + len(arrays) + i: i for i in range(len(earlier))},
        compiler_params=params(18),
        cost_estimate=cost(size, 6 * size),
        name=name,
    )(place, *arrays, *earlier)


def columns_kernel(place, *refs):
    pieces, out = refs[:2], refs[2]
    size = pieces[0].shape[0]
    width = out.shape[0]
    for p in range(4):

        @pl.when(place[0] == p)
        def _():
            for k in range(2):
                part = pieces[k][:, p * width : (p + 1) * width].astype(f32)
                q = (p & 1) ^ k
                out[:, q * size : (q + 1) * size] = jnp.transpose(part).astype(bf16)


def columns(place, pieces):
    half = pieces[0].shape[0]
    return pl.pallas_call(
        columns_kernel,
        grid_spec=pltpu.PrefetchScalarGridSpec(
            num_scalar_prefetch=1,
            grid=(1,),
            in_specs=[whole((half, D))] * 2,
            out_specs=whole((D // 4, 2 * half)),
        ),
        out_shape=jax.ShapeDtypeStruct((D // 4, 2 * half), bf16),
        compiler_params=params(8),
        cost_estimate=cost(half * D, 8 * half * D),
        name="columns",
    )(place, *pieces)


def on_device(
    residual_in,
    cotangent,
    w_qkv,
    b_qv,
    w_out,
    b_out,
    w_up,
    b_up,
    w_down,
    b_down,
    ln_gain,
    ln_bias,
    selection,
    lengths,
    valid,
):
    rows = residual_in.shape[0]
    heads = selection.shape[0]
    blocks = rows // QB
    half = rows // 2
    count = lax.axis_size("tok")
    position = lax.axis_index("tok")
    member = lax.axis_index("head")
    width = D // 4
    first_row = position * rows
    chosen = lax.dynamic_slice_in_dim(selection, position * blocks, blocks, 1).reshape(heads, -1)
    per_device = rows // KB
    starts = slot_of(chosen // per_device, position, count) * rows + (chosen % per_device) * KB
    place = jnp.stack(
        [
            member,
            position,
            lengths[0],
            slot_of(position, position, count) * rows,
            slot_of(jnp.maximum(position - 1, 0), position, count) * rows,
            position if ring_form(count) else 0,
        ]
    ).astype(jnp.int32)

    first_pieces = share_features(residual_in.T)
    small = jnp.concatenate(
        [ln_gain.reshape(-1, width), ln_bias.reshape(-1, width), b_out, b_down], axis=0
    )
    small = jnp.pad(small, ((0, 128 - small.shape[0]), (0, 0)))
    param_pieces = share_features(small.T)

    split = jnp.transpose(w_qkv, (0, 2, 3, 1)).reshape(LAYERS, 3, heads, HD, D)
    w_all = jnp.concatenate(
        [
            jnp.pad(split[:, 0], ((0, 0), (0, 0), (0, WIDE - HD), (0, 0))),
            jnp.concatenate([split[:, 1], split[:, 2]], axis=2),
        ],
        axis=1,
    ).reshape(LAYERS, 2 * heads * WIDE, D)
    b_split = b_qv.reshape(LAYERS, 2, heads, HD)
    b_all = (
        jnp.concatenate(
            [
                jnp.pad(b_split[:, 0], ((0, 0), (0, 0), (0, HD))),
                jnp.pad(b_split[:, 1], ((0, 0), (0, 0), (HD, 0))),
            ],
            axis=1,
        )
        .reshape(LAYERS, 1, 2 * heads * WIDE)
        .astype(f32)
    )
    w_mix = jnp.pad(
        w_out.reshape(LAYERS, heads, HD, D), ((0, 0), (0, 0), (HD, 0), (0, 0))
    ).reshape(LAYERS, heads * WIDE, D)
    b_inner = b_up.astype(f32)

    far_valid = jnp.tile(valid.reshape(-1, KB), (1, SEL)).astype(f32)
    padded = jnp.concatenate([jnp.zeros((WINDOW,), jnp.int32), valid])
    near = lax.dynamic_slice_in_dim(padded, first_row, rows + WINDOW).reshape(-1, WINDOW)
    near_valid = jnp.concatenate([near[:-1], near[1:]], axis=1).astype(f32)
    own_valid = lax.dynamic_slice_in_dim(valid, first_row + (member & 1) * half, half)
    own_valid = own_valid.astype(f32)[:, None]
    mask = masks(place, chosen, near_valid, far_valid, heads, rows)

    pieces = first_pieces
    lows = []
    kept = []
    squares = []
    for l in range(LAYERS):
        normed, queries, *own_kv = project(
            place, pieces, None if l else param_pieces, w_all[l], b_all[l], rows, heads
        )
        if l == 0:
            own_kv, (low_first, param) = own_kv[:2], own_kv[2:]
            residual = low_first
        parts = gather_blocks(own_kv)
        mixed, probs, *pieces = attend(place, starts, queries, w_mix[l], mask, parts, count)
        residual, low_second, normed_own, branch_squares = add_norm(
            place, sum_rows(pieces), residual, param, own_valid, rows, B_OUT + l, 2 * l + 1
        )
        fed, slope, *pieces = feed(
            place, share_rows(normed_own), w_up[l], b_inner[l : l + 1], w_down[l]
        )
        residual, low_next, normed_own, second_squares = add_norm(
            place,
            sum_rows(pieces),
            residual,
            param,
            own_valid,
            rows,
            B_DOWN + l,
            2 * l + 2 if l + 1 < LAYERS else None,
        )
        squares.append((second_squares[1], branch_squares[0], second_squares[0]))
        kept.append((normed, queries, parts, mixed, probs, low_second, fed, slope))
        lows.append(low_next)
        if l + 1 < LAYERS:
            pieces = share_rows(normed_own)
    residual_out = columns(place, share_rows(lows[-1])).T

    gradient, sums_down = turn(place, share_features(cotangent.T))
    sums_down = sums_down[0]
    grad_pieces = (gradient,)
    grads = [None] * LAYERS
    placed_feed = placed_mix = ()
    shapes_mix = ((3, heads * HD, D), (heads * HD, D))
    for l in reversed(range(LAYERS)):
        last = l == 0
        normed, queries, parts, mixed, probs, low_second, fed, slope = kept[l]
        inner, grad_b_up, *pieces = feed_back(place, grad_pieces, w_up[l], w_down[l], slope)
        down_pieces = square_grads(place, after(fed, pieces), 1, grad_pieces, COLUMN_FIRST)
        feeding = Bundle(down_pieces, COLUMN_FIRST)
        feeding.send()
        up_pieces = square_grads(place, fed, 0, (inner,), COLUMN_FIRST)
        terms, _ = lax.optimization_barrier((sum_rows(pieces), up_pieces))
        terms = feeding.take(terms)
        feeding.add(up_pieces)
        if last:
            terms = feed_before.take(terms)
            feed_before.send()
        gradient, low, second_sums = norm_back(
            place, terms, low_second, gradient, param, rows, 2 * l + 1
        )
        pieces = share_rows(low)
        dq, branch_full, *kv_grads = attend_back(
            place, starts, queries, probs, w_mix[l], pieces, parts, count
        )
        kv_grads = feeding.take(kv_grads)
        if last:
            kv_grads = mix_before.take(feed_before.take(kv_grads))
        kv_terms = return_blocks(kv_grads, lambda other: other)
        if last:
            kv_terms, residual_out = lax.optimization_barrier((kv_terms, residual_out))
        dkv, bias_sums, first_sums, *pieces = project_back(
            place, dq, w_all[l], normed, param, kv_terms, 2 * l
        )
        if not last:
            feeding.send(dkv)
        groups = ((0, 3, 0), (1, 3, 0), (1, 3, HD), (2, 4, HD))
        mix_pieces = mix_grads(
            place, (dq, dkv, mixed, normed, branch_full), groups, COLUMN_FIRST
        )
        mix = Bundle(mix_pieces, COLUMN_FIRST)
        if last:
            finish_in_turn(dkv, feed_before, mix_before, feeding, mix)
        else:
            mix.send()
        terms, _ = lax.optimization_barrier((sum_rows(pieces), mix_pieces))
        if not last:
            terms = feeding.take(terms)
            feeding.send()
            feed_before, mix_before = feeding, mix
        gradient, low, low_sums = norm_back(
            place, terms, lows[l - 1] if l else low_first, gradient, param, rows, 2 * l
        )
        pieces = share_rows(low)
        if not last:
            pieces = mix.take(pieces)
            mix.send()
        grad_pieces = pieces
        grads[l] = (
            None,
            grad_b_up[0],
            jnp.concatenate(
                [
                    bias_sums[:heads, :HD].reshape(-1),
                    bias_sums[heads:, HD:].reshape(-1),
                    jnp.zeros((D - 2 * heads * HD,), f32),
                ]
            ),
            None,
            None,
            second_sums[2],
            sums_down,
            first_sums,
            second_sums,
        )
        sums_down = low_sums[2]
    grad_residual = columns(place, pieces).T
    for l, bundles in ((1, (feed_before, mix_before)), (0, (feeding, mix))):
        placed_feed = place_call(
            functools.partial(feed_place_kernel, order=COLUMN_FIRST),
            "feed_place",
            place,
            [bundles[0].finish()],
            placed_feed,
            ((D, D), (D, D)),
            l,
        )
        done = bundles[1].finish()
        if l == 0:
            done, placed_feed, placed_mix = lax.optimization_barrier(
                (done, placed_feed, placed_mix)
            )
        placed_mix = place_call(
            functools.partial(mix_place_kernel, bundles=((COLUMN_FIRST, (0, 1, 2, 3)),)),
            "mix_place",
            place,
            [done],
            placed_mix,
            shapes_mix,
            l,
        )

    first = jnp.concatenate([grads[l][7] for l in range(LAYERS)], axis=0)
    first = after(first, feeding.kept)
    first = first + swap(first, "head", 2)
    over_all = jnp.concatenate(
        [first]
        + [grads[l][8][:2] for l in range(LAYERS)]
        + [jnp.stack([grads[l][5] for l in range(LAYERS)])]
        + [jnp.stack([grads[l][6] for l in range(LAYERS)])]
        + [jnp.stack([vector for layer in squares for vector in layer])],
        axis=0,
    )
    over_tok = jnp.stack(
        [grads[l][1] for l in range(LAYERS)] + [grads[l][2] for l in range(LAYERS)]
    )
    packed = small_sum(
        jnp.concatenate([over_all + swap(over_all, "head", 1), over_tok], axis=0), "tok"
    )
    stat_row = 4 * LAYERS + 2 * LAYERS
    tok_row = stat_row + 3 * LAYERS
    mine = lax.dynamic_slice_in_dim(packed[:stat_row], member * width, width, 1)
    norms = mine[: 4 * LAYERS].reshape(2, LAYERS, 2, width)
    grad_ln_gain = jnp.stack([norms[0, :, 0], norms[1, :, 0]], axis=1)
    grad_ln_bias = jnp.stack([norms[0, :, 1], norms[1, :, 1]], axis=1)
    grad_b_out = mine[4 * LAYERS : 5 * LAYERS]
    grad_b_down = mine[5 * LAYERS : 6 * LAYERS]
    square_sums = jnp.sum(packed[stat_row:tok_row], axis=-1).reshape(LAYERS, 3)
    valid_count = jnp.maximum(jnp.sum(valid.astype(f32)), 1.0)
    statistics = jnp.sqrt(square_sums / (valid_count * D))
    grad_b_up = packed[tok_row : tok_row + LAYERS]
    grad_b_qv = packed[tok_row + LAYERS :, : 2 * heads * HD].reshape(LAYERS, 2, heads * HD)
    return (
        residual_out,
        grad_residual,
        jnp.transpose(placed_mix[0], (0, 3, 1, 2)),
        grad_b_qv,
        placed_mix[1],
        grad_b_out,
        placed_feed[1],
        grad_b_up,
        placed_feed[0],
        grad_b_down,
        grad_ln_gain,
        grad_ln_bias,
        statistics,
    )


def solution(mesh):
    in_specs = (
        P("tok", "head"),
        P("tok", "head"),
        P(None, None, None, "head"),
        P(None, None, "head"),
        P(None, "head", None),
        P(None, "head"),
        P(None, None, "head"),
        P(None, "head"),
        P(None, "head", None),
        P(None, "head"),
        P(None, None, "head"),
        P(None, None, "head"),
        P("head", None, None),
        P(),
        P(),
    )
    out_specs = (
        P("tok", "head"),
        P("tok", "head"),
        P(None, None, None, "head"),
        P(None, None, "head"),
        P(None, "head", None),
        P(None, "head"),
        P(None, None, "head"),
        P(None, "head"),
        P(None, "head", None),
        P(None, "head"),
        P(None, None, "head"),
        P(None, None, "head"),
        P(),
    )
    return jax.shard_map(
        on_device, mesh=mesh, in_specs=in_specs, out_specs=out_specs, check_vma=False
    )
```
